512 devices in a mesh: gx: 16 (over x, y), gy: 32 (over z, core).
Axes of the slice: x: 4, y: 4, z: 16, core: 2. Of those that a mesh axis runs over, the one named last changes fastest.
Arguments:
- displacement: float32 [3, 192, 256, 128], P(None, 'gx', 'gy'), may hold values from -6 to 6
- adjoint_load: float32 [3, 192, 256, 128], P(None, 'gx', 'gy'), may hold values from -24 to 24
- density: float32 [192, 256, 128], P('gx', 'gy'), may hold values from 0.1 to 1
- fixed_mask: int32 [192, 256, 128], P('gx', 'gy'), may hold values 0 or 1
- load_nodes: int32 [3, 2048], replicated, may hold values from 0 to 255, as said below
- load_forces: float32 [3, 2048], replicated, may hold values from -16 to 16
Outputs:
- adjoint: float32 [3, 192, 256, 128], P(None, 'gx', 'gy')
- sensitivity: float32 [192, 256, 128], P('gx', 'gy')
The draws below stay inside these ranges and needn't reach their ends.
Inputs may be any that keep to these rules, and one draw needn't show every extreme that they name: `load_nodes`: row 0 holds x coordinates below 192, row 1 y coordinates below 256, row 2 z coordinates below 128; loads may share a node, and then add.
All inputs are finite; a program needn't handle non-finite values. No bound on the sum of `fixed_mask` on one device may be relied on, other than what follows from the above.
Results may differ from the reference program's by a relative error of at most 0.0003.
Values sent between devices are 32-bit elements; how exact they have to be, the bound alone decides.
No kernel may reach another device: no remote copies, remote signals or barrier semaphores. Data moves between devices by JAX's collectives and lax.ppermute only.
A program may use at most 64 MiB of HBM per device.

```python
import math
import jax
import jax.numpy as jnp
import numpy as np
from jax import lax

NZ = 128
ITERS = 3
NX = 192
NY = 256
LOADS = 2048


def broad_field(key, base_lo, base_hi, wave_amp, flip_chance):
    key_base, key_sign, key_waves, key_phase = jax.random.split(key, 4)
    across = jnp.arange(NX, dtype=jnp.float32) / NX
    along = jnp.arange(NY, dtype=jnp.float32) / NY
    depth = jnp.arange(NZ, dtype=jnp.float32) / NZ
    base = jax.random.uniform(key_base, (3,), jnp.float32, base_lo, base_hi)
    flips = jnp.where(jax.random.uniform(key_sign, (3,), jnp.float32) < flip_chance, -1.0, 1.0)
    base = base * flips
    waves = jax.random.randint(key_waves, (3, 3), 1, 3).astype(jnp.float32)
    phase = jax.random.uniform(key_phase, (3,), jnp.float32, 0.0, 2.0 * math.pi)
    angle = 2.0 * math.pi * (waves[:, 0, None, None, None] * across[None, :, None, None] + waves[:, 1, None, None, None] * along[None, None, :, None] + waves[:, 2, None, None, None] * depth[None, None, None, :]) + phase[:, None, None, None]
    return base[:, None, None, None] + wave_amp * jnp.sin(angle)


def draw_adjoint_load(key, part):
    key = jax.random.fold_in(key, 11)
    key_noise = jax.random.fold_in(key, 0)
    key_broad = jax.random.fold_in(key, 2)
    across = jnp.arange(NX, dtype=jnp.float32) / max(NX - 1, 1)
    along = jnp.arange(NY, dtype=jnp.float32) / max(NY - 1, 1)
    profile = (1.0 + 2.0 * across[:, None]) * (1.0 + 2.0 * along[None, :]) / 3.0
    broad = broad_field(key_broad, 0.8, 1.4, 0.8, 0.5)
    random_part = 0.4 * jax.random.normal(key_noise, (3, NX, NY, NZ), jnp.float32)
    result = (broad + random_part) * profile[None, :, :, None]
    return jnp.clip(result, -24.0, 24.0)


def draw_load_nodes(key, part):
    key = jax.random.fold_in(key, 5)
    key_x, key_y, key_z = jax.random.split(key, 3)
    coord_x = jax.random.randint(key_x, (LOADS,), 0, NX)
    coord_y = jax.random.randint(key_y, (LOADS,), 0, NY)
    coord_z = jax.random.randint(key_z, (LOADS,), 0, NZ)
    nodes = jnp.stack([coord_x, coord_y, coord_z]).astype(jnp.int32)
    far_corner = jnp.array([NX - 1, NY - 1, NZ - 1], jnp.int32)
    nodes = nodes.at[:, 0].set(far_corner)
    nodes = nodes.at[:, 1].set(jnp.zeros((3,), jnp.int32))
    return nodes


def place_ends(values, key, least, top_value):
    shape = values.shape
    spot = [jax.random.randint(jax.random.fold_in(key, axis), (), 0, shape[axis]) for axis in range(len(shape))]
    values = values.at[tuple(spot)].set(least)
    longest = shape.index(max(shape))
    spot[longest] = (spot[longest] + 1) % shape[longest]
    return values.at[tuple(spot)].set(top_value)


def steps_of(own_key, dims, cuts, least, largest):
    gain = 1.0
    for position, parts in cuts:
        steps = jax.random.uniform(jax.random.fold_in(jax.random.fold_in(own_key, 6), position), (parts,), jnp.float32, least / len(cuts), largest / len(cuts))
        gain = gain * jnp.repeat(jnp.exp(steps), dims[position] // parts).reshape((-1,) + (1,) * (len(dims) - 1 - position))
    return gain


def centred(stream_key, extent, scale, most, cuts=(), kind=jnp.bfloat16):
    factor_of = steps_of(stream_key, extent, cuts, -0.22, 0.18) if cuts else 1.0
    drawn = jax.random.normal(stream_key, extent, jnp.float32) * scale * factor_of
    return jnp.minimum(jnp.maximum(drawn, -most), most).astype(kind)


def setup_inputs(seed: int = 0) -> dict:
    key_list = jax.random.split(jax.random.key(seed), 7)
    displacement = centred(key_list[0], (3, NX, NY, NZ), 1.0, 6.0, ((1, 16), (2, 32)), jnp.float32)
    adjoint_load = draw_adjoint_load(jax.random.fold_in(key_list[6], 71), 0)
    density = jnp.clip(0.1 + 0.9 * jax.random.uniform(key_list[2], (NX, NY, NZ), jnp.float32) ** steps_of(key_list[2], (NX, NY, NZ), ((0, 16), (1, 32)), -0.2, 0.2), 0.1, 1.0)
    fixed_mask = place_ends((jax.random.randint(key_list[3], (NX, NY, NZ), 0, 8) < 1).astype(jnp.int32), jax.random.fold_in(key_list[3], 1), 0, 1)
    load_nodes = draw_load_nodes(jax.random.fold_in(key_list[6], 71), 0)
    load_forces = centred(key_list[5], (3, LOADS), 4.0, 16.0, (), jnp.float32)
    return dict(displacement=displacement, adjoint_load=adjoint_load, density=density, fixed_mask=fixed_mask, load_nodes=load_nodes, load_forces=load_forces)


POISSON = 0.3
PENALTY = 3.0
SOFT = 0.001
CORNERS = [(a, b, c) for c in (0, 1) for b in (0, 1) for a in (0, 1)]

def element_stiffness():
    lame_first = POISSON / ((1.0 + POISSON) * (1.0 - 2.0 * POISSON))
    shear_mod = 1.0 / (2.0 * (1.0 + POISSON))
    elastic = np.zeros((6, 6))
    elastic[:3, :3] = lame_first
    for axis_number in range(3):
        elastic[axis_number, axis_number] = lame_first + 2.0 * shear_mod
        elastic[axis_number + 3, axis_number + 3] = shear_mod
    points = [0.5 - 0.5 / np.sqrt(3.0), 0.5 + 0.5 / np.sqrt(3.0)]
    matrix = np.zeros((24, 24))
    for point_x in points:
        for point_y in points:
            for point_z in points:
                coords = (point_x, point_y, point_z)
                strain = np.zeros((6, 24))
                for number, corner in enumerate(CORNERS):
                    factors = [coords[d] if corner[d] else 1.0 - coords[d] for d in range(3)]
                    slopes = [1.0 if corner[d] else -1.0 for d in range(3)]
                    derivs = [slopes[0] * factors[1] * factors[2], factors[0] * slopes[1] * factors[2], factors[0] * factors[1] * slopes[2]]
                    column = 3 * number
                    strain[0, column] = derivs[0]
                    strain[1, column + 1] = derivs[1]
                    strain[2, column + 2] = derivs[2]
                    strain[3, column] = derivs[1]
                    strain[3, column + 1] = derivs[0]
                    strain[4, column + 1] = derivs[2]
                    strain[4, column + 2] = derivs[1]
                    strain[5, column] = derivs[2]
                    strain[5, column + 2] = derivs[0]
                matrix += strain.T @ elastic @ strain / 8.0
    return matrix

def filter_table():
    entries = []
    for offset_x in (-1, 0, 1):
        for offset_y in (-1, 0, 1):
            for offset_z in (-1, 0, 1):
                distance = float(np.sqrt(offset_x ** 2 + offset_y ** 2 + offset_z ** 2))
                result = 1.5 - distance
                if result > 0:
                    entries.append(((offset_x, offset_y, offset_z), result))
    return entries

def smooth(padded, out_x, out_y):
    layers = padded.shape[2]
    deeper = jnp.pad(padded, ((0, 0), (0, 0), (1, 1)))
    summed = jnp.zeros((out_x, out_y, layers), jnp.float32)
    for offset, weight in filter_table():
        summed = summed + weight * deeper[1 + offset[0]:1 + offset[0] + out_x, 1 + offset[1]:1 + offset[1] + out_y, 1 + offset[2]:1 + offset[2] + layers]
    return summed

def plane_stack(lower_plane, upper_plane):
    count_y, count_z = (lower_plane.shape[1], lower_plane.shape[2])
    lower_pad = jnp.pad(lower_plane, ((0, 0), (0, 1), (0, 1)))
    upper_pad = jnp.pad(upper_plane, ((0, 0), (0, 1), (0, 1)))
    portions = []
    for a, b, c in CORNERS:
        source = lower_pad if a == 0 else upper_pad
        portions.append(source[:, b:b + count_y, c:c + count_z])
    return jnp.concatenate(portions, axis=0)

def split_forces(forces):
    count_y, count_z = (forces.shape[1], forces.shape[2])
    lower_part = jnp.zeros((3, count_y, count_z), jnp.float32)
    second = jnp.zeros((3, count_y, count_z), jnp.float32)
    for number, (a, b, c) in enumerate(CORNERS):
        portion = jnp.pad(forces[3 * number:3 * number + 3], ((0, 0), (b, 0), (c, 0)))[:, :count_y, :count_z]
        if a == 0:
            lower_part = lower_part + portion
        else:
            second = second + portion
    return (lower_part, second)

def node_planes(field):
    planes = jnp.moveaxis(field, 1, 0)
    upper_planes = jnp.concatenate([planes[1:], jnp.zeros_like(planes[:1])], axis=0)
    return (planes, upper_planes)

def assemble(making, planes, upper_planes, modulus):

    def advance(running, inputs):
        forces = making(inputs[0], inputs[1], inputs[2])
        lower_part, second = split_forces(forces)
        return (second, running + lower_part)
    initial = jnp.zeros((3, modulus.shape[1], modulus.shape[2]), jnp.float32)
    _, result = lax.scan(advance, initial, (planes, upper_planes, modulus))
    return jnp.moveaxis(result, 0, 1)

def reference(displacement, adjoint_load, density, fixed_mask, load_nodes, load_forces):
    stiffness = jnp.asarray(element_stiffness(), dtype=jnp.float32)
    corner_diag = jnp.diagonal(stiffness)
    rim = ((1, 1), (1, 1), (0, 0))
    unity_grid = jnp.ones_like(density)
    weights = smooth(jnp.pad(unity_grid, rim), NX, NY)
    physical = smooth(jnp.pad(density, rim), NX, NY) / weights
    modulus = SOFT + (1.0 - SOFT) * physical ** 3
    free_nodes = (1 - fixed_mask).astype(jnp.float32)[None]
    placed = jnp.zeros((3, NX, NY, NZ), jnp.float32).at[:, load_nodes[0], load_nodes[1], load_nodes[2]].add(load_forces)
    right_side = free_nodes * (adjoint_load + placed)

    def apply_forces(lower_plane, upper_plane, plane_mod):
        stacked = plane_stack(lower_plane, upper_plane)
        forces = jnp.dot(stiffness, stacked.reshape(24, -1), precision=lax.Precision.HIGHEST).reshape(stacked.shape)
        return forces * plane_mod[None]

    def diag_forces(lower_plane, upper_plane, plane_mod):
        return corner_diag[:, None, None] * plane_mod[None]
    zero_field = jnp.zeros((3, NX, NY, NZ), jnp.float32)
    zero_planes, zero_upper = node_planes(zero_field)
    diagonal = free_nodes * assemble(diag_forces, zero_planes, zero_upper, modulus) + (1.0 - free_nodes)

    def operate(field):
        planes, upper_planes = node_planes(free_nodes * field)
        return free_nodes * assemble(apply_forces, planes, upper_planes, modulus) + (1.0 - free_nodes) * field
    adjoint = jnp.zeros_like(right_side)
    residual = right_side
    scaled = residual / diagonal
    direction = scaled
    norm_now = jnp.sum(residual * scaled)
    for iteration in range(ITERS):
        product_field = operate(direction)
        step_size = norm_now / jnp.sum(direction * product_field)
        adjoint = adjoint + step_size * direction
        if iteration + 1 < ITERS:
            residual = residual - step_size * product_field
            scaled = residual / diagonal
            norm_next = jnp.sum(residual * scaled)
            direction = scaled + norm_next / norm_now * direction
            norm_now = norm_next
    disp_planes, disp_upper = node_planes(displacement)
    adj_planes, adj_upper = node_planes(adjoint)

    def energy_plane(running, inputs):
        disp_elem = plane_stack(inputs[0], inputs[1])
        adj_elem = plane_stack(inputs[2], inputs[3])
        forces = jnp.dot(stiffness, adj_elem.reshape(24, -1), precision=lax.Precision.HIGHEST).reshape(adj_elem.shape)
        return (running, lax.optimization_barrier(jnp.sum(disp_elem * forces, axis=0)))
    _, energy = lax.scan(energy_plane, jnp.zeros((), jnp.float32), (disp_planes, disp_upper, adj_planes, adj_upper))
    derived = PENALTY * (1.0 - SOFT) * physical ** 2 * energy / weights
    sensitivity = smooth(jnp.pad(derived, rim), NX, NY)
    return (adjoint, sensitivity)
```

```python
import functools

import jax
import jax.numpy as jnp
import numpy as np
from jax import lax
from jax.experimental import pallas as pl
from jax.experimental.pallas import tpu as pltpu
from jax.sharding import Mesh, PartitionSpec as P

POISSON = 0.3
PENALTY = 3.0
SOFT = 0.001
CORNERS = [(a, b, c) for c in (0, 1) for b in (0, 1) for a in (0, 1)]
EDGE = float(1.5 - np.sqrt(2.0))

RX, RY, NZ = 12, 8, 128
NI = RX + 8
NJ = 16
LOW_X, UP_X = 20, 27
BLOCKS = 128
F32 = jnp.float32


def element_stiffness():
    lame_first = POISSON / ((1.0 + POISSON) * (1.0 - 2.0 * POISSON))
    shear_mod = 1.0 / (2.0 * (1.0 + POISSON))
    elastic = np.zeros((6, 6))
    elastic[:3, :3] = lame_first
    for axis_number in range(3):
        elastic[axis_number, axis_number] = lame_first + 2.0 * shear_mod
        elastic[axis_number + 3, axis_number + 3] = shear_mod
    points = [0.5 - 0.5 / np.sqrt(3.0), 0.5 + 0.5 / np.sqrt(3.0)]
    matrix = np.zeros((24, 24))
    for point_x in points:
        for point_y in points:
            for point_z in points:
                coords = (point_x, point_y, point_z)
                strain = np.zeros((6, 24))
                for number, corner in enumerate(CORNERS):
                    factors = [coords[d] if corner[d] else 1.0 - coords[d] for d in range(3)]
                    slopes = [1.0 if corner[d] else -1.0 for d in range(3)]
                    derivs = [
                        slopes[0] * factors[1] * factors[2],
                        factors[0] * slopes[1] * factors[2],
                        factors[0] * factors[1] * slopes[2],
                    ]
                    column = 3 * number
                    strain[0, column] = derivs[0]
                    strain[1, column + 1] = derivs[1]
                    strain[2, column + 2] = derivs[2]
                    strain[3, column] = derivs[1]
                    strain[3, column + 1] = derivs[0]
                    strain[4, column + 1] = derivs[2]
                    strain[4, column + 2] = derivs[1]
                    strain[5, column] = derivs[2]
                    strain[5, column + 2] = derivs[0]
                matrix += strain.T @ elastic @ strain / 8.0
    return matrix


def modal_stiffness():
    one = np.array([[1.0, 1.0], [-1.0, 1.0]])
    change = np.zeros((8, 8))
    for row, (a, b, c) in enumerate(CORNERS):
        for column, (p, q, r) in enumerate(CORNERS):
            change[row, column] = one[a, p] * one[b, q] * one[c, r]
    inverse = np.linalg.inv(np.kron(change, np.eye(3)))
    modal = inverse.T @ element_stiffness() @ inverse
    modes = [corner + (d,) for corner in CORNERS for d in range(3)]
    rows = {}
    for i, row in enumerate(modes):
        terms = [(modes[j], float(modal[i, j])) for j in range(24) if abs(modal[i, j]) > 1e-12]
        if terms:
            rows[row] = terms
    return rows


MODAL = modal_stiffness()
CORNER_DIAG = float(element_stiffness()[0, 0])


def pack_x_kernel(load, disp, dens, mask, low, up):
    for c in range(3):
        low[3 * c : 3 * c + 3] = load[c, RX - 3 : RX]
        up[4 * c : 4 * c + 4] = load[c, 0:4]
        low[17 + c] = disp[c, RX - 1]
        up[21 + 2 * c : 23 + 2 * c] = disp[c, 0:2]
    low[9:12] = (1 - mask[RX - 3 : RX]).astype(F32)
    up[12:16] = (1 - mask[0:4]).astype(F32)
    low[12:17] = dens[RX - 5 : RX]
    up[16:21] = dens[0:5]


def loads_kernel(nodes, forces, out):
    first_x = (lax.axis_index("x") * lax.axis_size("y") + lax.axis_index("y")) * RX - 3
    first_y = (lax.axis_index("z") * lax.axis_size("c") + lax.axis_index("c")) * RY
    count = (NI - 1) * RY
    chunk = 256
    place = lax.broadcasted_iota(jnp.int32, (count, chunk), 0)
    depth = lax.broadcasted_iota(jnp.int32, (NZ, chunk), 0)
    total = jnp.zeros((9 * count, NZ), F32)
    for start in range(0, nodes.shape[1], chunk):
        cols = slice(start, start + chunk)
        local_x = nodes[0:1, cols] - first_x
        local_y = nodes[1:2, cols] - first_y
        inside = (local_x >= 0) & (local_x < NI - 1) & (local_y >= 0) & (local_y < RY)
        spot = jnp.where(inside, local_x * RY + local_y, -1)
        hit = place == spot
        layer = jnp.where(depth == nodes[2:3, cols], 1.0, 0.0).astype(jnp.bfloat16)
        parts = []
        for c in range(3):
            rest = forces[c : c + 1, cols]
            for _ in range(3):
                head = rest.astype(jnp.bfloat16).astype(F32)
                rest = rest - head
                parts.append(jnp.where(hit, head, 0.0).astype(jnp.bfloat16))
        total = total + lax.dot_general(
            jnp.concatenate(parts, axis=0),
            layer,
            (((1,), (1,)), ((), ())),
            preferred_element_type=F32,
        )
    for c in range(3):
        base = 3 * c * count
        summed = (
            total[base : base + count]
            + total[base + count : base + 2 * count]
            + total[base + 2 * count : base + 3 * count]
        )
        out[c] = summed.reshape(NI - 1, RY, NZ)


def pack_y_kernel(load, disp, dens, mask, placed, low, up, ld, fr, dn, di, first, second):
    for c in range(3):
        ld[c, 0:3] = low[3 * c : 3 * c + 3] + placed[c, 0:3]
        ld[c, 3 : 3 + RX] = load[c] + placed[c, 3 : 3 + RX]
        ld[c, 3 + RX : 7 + RX] = up[4 * c : 4 * c + 4] + placed[c, 3 + RX : 7 + RX]
        di[c, 0] = low[17 + c]
        di[c, 1 : 1 + RX] = disp[c]
        di[c, 1 + RX : 3 + RX] = up[21 + 2 * c : 23 + 2 * c]
    fr[0:3] = low[9:12]
    fr[3 : 3 + RX] = (1 - mask[...]).astype(F32)
    fr[3 + RX : 7 + RX] = up[12:16]
    dn[0:5] = low[12:17]
    dn[5 : 5 + RX] = dens[...]
    dn[5 + RX : 10 + RX] = up[16:21]
    even = lax.axis_index("c") == 0

    def rows_for_upper(out):
        for c in range(3):
            out[19 * c : 19 * c + 19] = ld[c, :, 4:8]
        out[57:76] = fr[:, 4:8]
        out[76:98] = dn[:, 4:8]
        for p in range(22):
            out[98 + p // 4, p % 4 : p % 4 + 1] = dn[p, 3:4]
        for n in range(45):
            out[104 + n // 4, n % 4 : n % 4 + 1] = di[n // 15, n % 15, 7:8]

    def rows_for_lower(out):
        for c in range(3):
            out[19 * c : 19 * c + 19] = ld[c, :, 0:4]
        out[57:76] = fr[:, 0:4]
        out[76:98] = dn[:, 0:4]
        for p in range(22):
            out[98 + p // 4, p % 4 : p % 4 + 1] = dn[p, 4:5]
        for n in range(45):
            out[104 + n // 2, 2 * (n % 2) : 2 * (n % 2) + 2] = di[n // 15, n % 15, 0:2]

    @pl.when(even)
    def _():
        rows_for_upper(first)
        rows_for_lower(second)

    @pl.when(jnp.logical_not(even))
    def _():
        rows_for_lower(first)
        rows_for_upper(second)


def up_z(v, lane):
    return jnp.where(lane < NZ - 1, pltpu.roll(v, NZ - 1, 1), 0.0)


def down_z(v, lane):
    return jnp.where(lane > 0, pltpu.roll(v, 1, 1), 0.0)


def up_y(v):
    return pltpu.roll(v, NJ - 1, 0)


def down_y(v):
    return pltpu.roll(v, 1, 0)


def gather_yz(v, lane):
    above = up_z(v, lane)
    result = {}
    for c, part in ((0, v + above), (1, above - v)):
        higher = up_y(part)
        result[0, c] = part + higher
        result[1, c] = higher - part
    return result


YZ = [(b, c) for b in (0, 1) for c in (0, 1)]


def main_kernel(ld, fr, dn, di, first, second, basis, senses, sums, LD, FR, DN, DI, MOD, SC, W, Z, G, N, F, DV, HP):
    gx = lax.axis_index("x") * lax.axis_size("y") + lax.axis_index("y")
    gy = lax.axis_index("z") * lax.axis_size("c") + lax.axis_index("c")
    extent_x = RX * lax.axis_size("x") * lax.axis_size("y")
    extent_y = RY * lax.axis_size("z") * lax.axis_size("c")
    lane = lax.broadcasted_iota(jnp.int32, (NJ, NZ), 1)
    row = lax.broadcasted_iota(jnp.int32, (NJ, NZ), 0)

    LD[:, :, 4:12] = ld[...]
    FR[:, 4:12] = fr[...]
    DN[:, 8:16] = dn[...]
    DI[:, :, 4:12] = di[...]
    DI[:, :, 0:4] = jnp.zeros((3, 15, 4, NZ), F32)
    DI[:, :, 12:16] = jnp.zeros((3, 15, 4, NZ), F32)

    def fill(below, above):
        for c in range(3):
            LD[c, :, 0:4] = below[19 * c : 19 * c + 19]
            LD[c, :, 12:16] = above[19 * c : 19 * c + 19]
        FR[:, 0:4] = below[57:76]
        FR[:, 12:16] = above[57:76]
        DN[:, 4:8] = below[76:98]
        DN[:, 16:20] = above[76:98]
        for p in range(22):
            DN[p, 3:4] = below[98 + p // 4, p % 4 : p % 4 + 1]
            DN[p, 20:21] = above[98 + p // 4, p % 4 : p % 4 + 1]
        for n in range(45):
            DI[n // 15, n % 15, 3:4] = below[104 + n // 4, n % 4 : n % 4 + 1]
            DI[n // 15, n % 15, 12:14] = above[104 + n // 2, 2 * (n % 2) : 2 * (n % 2) + 2]

    even = lax.axis_index("c") == 0

    @pl.when(even)
    def _():
        fill(second, first)

    @pl.when(jnp.logical_not(even))
    def _():
        fill(first, second)

    place_y = gy * RY - 4 + row
    inside_y = jnp.where((place_y >= 0) & (place_y < extent_y), 1.0, 0.0)
    near_y = 2.0 - jnp.where(place_y == 0, 1.0, 0.0) - jnp.where(place_y == extent_y - 1, 1.0, 0.0)
    near_z = 2.0 - jnp.where(lane == 0, 1.0, 0.0) - jnp.where(lane == NZ - 1, 1.0, 0.0)
    part_a = 1.5 + 0.5 * (near_y + near_z) + EDGE * near_y * near_z
    part_b = 0.5 + EDGE * (near_y + near_z)

    def filter_parts(p, _):
        cells = DN[p, 4:20]
        beside = DN[p, 3:19] + DN[p, 5:21]
        deep = up_z(cells, lane) + down_z(cells, lane)
        deep_beside = up_z(beside, lane) + down_z(beside, lane)
        N[0, p] = 1.5 * cells + 0.5 * (deep + beside) + EDGE * deep_beside
        N[1, p] = 0.5 * cells + EDGE * (deep + beside)
        return 0

    lax.fori_loop(0, NI + 2, filter_parts, 0)

    def modulus(i, _):
        place_x = gx * RX - 4 + i
        inside_x = jnp.where((place_x >= 0) & (place_x < extent_x), 1.0, 0.0)
        near_x = 2.0 - jnp.where(place_x == 0, 1.0, 0.0) - jnp.where(place_x == extent_x - 1, 1.0, 0.0)
        weights = part_a + near_x * part_b
        physical = (N[0, i + 1] + N[1, i] + N[1, i + 2]) / weights
        squared = physical * physical
        inside = inside_y * inside_x
        mod = inside * (SOFT + (1.0 - SOFT) * squared * physical)
        MOD[i] = mod
        SC[i] = inside * (PENALTY * (1.0 - SOFT)) * squared / weights
        deep = mod + down_z(mod, lane)
        HP[i] = deep + down_y(deep)
        return 0

    lax.fori_loop(0, NI, modulus, 0)

    owned_row = (row >= 4) & (row < 12)
    zero = jnp.zeros((NJ, NZ), F32)

    def store_gather(c, i, v):
        for (b, s), value in gather_yz(v, lane).items():
            G[4 * c + 2 * b + s, i] = value

    def start(i, total):
        diagonal = CORNER_DIAG * (HP[i] + HP[i - 1])
        inverse = jnp.where(FR[i - 1] > 0.5, 1.0 / diagonal, 0.0)
        W[i] = inverse
        own = (i >= 4) & (i < 4 + RX)
        part = zero
        for c in range(3):
            load = LD[c, i - 1]
            z = inverse * load
            Z[0, c, i] = z
            part = part + z * load
            store_gather(c, i, z)
        return total + jnp.where(own, part, 0.0)

    bz = lax.fori_loop(1, NI, start, zero)

    def modes_of(low_plane, high_plane):
        result = {}
        for c in range(3):
            for b, s in YZ:
                near, far = low_plane[c, b, s], high_plane[c, b, s]
                result[0, b, s, c] = near + far
                result[1, b, s, c] = far - near
        return result

    def stiff(modes):
        forces = {}
        for mode, terms in MODAL.items():
            value = None
            for other, factor in terms:
                term = modes[other] * factor
                value = term if value is None else value + term
            forces[mode] = value
        return forces

    def planes_of(ref, i, rows):
        return {(c, b, s): ref[4 * c + 2 * b + s, i, rows] for c in range(3) for b, s in YZ}

    def gather_disp(p, _):
        for c in range(3):
            for (b, s), value in gather_yz(DI[c, p], lane).items():
                N[4 * c + 2 * b + s, p] = value
        return 0

    lax.fori_loop(0, 15, gather_disp, 0)
    numbers = {mode: n for n, mode in enumerate(MODAL)}

    for tile in range(2):
        rows = slice(8 * tile, 8 * tile + 8)

        def disp_forces(p, _, rows=rows):
            forces = stiff(modes_of(planes_of(N, p, rows), planes_of(N, p + 1, rows)))
            for mode, value in forces.items():
                F[numbers[mode], p, rows] = value
            return 0

        lax.fori_loop(0, 14, disp_forces, 0)

    def apply(k):
        begin, end = 1 + k, NI - 1 - k
        for tile in range(2):
            rows = slice(8 * tile, 8 * tile + 8)
            blank = jnp.zeros((8, NZ), F32)

            def elements(i, carry, rows=rows):
                passed = carry
                modes = modes_of(planes_of(G, i, rows), planes_of(G, i + 1, rows))
                young = MOD[i, rows]
                forces = stiff(modes)
                energy = blank
                for mode, n in numbers.items():
                    energy = energy + modes[mode] * F[n, jnp.clip(i - 3, 0, 13), rows]
                DV[k, i, rows] = energy * SC[i, rows]
                following = []
                for c in range(3):
                    for b, s in YZ:
                        slope = forces[1, b, s, c] * young
                        if (0, b, s, c) in forces:
                            level = forces[0, b, s, c] * young
                            low, high = level - slope, level + slope
                        else:
                            low, high = -slope, slope
                        N[4 * c + 2 * b + s, i, rows] = passed[len(following)] + low
                        following.append(high)
                return tuple(following)

            lax.fori_loop(begin, end, elements, (blank,) * 12)

    def image(c, i):
        levels = []
        for b in (0, 1):
            level, slope = N[4 * c + 2 * b, i], N[4 * c + 2 * b + 1, i]
            levels.append(level - slope + down_z(level + slope, lane))
        return levels[0] - levels[1] + down_y(levels[0] + levels[1])

    apply(0)

    def first_image(i, totals):
        own = (i >= 4) & (i < 4 + RX)
        inverse = W[i]
        parts = [zero, zero, zero]
        for c in range(3):
            q = image(c, i)
            z = Z[0, c, i]
            y = inverse * q - z
            Z[1, c, i] = y
            parts = [parts[0] + z * q, parts[1] + y * LD[c, i - 1], parts[2] + y * q]
            store_gather(c, i, y)
        return tuple(t + jnp.where(own, p, 0.0) for t, p in zip(totals, parts))

    h00, b1, h01 = lax.fori_loop(2, NI - 1, first_image, (zero,) * 3)
    apply(1)

    def second_image(i, totals):
        own = (i >= 4) & (i < 4 + RX)
        inverse = W[i]
        parts = [zero, zero, zero]
        for c in range(3):
            q = image(c, i)
            z = Z[1, c, i]
            y = inverse * q - z
            Z[2, c, i] = y
            parts = [parts[0] + z * q, parts[1] + y * LD[c, i - 1], parts[2] + y * q]
            store_gather(c, i, y)
        return tuple(t + jnp.where(own, p, 0.0) for t, p in zip(totals, parts))

    h11, b2, h12 = lax.fori_loop(3, NI - 2, second_image, (zero,) * 3)
    apply(2)

    def third_image(i, totals):
        parts = [zero, zero]
        for c in range(3):
            q = image(c, i)
            parts = [parts[0] + Z[2, c, i] * q, parts[1] + Z[0, c, i] * q]
        return tuple(t + p for t, p in zip(totals, parts))

    h22, h02 = lax.fori_loop(4, 4 + RX, third_image, (zero,) * 2)

    lanes = lax.broadcasted_iota(jnp.int32, (1, NZ), 1)
    line = jnp.zeros((1, NZ), F32)
    for n, value in enumerate((bz, b1, b2, h00, h01, h02, h11, h12, h22)):
        whole = jnp.sum(jnp.where(owned_row, value, 0.0), axis=0, keepdims=True)
        whole = jnp.sum(whole, axis=1, keepdims=True)
        line = line + jnp.where(lanes == n, whole, 0.0)
    for n in range(sums.shape[0]):
        sums[n] = line

    lane8 = lax.broadcasted_iota(jnp.int32, (RY, NZ), 1)
    for k in range(3):

        def sense_parts(i, _, k=k):
            cells = DV[k, i, 4:12]
            beside = DV[k, i, 3:11] + DV[k, i, 5:13]
            deep = up_z(cells, lane8) + down_z(cells, lane8)
            deep_beside = up_z(beside, lane8) + down_z(beside, lane8)
            N[0, i, 0:8] = 1.5 * cells + 0.5 * (deep + beside) + EDGE * deep_beside
            N[1, i, 0:8] = 0.5 * cells + EDGE * (deep + beside)
            return 0

        lax.fori_loop(3, NI - 3, sense_parts, 0)
        for i in range(4, 4 + RX):
            senses[k, i - 4] = N[0, i, 0:8] + N[1, i - 1, 0:8] + N[1, i + 1, 0:8]
    basis[...] = Z[:, :, 4 : 4 + RX, 4:12]


def final_kernel(gathered, basis, senses, adjoint, sensitivity):
    total = jnp.sum(gathered[...], axis=0)

    def value(n):
        return jnp.broadcast_to(total[:, n : n + 1], (1, NZ))

    b0, b1, b2, h00, h01, h02, h11, h12, h22 = [value(n) for n in range(9)]
    l1, l2 = h01 / h00, h02 / h00
    d1 = h11 - l1 * h01
    e = h12 - l1 * h02
    fine1 = d1 > 0.0
    l3 = jnp.where(fine1, e / d1, 0.0)
    d2 = h22 - l2 * h02 - l3 * e
    t1 = b1 - l1 * b0
    t2 = b2 - l2 * b0 - l3 * t1
    c2 = jnp.where(d2 > 0.0, t2 / d2, 0.0)
    c1 = jnp.where(fine1, t1 / d1, 0.0) - l3 * c2
    c0 = b0 / h00 - l1 * c1 - l2 * c2
    adjoint[...] = c0 * basis[0] + c1 * basis[1] + c2 * basis[2]
    sensitivity[...] = c0 * senses[0] + c1 * senses[1] + c2 * senses[2]


VMEM = pl.BlockSpec(memory_space=pltpu.VMEM)


def call(kernel, inputs, outs, scratch=(), limit=None):
    single = not isinstance(outs, list)
    shapes = [outs] if single else outs
    result = pl.pallas_call(
        kernel,
        out_shape=[jax.ShapeDtypeStruct(s, F32) for s in shapes],
        in_specs=[VMEM] * len(inputs),
        out_specs=[VMEM] * len(shapes),
        scratch_shapes=[pltpu.VMEM(s, F32) for s in scratch],
        compiler_params=pltpu.CompilerParams(vmem_limit_bytes=limit or 32 * 1024 * 1024),
    )(*inputs)
    return result[0] if single else result


def shards(displacement, adjoint_load, density, fixed_mask, load_nodes, load_forces):
    gx, gy = ("x", "y"), ("z", "c")
    count_x = lax.axis_size("x") * lax.axis_size("y")
    count_y = lax.axis_size("z") * lax.axis_size("c")
    own = (adjoint_load, displacement, density, fixed_mask)
    low, up = call(pack_x_kernel, own, [(LOW_X, RY, NZ), (UP_X, RY, NZ)])
    low = lax.ppermute(low, gx, [(i, i + 1) for i in range(count_x - 1)])
    up = lax.ppermute(up, gx, [(i + 1, i) for i in range(count_x - 1)])
    placed = call(loads_kernel, (load_nodes, load_forces), (3, NI - 1, RY, NZ))
    ld, fr, dn, di, first, second = call(
        pack_y_kernel,
        own + (placed, low, up),
        [
            (3, NI - 1, RY, NZ),
            (NI - 1, RY, NZ),
            (NI + 2, RY, NZ),
            (3, RX + 3, RY, NZ),
            (BLOCKS, 4, NZ),
            (BLOCKS, 4, NZ),
        ],
    )
    first = lax.ppermute(first, "c", [(0, 1), (1, 0)])
    pairs = [(i, i + 1) for i in range(1, count_y - 1, 2)]
    second = lax.ppermute(second, gy, pairs + [(j, i) for i, j in pairs])
    near = lax.axis_size("c") * count_x
    far = lax.axis_size("z")
    basis, senses, sums = call(
        main_kernel,
        (ld, fr, dn, di, first, second),
        [(3, 3, RX, RY, NZ), (3, RX, RY, NZ), (near, 1, NZ)],
        [
            (3, NI - 1, NJ, NZ),
            (NI - 1, NJ, NZ),
            (NI + 2, 24, NZ),
            (3, RX + 3, NJ, NZ),
            (NI, NJ, NZ),
            (NI, NJ, NZ),
            (NI, NJ, NZ),
            (3, 3, NI, NJ, NZ),
            (12, NI, NJ, NZ),
            (12, NI + 2, NJ, NZ),
            (len(MODAL), 14, NJ, NZ),
            (3, NI, NJ, NZ),
            (NI, NJ, NZ),
        ],
        48 * 1024 * 1024,
    )
    sums = lax.all_to_all(sums, ("x", "y", "c"), 0, 0, tiled=True)
    sums = jnp.broadcast_to(jnp.sum(sums, axis=0, keepdims=True), (far, 1, NZ))
    sums = lax.all_to_all(sums, "z", 0, 0, tiled=True)
    adjoint, sensitivity = call(
        final_kernel, (sums, basis, senses), [(3, RX, RY, NZ), (RX, RY, NZ)]
    )
    return adjoint, sensitivity


def solution(mesh):
    size_x, size_y = mesh.shape["gx"], mesh.shape["gy"]
    side = int(round(size_x**0.5))
    whole = Mesh(
        mesh.devices.reshape(side, size_x // side, size_y // 2, 2), ("x", "y", "z", "c")
    )
    field = P(None, ("x", "y"), ("z", "c"), None)
    grid = P(("x", "y"), ("z", "c"), None)
    return jax.shard_map(
        shards,
        mesh=whole,
        in_specs=(field, field, grid, grid, P(), P()),
        out_specs=(field, grid),
        check_vma=False,
    )
```

```python
import functools

import jax
import jax.numpy as jnp
import numpy as np
from jax import lax
from jax.experimental import pallas as pl
from jax.experimental.pallas import tpu as pltpu
from jax.sharding import Mesh, PartitionSpec as P

POISSON = 0.3
PENALTY = 3.0
SOFT = 0.001
CORNERS = [(a, b, c) for c in (0, 1) for b in (0, 1) for a in (0, 1)]
EDGE = float(1.5 - np.sqrt(2.0))

RX, RY, NZ = 12, 8, 128
NI = RX + 8
LOW_X, UP_X = 20, 27
BLOCKS = 128
F32 = jnp.float32


def element_stiffness():
    lame_first = POISSON / ((1.0 + POISSON) * (1.0 - 2.0 * POISSON))
    shear_mod = 1.0 / (2.0 * (1.0 + POISSON))
    elastic = np.zeros((6, 6))
    elastic[:3, :3] = lame_first
    for axis_number in range(3):
        elastic[axis_number, axis_number] = lame_first + 2.0 * shear_mod
        elastic[axis_number + 3, axis_number + 3] = shear_mod
    points = [0.5 - 0.5 / np.sqrt(3.0), 0.5 + 0.5 / np.sqrt(3.0)]
    matrix = np.zeros((24, 24))
    for point_x in points:
        for point_y in points:
            for point_z in points:
                coords = (point_x, point_y, point_z)
                strain = np.zeros((6, 24))
                for number, corner in enumerate(CORNERS):
                    factors = [coords[d] if corner[d] else 1.0 - coords[d] for d in range(3)]
                    slopes = [1.0 if corner[d] else -1.0 for d in range(3)]
                    derivs = [
                        slopes[0] * factors[1] * factors[2],
                        factors[0] * slopes[1] * factors[2],
                        factors[0] * factors[1] * slopes[2],
                    ]
                    column = 3 * number
                    strain[0, column] = derivs[0]
                    strain[1, column + 1] = derivs[1]
                    strain[2, column + 2] = derivs[2]
                    strain[3, column] = derivs[1]
                    strain[3, column + 1] = derivs[0]
                    strain[4, column + 1] = derivs[2]
                    strain[4, column + 2] = derivs[1]
                    strain[5, column] = derivs[2]
                    strain[5, column + 2] = derivs[0]
                matrix += strain.T @ elastic @ strain / 8.0
    return matrix


def modal_stiffness():
    one = np.array([[1.0, 1.0], [-1.0, 1.0]])
    change = np.zeros((8, 8))
    for row, (a, b, c) in enumerate(CORNERS):
        for column, (p, q, r) in enumerate(CORNERS):
            change[row, column] = one[a, p] * one[b, q] * one[c, r]
    inverse = np.linalg.inv(np.kron(change, np.eye(3)))
    modal = inverse.T @ element_stiffness() @ inverse
    modes = [corner + (d,) for corner in CORNERS for d in range(3)]
    return {(modes[i], modes[j]): float(modal[i, j]) for i in range(24) for j in range(24)}


MODAL_VALUE = modal_stiffness()
CORNER_DIAG = float(element_stiffness()[0, 0])


def pack_x_kernel(load, disp, dens, mask, low, up, flags, done):
    copies = [(mask.at[RX - 3 : RX], flags.at[0:3]), (mask.at[0:4], flags.at[3:7])]
    for c in range(3):
        copies.append((load.at[c, RX - 3 : RX], low.at[3 * c : 3 * c + 3]))
        copies.append((load.at[c, 0:4], up.at[4 * c : 4 * c + 4]))
        copies.append((disp.at[c, RX - 1 : RX], low.at[17 + c : 18 + c]))
        copies.append((disp.at[c, 0:2], up.at[21 + 2 * c : 23 + 2 * c]))
    copies.append((dens.at[RX - 5 : RX], low.at[12:17]))
    copies.append((dens.at[0:5], up.at[16:21]))
    copies = [
        pltpu.make_async_copy(source, target, done.at[n])
        for n, (source, target) in enumerate(copies)
    ]
    for copy in copies:
        copy.start()
    for copy in copies:
        copy.wait()
    low[9:12] = (1 - flags[0:3]).astype(F32)
    up[12:16] = (1 - flags[3:7]).astype(F32)


def loads_kernel(nodes, forces, out):
    first_x = (lax.axis_index("x") * lax.axis_size("y") + lax.axis_index("y")) * RX - 3
    first_y = (lax.axis_index("z") * lax.axis_size("c") + lax.axis_index("c")) * RY
    count = (NI - 1) * RY
    chunk = 256
    place = lax.broadcasted_iota(jnp.int32, (count, chunk), 0)
    depth = lax.broadcasted_iota(jnp.int32, (NZ, chunk), 0)
    total = jnp.zeros((9 * count, NZ), F32)
    for start in range(0, nodes.shape[1], chunk):
        cols = slice(start, start + chunk)
        local_x = nodes[0:1, cols] - first_x
        local_y = nodes[1:2, cols] - first_y
        inside = (local_x >= 0) & (local_x < NI - 1) & (local_y >= 0) & (local_y < RY)
        spot = jnp.where(inside, local_x * RY + local_y, -1)
        hit = place == spot
        layer = jnp.where(depth == nodes[2:3, cols], 1.0, 0.0).astype(jnp.bfloat16)
        parts = []
        for c in range(3):
            rest = forces[c : c + 1, cols]
            for _ in range(3):
                head = rest.astype(jnp.bfloat16).astype(F32)
                rest = rest - head
                parts.append(jnp.where(hit, head, 0.0).astype(jnp.bfloat16))
        total = total + lax.dot_general(
            jnp.concatenate(parts, axis=0),
            layer,
            (((1,), (1,)), ((), ())),
            preferred_element_type=F32,
        )
    for c in range(3):
        base = 3 * c * count
        summed = (
            total[base : base + count]
            + total[base + count : base + 2 * count]
            + total[base + 2 * count : base + 3 * count]
        )
        out[c] = summed.reshape(NI - 1, RY, NZ)


def pack_y_kernel(load, disp, dens, mask, placed, low, up, ld, fr, dn, di, first, second):
    for c in range(3):
        ld[c, 0:3] = low[3 * c : 3 * c + 3] + placed[c, 0:3]
        ld[c, 3 : 3 + RX] = load[c] + placed[c, 3 : 3 + RX]
        ld[c, 3 + RX : 7 + RX] = up[4 * c : 4 * c + 4] + placed[c, 3 + RX : 7 + RX]
        di[c, 0] = low[17 + c]
        di[c, 1 : 1 + RX] = disp[c]
        di[c, 1 + RX : 3 + RX] = up[21 + 2 * c : 23 + 2 * c]
    fr[0:3] = low[9:12]
    fr[3 : 3 + RX] = (1 - mask[...]).astype(F32)
    fr[3 + RX : 7 + RX] = up[12:16]
    dn[0:5] = low[12:17]
    dn[5 : 5 + RX] = dens[...]
    dn[5 + RX : 10 + RX] = up[16:21]
    even = lax.axis_index("c") == 0

    def rows_for_upper(out):
        for c in range(3):
            out[19 * c : 19 * c + 19] = ld[c, :, 4:8]
        out[57:76] = fr[:, 4:8]
        out[76:98] = dn[:, 4:8]
        for p in range(22):
            out[98 + p // 4, p % 4 : p % 4 + 1] = dn[p, 3:4]
        for n in range(45):
            out[104 + n // 4, n % 4 : n % 4 + 1] = di[n // 15, n % 15, 7:8]

    def rows_for_lower(out):
        for c in range(3):
            out[19 * c : 19 * c + 19] = ld[c, :, 0:4]
        out[57:76] = fr[:, 0:4]
        out[76:98] = dn[:, 0:4]
        for p in range(22):
            out[98 + p // 4, p % 4 : p % 4 + 1] = dn[p, 4:5]
        for n in range(45):
            out[104 + n // 2, 2 * (n % 2) : 2 * (n % 2) + 2] = di[n // 15, n % 15, 0:2]

    @pl.when(even)
    def _():
        rows_for_upper(first)
        rows_for_lower(second)

    @pl.when(jnp.logical_not(even))
    def _():
        rows_for_lower(first)
        rows_for_upper(second)


def up_z(v, lane):
    return jnp.where(lane < NZ - 1, pltpu.roll(v, NZ - 1, 1), 0.0)


def down_z(v, lane):
    return jnp.where(lane > 0, pltpu.roll(v, 1, 1), 0.0)


def axes(*ones):
    return tuple(int(n in ones) for n in range(3))


K_SHEAR = MODAL_VALUE[axes(1) + (0,), axes(0) + (1,)]
K_NORMAL = MODAL_VALUE[axes(0) + (0,), axes(0) + (0,)]
K_CROSS = MODAL_VALUE[axes(0) + (0,), axes(1) + (1,)]
K_BEND = MODAL_VALUE[axes(0, 1) + (0,), axes(0, 1) + (0,)]
K_BEND_OFF = MODAL_VALUE[axes(0, 1) + (0,), axes(1, 2) + (2,)]
K_TWIST = MODAL_VALUE[axes(0, 1) + (2,), axes(0, 2) + (1,)]
K_LAST = MODAL_VALUE[axes(0, 1, 2) + (0,), axes(0, 1, 2) + (0,)]
PAIRS = [(0, 1), (0, 2), (1, 2)]
BENDS = [(0, 1, 2), (1, 0, 2), (0, 2, 1)]


def combine(h):
    out = {}
    for d, e in PAIRS:
        out["s", d, e] = h[axes(e) + (d,)] + h[axes(d) + (e,)]
    normal = [h[axes(d) + (d,)] for d in range(3)]
    total = normal[0] + normal[1] + normal[2]
    for d in range(3):
        out["n", d] = normal[d] * ((K_NORMAL - K_CROSS) / K_CROSS) + total
    for d, e, f in BENDS:
        one, two = h[axes(d, e) + (d,)], h[axes(e, f) + (f,)]
        out["b", d, e] = one * (K_BEND / K_BEND_OFF) + two
        out["b", f, e] = two * (K_BEND / K_BEND_OFF) + one
    twist = [h[axes(*[n for n in range(3) if n != d]) + (d,)] for d in range(3)]
    total = twist[0] + twist[1] + twist[2]
    for d in range(3):
        out["t", d] = twist[d] + total
        out["l", d] = h[axes(0, 1, 2) + (d,)]
    return out


SCALES = {"s": K_SHEAR, "n": K_CROSS, "b": K_BEND_OFF, "t": K_TWIST, "l": K_LAST}


def mode_of(key):
    kind = key[0]
    if kind == "s":
        return axes(key[2]) + (key[1],)
    if kind == "n":
        return axes(key[1]) + (key[1],)
    if kind == "b":
        return axes(key[1], key[2]) + (key[1],)
    if kind == "t":
        return axes(*[n for n in range(3) if n != key[1]]) + (key[1],)
    return axes(0, 1, 2) + (key[1],)


def modes_of(near, far):
    result = {}
    for key in near:
        c, b, s = key
        result[0, b, s, c] = near[key] + far[key]
        result[1, b, s, c] = far[key] - near[key]
    return result


KEYS = [("s", d, e) for d, e in PAIRS] + [("n", d) for d in range(3)]
KEYS += [("b", d, e) for d, e, f in BENDS] + [("b", f, e) for d, e, f in BENDS]
KEYS += [("t", d) for d in range(3)] + [("l", d) for d in range(3)]
NUMBER = {key: n for n, key in enumerate(KEYS)}
PARTS = [(c, s) for c in range(3) for s in (0, 1)]


def main_kernel(ld, fr, dn, di, first, second, basis, senses, sums, L1, FR1, D1, DN, MOD, SC, HP, W, Z, G, DS, SS, F, DV):
    gx = lax.axis_index("x") * lax.axis_size("y") + lax.axis_index("y")
    gy = lax.axis_index("z") * lax.axis_size("c") + lax.axis_index("c")
    extent_x = RX * lax.axis_size("x") * lax.axis_size("y")
    extent_y = RY * lax.axis_size("z") * lax.axis_size("c")
    lane = lax.broadcasted_iota(jnp.int32, (8, NZ), 1)
    row = lax.broadcasted_iota(jnp.int32, (8, NZ), 0)
    upper_half = row < 4

    DN[:, 16:24] = dn[...]
    D1[...] = jnp.zeros(D1.shape, F32)

    def fill(below, above):
        for c in range(3):
            L1[c, :, 0:4] = above[19 * c : 19 * c + 19]
            L1[c, :, 4:8] = below[19 * c : 19 * c + 19]
        FR1[:, 0:4] = above[57:76]
        FR1[:, 4:8] = below[57:76]
        DN[:, 12:16] = below[76:98]
        DN[:, 24:28] = above[76:98]
        for p in range(22):
            DN[p, 11:12] = below[98 + p // 4, p % 4 : p % 4 + 1]
            DN[p, 28:29] = above[98 + p // 4, p % 4 : p % 4 + 1]
        for n in range(45):
            D1[n // 15, n % 15, 7:8] = below[104 + n // 4, n % 4 : n % 4 + 1]
            D1[n // 15, n % 15, 0:2] = above[104 + n // 2, 2 * (n % 2) : 2 * (n % 2) + 2]

    even = lax.axis_index("c") == 0

    @pl.when(even)
    def _():
        fill(second, first)

    @pl.when(jnp.logical_not(even))
    def _():
        fill(first, second)

    load_of = lambda c, i, t: (L1 if t else ld)[c, i - 1]
    free_of = lambda i, t: (FR1 if t else fr)[i - 1]
    disp_of = lambda c, p, t: (D1 if t else di)[c, p]

    near_z = 2.0 - jnp.where(lane == 0, 1.0, 0.0) - jnp.where(lane == NZ - 1, 1.0, 0.0)
    inside_y, part_a, part_b = [], [], []
    for t in range(2):
        place_y = gy * RY + (row if t == 0 else jnp.where(upper_half, row + 8, row - 8))
        inside_y.append(jnp.where((place_y >= 0) & (place_y < extent_y), 1.0, 0.0))
        near_y = 2.0 - jnp.where(place_y == 0, 1.0, 0.0) - jnp.where(place_y == extent_y - 1, 1.0, 0.0)
        part_a.append(1.5 + 0.5 * (near_y + near_z) + EDGE * near_y * near_z)
        part_b.append(0.5 + EDGE * (near_y + near_z))

    def filter_parts(cells, beside):
        deep = up_z(cells, lane) + down_z(cells, lane)
        deep_beside = up_z(beside, lane) + down_z(beside, lane)
        around = deep + beside
        return (
            1.5 * cells + 0.5 * around + EDGE * deep_beside,
            0.5 * cells + EDGE * around,
        )

    def density_rows(p, t, shift):
        if t == 0:
            return DN[p, 16 + shift : 24 + shift]
        return jnp.where(
            upper_half, DN[p, 24 + shift : 32 + shift], DN[p, 8 + shift : 16 + shift]
        )

    for t in range(2):
        window = []
        for p in range(NI + 2):
            beside = density_rows(p, t, -1) + density_rows(p, t, 1)
            window.append(filter_parts(density_rows(p, t, 0), beside))
            i = p - 2
            if i < 0:
                continue
            place_x = gx * RX - 4 + i
            inside_x = jnp.where((place_x >= 0) & (place_x < extent_x), 1.0, 0.0)
            near_x = 2.0 - jnp.where(place_x == 0, 1.0, 0.0) - jnp.where(place_x == extent_x - 1, 1.0, 0.0)
            inverse = 1.0 / (part_a[t] + near_x * part_b[t])
            physical = (window[-2][0] + window[-3][1] + window[-1][1]) * inverse
            squared = physical * physical
            inside = inside_y[t] * inside_x
            mod = inside * (SOFT + (1.0 - SOFT) * (squared * physical))
            MOD[i, t] = mod
            if 3 <= i <= NI - 4:
                SC[i - 3, t] = (inside * (PENALTY * (1.0 - SOFT))) * (squared * inverse)
            deep = mod + down_z(mod, lane)
            HP[i, 8 + 8 * t : 16 + 8 * t] = deep
            if t == 1:
                HP[i, 0:8] = deep

    zero = jnp.zeros((8, NZ), F32)

    def store_parts(c, i, t, v):
        above = up_z(v, lane)
        for s, part in ((0, v + above), (1, above - v)):
            G[2 * c + s, i, 8 * t : 8 * t + 8] = part
            if t == 0:
                G[2 * c + s, i, 16:24] = part

    def in_block(i, t):
        return t == 0 and 4 <= i < 4 + RX

    bz = zero
    for t in range(2):
        before = None
        for i in range(NI):
            summed = HP[i, 8 + 8 * t : 16 + 8 * t] + HP[i, 7 + 8 * t : 15 + 8 * t]
            if i > 0:
                inverse = jnp.where(free_of(i, t) > 0.5, (1.0 / CORNER_DIAG) / (summed + before), 0.0)
                W[i, t] = inverse
                for c in range(3):
                    load = load_of(c, i, t)
                    z = inverse * load
                    Z[0, c, i, t] = z
                    store_parts(c, i, t, z)
                    if in_block(i, t):
                        bz = bz + z * load
            before = summed

    def yz_modes(i, t):
        result = {}
        for c, s in PARTS:
            part = G[2 * c + s, i, 8 * t : 8 * t + 8]
            higher = G[2 * c + s, i, 8 * t + 1 : 8 * t + 9]
            result[c, 0, s] = part + higher
            result[c, 1, s] = higher - part
        return result

    def apply(k):
        for t in range(2):
            near = yz_modes(1 + k, t)
            passed = None
            for i in range(1 + k, NI - 1 - k):
                far = yz_modes(i + 1, t)
                modes = modes_of(near, far)
                mixed = combine(modes)
                if 3 <= i <= NI - 4:
                    energy = None
                    for key, n in NUMBER.items():
                        factor = mixed[key] if key[0] == "s" else modes[mode_of(key)]
                        term = factor * F[n, i - 3, t]
                        energy = term if energy is None else energy + term
                    value = energy * SC[i - 3, t]
                    DV[k, i - 3, 8 + 8 * t : 16 + 8 * t] = value
                    if t == 1:
                        DV[k, i - 3, 0:8] = value
                young = MOD[i, t]
                scaled = {kind: young * factor for kind, factor in SCALES.items()}
                forces = {}
                for key, value in mixed.items():
                    force = scaled[key[0]] * value
                    forces[mode_of(key)] = force
                    if key[0] == "s":
                        forces[axes(key[1]) + (key[2],)] = force
                following = {}
                for c, s in PARTS:
                    node = {}
                    for b in (0, 1):
                        slope = forces[1, b, s, c]
                        if (0, b, s, c) in forces:
                            level = forces[0, b, s, c]
                            low, following[c, b, s] = level - slope, level + slope
                            node[b] = low if passed is None else passed[c, b, s] + low
                        else:
                            following[c, b, s] = slope
                            node[b] = -slope if passed is None else passed[c, b, s] - slope
                    if i > 1 + k:
                        DS[2 * c + s, i, t] = node[0] - node[1]
                        both = node[0] + node[1]
                        SS[2 * c + s, i, 8 + 8 * t : 16 + 8 * t] = both
                        if t == 1:
                            SS[2 * c + s, i, 0:8] = both
                passed, near = following, far

    def image(c, i, t):
        level, slope = [
            DS[2 * c + s, i, t] + SS[2 * c + s, i, 7 + 8 * t : 15 + 8 * t] for s in (0, 1)
        ]
        return level - slope + down_z(level + slope, lane)

    for p in range(RX + 3):
        for t in range(2):
            for c in range(3):
                v = disp_of(c, p, t)
                above = up_z(v, lane)
                for s, part in ((0, v + above), (1, above - v)):
                    SS[2 * c + s, p, 8 * t : 8 * t + 8] = part
                    if t == 0:
                        SS[2 * c + s, p, 16:24] = part
    for t in range(2):
        near = None
        for p in range(RX + 3):
            far = {}
            for c, s in PARTS:
                part = SS[2 * c + s, p, 8 * t : 8 * t + 8]
                higher = SS[2 * c + s, p, 8 * t + 1 : 8 * t + 9]
                far[c, 0, s] = part + higher
                far[c, 1, s] = higher - part
            if near is not None:
                for key, value in combine(modes_of(near, far)).items():
                    F[NUMBER[key], p - 1, t] = value * SCALES[key[0]]
            near = far

    def add(total, i, t, one, two):
        return total + one * two if in_block(i, t) else total

    h00 = b1 = h01 = h11 = b2 = h12 = h22 = h02 = zero
    apply(0)
    for t in range(2):
        for i in range(2, NI - 1):
            for c in range(3):
                q = image(c, i, t)
                z = Z[0, c, i, t]
                y = W[i, t] * q - z
                Z[1, c, i, t] = y
                store_parts(c, i, t, y)
                h00 = add(h00, i, t, z, q)
                h01 = add(h01, i, t, y, q)
                if in_block(i, t):
                    b1 = b1 + y * load_of(c, i, t)
    apply(1)
    for t in range(2):
        for i in range(3, NI - 2):
            for c in range(3):
                q = image(c, i, t)
                z = Z[1, c, i, t]
                y = W[i, t] * q - z
                Z[2, c, i, t] = y
                store_parts(c, i, t, y)
                h11 = add(h11, i, t, z, q)
                h12 = add(h12, i, t, y, q)
                if in_block(i, t):
                    b2 = b2 + y * load_of(c, i, t)
    apply(2)
    for i in range(4, 4 + RX):
        for c in range(3):
            q = image(c, i, 0)
            h22 = add(h22, i, 0, Z[2, c, i, 0], q)
            h02 = add(h02, i, 0, Z[0, c, i, 0], q)

    lanes = lax.broadcasted_iota(jnp.int32, (1, NZ), 1)
    line = jnp.zeros((1, NZ), F32)
    for n, value in enumerate((bz, b1, b2, h00, h01, h02, h11, h12, h22)):
        whole = jnp.sum(value, axis=0, keepdims=True)
        whole = jnp.sum(whole, axis=1, keepdims=True)
        line = line + jnp.where(lanes == n, whole, 0.0)
    for n in range(sums.shape[0]):
        sums[n] = line

    for k in range(3):
        window = []
        for p in range(RX + 2):
            beside = DV[k, p, 7:15] + DV[k, p, 9:17]
            window.append(filter_parts(DV[k, p, 8:16], beside))
            if p >= 2:
                senses[k, p - 2] = window[-2][0] + window[-3][1] + window[-1][1]
        for c in range(3):
            basis[k, c] = Z[k, c, 4 : 4 + RX, 0]


def final_kernel(gathered, basis, senses, adjoint, sensitivity):
    total = jnp.sum(gathered[...], axis=0)

    def value(n):
        return jnp.broadcast_to(total[:, n : n + 1], (1, NZ))

    b0, b1, b2, h00, h01, h02, h11, h12, h22 = [value(n) for n in range(9)]
    l1, l2 = h01 / h00, h02 / h00
    d1 = h11 - l1 * h01
    e = h12 - l1 * h02
    fine1 = d1 > 0.0
    l3 = jnp.where(fine1, e / d1, 0.0)
    d2 = h22 - l2 * h02 - l3 * e
    t1 = b1 - l1 * b0
    t2 = b2 - l2 * b0 - l3 * t1
    c2 = jnp.where(d2 > 0.0, t2 / d2, 0.0)
    c1 = jnp.where(fine1, t1 / d1, 0.0) - l3 * c2
    c0 = b0 / h00 - l1 * c1 - l2 * c2
    adjoint[...] = c0 * basis[0] + c1 * basis[1] + c2 * basis[2]
    sensitivity[...] = c0 * senses[0] + c1 * senses[1] + c2 * senses[2]


VMEM = pl.BlockSpec(memory_space=pltpu.VMEM)


def call(kernel, inputs, outs, scratch=(), limit=None):
    single = not isinstance(outs, list)
    shapes = [outs] if single else outs
    result = pl.pallas_call(
        kernel,
        out_shape=[jax.ShapeDtypeStruct(s, F32) for s in shapes],
        in_specs=[VMEM] * len(inputs),
        out_specs=[VMEM] * len(shapes),
        scratch_shapes=[pltpu.VMEM(s, F32) for s in scratch],
        compiler_params=pltpu.CompilerParams(vmem_limit_bytes=limit or 32 * 1024 * 1024),
    )(*inputs)
    return result[0] if single else result


MAIN_SCRATCH = [
    (3, NI - 1, 8, NZ),
    (NI - 1, 8, NZ),
    (3, RX + 3, 8, NZ),
    (NI + 2, 40, NZ),
    (NI, 2, 8, NZ),
    (RX + 2, 2, 8, NZ),
    (NI, 24, NZ),
    (NI, 2, 8, NZ),
    (3, 3, NI, 2, 8, NZ),
    (6, NI, 24, NZ),
    (6, NI, 2, 8, NZ),
    (6, NI, 24, NZ),
    (len(KEYS), RX + 2, 2, 8, NZ),
    (3, RX + 2, 24, NZ),
]


def shards(displacement, adjoint_load, density, fixed_mask, load_nodes, load_forces):
    gx, gy = ("x", "y"), ("z", "c")
    count_x = lax.axis_size("x") * lax.axis_size("y")
    count_y = lax.axis_size("z") * lax.axis_size("c")
    own = (adjoint_load, displacement, density, fixed_mask)
    low, up = pl.pallas_call(
        pack_x_kernel,
        out_shape=[
            jax.ShapeDtypeStruct((LOW_X, RY, NZ), F32),
            jax.ShapeDtypeStruct((UP_X, RY, NZ), F32),
        ],
        in_specs=[pl.BlockSpec(memory_space=pl.ANY)] * 4,
        out_specs=[VMEM] * 2,
        scratch_shapes=[
            pltpu.VMEM((7, RY, NZ), jnp.int32),
            pltpu.SemaphoreType.DMA((16,)),
        ],
    )(*own)
    low = lax.ppermute(low, gx, [(i, i + 1) for i in range(count_x - 1)])
    up = lax.ppermute(up, gx, [(i + 1, i) for i in range(count_x - 1)])
    placed = call(loads_kernel, (load_nodes, load_forces), (3, NI - 1, RY, NZ))
    ld, fr, dn, di, first, second = call(
        pack_y_kernel,
        own + (placed, low, up),
        [
            (3, NI - 1, RY, NZ),
            (NI - 1, RY, NZ),
            (NI + 2, RY, NZ),
            (3, RX + 3, RY, NZ),
            (BLOCKS, 4, NZ),
            (BLOCKS, 4, NZ),
        ],
    )
    pairs = [(i, i + 1) for i in range(1, count_y - 1, 2)]
    second = lax.ppermute(second, gy, pairs + [(j, i) for i, j in pairs])
    first = lax.ppermute(first, "c", [(0, 1), (1, 0)])
    near = lax.axis_size("c") * count_x
    far = lax.axis_size("z")
    basis, senses, sums = call(
        main_kernel,
        (ld, fr, dn, di, first, second),
        [(3, 3, RX, RY, NZ), (3, RX, RY, NZ), (near, 1, NZ)],
        MAIN_SCRATCH,
        48 * 1024 * 1024,
    )
    sums = lax.all_to_all(sums, ("x", "y", "c"), 0, 0, tiled=True)
    sums = jnp.broadcast_to(jnp.sum(sums, axis=0, keepdims=True), (far, 1, NZ))
    sums = lax.all_to_all(sums, "z", 0, 0, tiled=True)
    adjoint, sensitivity = call(
        final_kernel, (sums, basis, senses), [(3, RX, RY, NZ), (RX, RY, NZ)]
    )
    return adjoint, sensitivity


def solution(mesh):
    size_x, size_y = mesh.shape["gx"], mesh.shape["gy"]
    side = int(round(size_x**0.5))
    whole = Mesh(
        mesh.devices.reshape(side, size_x // side, size_y // 2, 2), ("x", "y", "z", "c")
    )
    field = P(None, ("x", "y"), ("z", "c"), None)
    grid = P(("x", "y"), ("z", "c"), None)
    return jax.shard_map(
        shards,
        mesh=whole,
        in_specs=(field, field, grid, grid, P(), P()),
        out_specs=(field, grid),
        check_vma=False,
    )
```

```python
import functools

import jax
import jax.numpy as jnp
import numpy as np
from jax import lax
from jax.experimental import pallas as pl
from jax.experimental.pallas import tpu as pltpu
from jax.sharding import Mesh, PartitionSpec as P

POISSON = 0.3
PENALTY = 3.0
SOFT = 0.001
CORNERS = [(a, b, c) for c in (0, 1) for b in (0, 1) for a in (0, 1)]
EDGE = float(1.5 - np.sqrt(2.0))

RX, RY, NZ = 12, 8, 128
NI = RX + 8
LOW_X, UP_X = 20, 27
NEAR, CORNER = 81, 46
CHUNK = 256
F32 = jnp.float32


def element_stiffness():
    lame_first = POISSON / ((1.0 + POISSON) * (1.0 - 2.0 * POISSON))
    shear_mod = 1.0 / (2.0 * (1.0 + POISSON))
    elastic = np.zeros((6, 6))
    elastic[:3, :3] = lame_first
    for axis_number in range(3):
        elastic[axis_number, axis_number] = lame_first + 2.0 * shear_mod
        elastic[axis_number + 3, axis_number + 3] = shear_mod
    points = [0.5 - 0.5 / np.sqrt(3.0), 0.5 + 0.5 / np.sqrt(3.0)]
    matrix = np.zeros((24, 24))
    for point_x in points:
        for point_y in points:
            for point_z in points:
                coords = (point_x, point_y, point_z)
                strain = np.zeros((6, 24))
                for number, corner in enumerate(CORNERS):
                    factors = [coords[d] if corner[d] else 1.0 - coords[d] for d in range(3)]
                    slopes = [1.0 if corner[d] else -1.0 for d in range(3)]
                    derivs = [
                        slopes[0] * factors[1] * factors[2],
                        factors[0] * slopes[1] * factors[2],
                        factors[0] * factors[1] * slopes[2],
                    ]
                    column = 3 * number
                    strain[0, column] = derivs[0]
                    strain[1, column + 1] = derivs[1]
                    strain[2, column + 2] = derivs[2]
                    strain[3, column] = derivs[1]
                    strain[3, column + 1] = derivs[0]
                    strain[4, column + 1] = derivs[2]
                    strain[4, column + 2] = derivs[1]
                    strain[5, column] = derivs[2]
                    strain[5, column + 2] = derivs[0]
                matrix += strain.T @ elastic @ strain / 8.0
    return matrix


def modal_stiffness():
    one = np.array([[1.0, 1.0], [-1.0, 1.0]])
    change = np.zeros((8, 8))
    for row, (a, b, c) in enumerate(CORNERS):
        for column, (p, q, r) in enumerate(CORNERS):
            change[row, column] = one[a, p] * one[b, q] * one[c, r]
    inverse = np.linalg.inv(np.kron(change, np.eye(3)))
    modal = inverse.T @ element_stiffness() @ inverse
    modes = [corner + (d,) for corner in CORNERS for d in range(3)]
    return {(modes[i], modes[j]): float(modal[i, j]) for i in range(24) for j in range(24)}


MODAL_VALUE = modal_stiffness()
CORNER_DIAG = float(element_stiffness()[0, 0])


def pack_x_kernel(load, disp, dens, mask, low, up, flags, done):
    copies = [(mask.at[RX - 3 : RX], flags.at[0:3]), (mask.at[0:4], flags.at[3:7])]
    for c in range(3):
        copies.append((load.at[c, RX - 3 : RX], low.at[3 * c : 3 * c + 3]))
        copies.append((load.at[c, 0:4], up.at[4 * c : 4 * c + 4]))
        copies.append((disp.at[c, RX - 1 : RX], low.at[17 + c : 18 + c]))
        copies.append((disp.at[c, 0:2], up.at[21 + 2 * c : 23 + 2 * c]))
    copies.append((dens.at[RX - 5 : RX], low.at[12:17]))
    copies.append((dens.at[0:5], up.at[16:21]))
    copies = [
        pltpu.make_async_copy(source, target, done.at[n])
        for n, (source, target) in enumerate(copies)
    ]
    for copy in copies:
        copy.start()
    for copy in copies:
        copy.wait()
    low[9:12] = (1 - flags[0:3]).astype(F32)
    up[12:16] = (1 - flags[3:7]).astype(F32)


def loads_kernel(nodes, forces, _, out):
    first_x = (lax.axis_index("x") * lax.axis_size("y") + lax.axis_index("y")) * RX - 3
    first_y = (lax.axis_index("z") * lax.axis_size("c") + lax.axis_index("c")) * RY
    count = (NI - 1) * RY
    chunk = CHUNK
    place = lax.broadcasted_iota(jnp.int32, (count, chunk), 0)
    depth = lax.broadcasted_iota(jnp.int32, (2 * NZ, chunk), 0)
    total = jnp.zeros((9 * count, 2 * NZ), F32)
    for start in range(0, nodes.shape[1], chunk):
        cols = slice(start, start + chunk)
        local_x = nodes[0:1, cols] - first_x
        local_y = nodes[1:2, cols] - first_y
        inside = (local_x >= 0) & (local_x < NI - 1) & (local_y >= -4) & (local_y < RY + 4)
        spot = jnp.where(inside, local_x * RY + (local_y & (RY - 1)), -1)
        hit = place == spot
        outer = jnp.where((local_y < 0) | (local_y >= RY), NZ, 0)
        layer = jnp.where(depth == nodes[2:3, cols] + outer, 1.0, 0.0).astype(jnp.bfloat16)
        parts = []
        for c in range(3):
            rest = forces[c : c + 1, cols]
            for _ in range(3):
                head = rest.astype(jnp.bfloat16).astype(F32)
                rest = rest - head
                parts.append(jnp.where(hit, head, 0.0).astype(jnp.bfloat16))
        total = total + lax.dot_general(
            jnp.concatenate(parts, axis=0),
            layer,
            (((1,), (1,)), ((), ())),
            preferred_element_type=F32,
        )
    for c in range(3):
        base = 3 * c * count
        summed = (
            total[base : base + count]
            + total[base + count : base + 2 * count]
            + total[base + 2 * count : base + 3 * count]
        )
        for t in range(2):
            out[c, :, t] = summed[:, t * NZ : t * NZ + NZ].reshape(NI - 1, RY, NZ)


def pack_y_kernel(which, load, disp, dens, mask, low, up, *rest):
    out = rest[-1]

    def write(rows, extra, count, at):
        free = lambda part: (1 - part).astype(F32)
        for c in range(3):
            out[12 * c : 12 * c + 12] = load[c, :, rows]
            q = NEAR + 7 * c
            out[q : q + 3] = low[3 * c : 3 * c + 3, rows]
            out[q + 3 : q + 7] = up[4 * c : 4 * c + 4, rows]
        out[36:48] = free(mask[:, rows])
        out[48:60] = dens[:, rows]
        q = NEAR + 21
        out[q : q + 3] = low[9:12, rows]
        out[q + 3 : q + 7] = up[12:16, rows]
        out[q + 7 : q + 12] = low[12:17, rows]
        out[q + 12 : q + 17] = up[16:21, rows]
        for p in range(12):
            out[60 + p // 4, p % 4 : p % 4 + 1] = dens[p, extra : extra + 1]
        for r in range(10):
            source = low[12 + r, extra : extra + 1] if r < 5 else up[11 + r, extra : extra + 1]
            out[NEAR + 38 + r // 4, r % 4 : r % 4 + 1] = source
        per = 4 // count
        for n in range(36):
            spot = count * (n % per)
            out[63 + n // per, spot : spot + count] = disp[n // 12, n % 12, at : at + count]
        for n in range(9):
            c, m = n // 3, n % 3
            source = low[17 + c] if m == 0 else up[20 + 2 * c + m]
            spot = count * (n % per)
            out[NEAR + 41 + n // per, spot : spot + count] = source[at : at + count]

    upper = lax.axis_index("c") == which

    @pl.when(upper)
    def _():
        write(slice(4, 8), 3, 1, 7)

    @pl.when(jnp.logical_not(upper))
    def _():
        write(slice(0, 4), 4, 2, 0)


def up_z(v, lane):
    return jnp.where(lane < NZ - 1, pltpu.roll(v, NZ - 1, 1), 0.0)


def down_z(v, lane):
    return jnp.where(lane > 0, pltpu.roll(v, 1, 1), 0.0)


def axes(*ones):
    return tuple(int(n in ones) for n in range(3))


K_SHEAR = MODAL_VALUE[axes(1) + (0,), axes(0) + (1,)]
K_NORMAL = MODAL_VALUE[axes(0) + (0,), axes(0) + (0,)]
K_CROSS = MODAL_VALUE[axes(0) + (0,), axes(1) + (1,)]
K_BEND = MODAL_VALUE[axes(0, 1) + (0,), axes(0, 1) + (0,)]
K_BEND_OFF = MODAL_VALUE[axes(0, 1) + (0,), axes(1, 2) + (2,)]
K_TWIST = MODAL_VALUE[axes(0, 1) + (2,), axes(0, 2) + (1,)]
K_LAST = MODAL_VALUE[axes(0, 1, 2) + (0,), axes(0, 1, 2) + (0,)]
PAIRS = [(0, 1), (0, 2), (1, 2)]
BENDS = [(0, 1, 2), (1, 0, 2), (0, 2, 1)]


def combine(h):
    out = {}
    for d, e in PAIRS:
        out["s", d, e] = h[axes(e) + (d,)] + h[axes(d) + (e,)]
    normal = [h[axes(d) + (d,)] for d in range(3)]
    total = normal[0] + normal[1] + normal[2]
    for d in range(3):
        out["n", d] = normal[d] * ((K_NORMAL - K_CROSS) / K_CROSS) + total
    for d, e, f in BENDS:
        one, two = h[axes(d, e) + (d,)], h[axes(e, f) + (f,)]
        out["b", d, e] = one * (K_BEND / K_BEND_OFF) + two
        out["b", f, e] = two * (K_BEND / K_BEND_OFF) + one
    twist = [h[axes(*[n for n in range(3) if n != d]) + (d,)] for d in range(3)]
    total = twist[0] + twist[1] + twist[2]
    for d in range(3):
        out["t", d] = twist[d] + total
        out["l", d] = h[axes(0, 1, 2) + (d,)]
    return out


SCALES = {"s": K_SHEAR, "n": K_CROSS, "b": K_BEND_OFF, "t": K_TWIST, "l": K_LAST}


def mode_of(key):
    kind = key[0]
    if kind == "s":
        return axes(key[2]) + (key[1],)
    if kind == "n":
        return axes(key[1]) + (key[1],)
    if kind == "b":
        return axes(key[1], key[2]) + (key[1],)
    if kind == "t":
        return axes(*[n for n in range(3) if n != key[1]]) + (key[1],)
    return axes(0, 1, 2) + (key[1],)


def modes_of(near, far):
    result = {}
    for key in near:
        c, b, s = key
        result[0, b, s, c] = near[key] + far[key]
        result[1, b, s, c] = far[key] - near[key]
    return result


KEYS = [("s", d, e) for d, e in PAIRS] + [("n", d) for d in range(3)]
KEYS += [("b", d, e) for d, e, f in BENDS] + [("b", f, e) for d, e, f in BENDS]
KEYS += [("t", d) for d in range(3)] + [("l", d) for d in range(3)]
NUMBER = {key: n for n, key in enumerate(KEYS)}
PARTS = [(c, s) for c in range(3) for s in (0, 1)]


def main_kernel(load, disp, dens, mask, low, up, placed, first, second, basis, senses, sums, L0, L1, FR1, D1, DN, MOD, SC, HP, W, Z, G, DS, SS, F, DV):
    gx = lax.axis_index("x") * lax.axis_size("y") + lax.axis_index("y")
    gy = lax.axis_index("z") * lax.axis_size("c") + lax.axis_index("c")
    extent_x = RX * lax.axis_size("x") * lax.axis_size("y")
    extent_y = RY * lax.axis_size("z") * lax.axis_size("c")
    lane = lax.broadcasted_iota(jnp.int32, (8, NZ), 1)
    row = lax.broadcasted_iota(jnp.int32, (8, NZ), 0)
    upper_half = row < 4

    DN[0:5, 16:24] = low[12:17]
    DN[5 : 5 + RX, 16:24] = dens[...]
    DN[5 + RX : 10 + RX, 16:24] = up[16:21]
    D1[...] = jnp.zeros(D1.shape, F32)

    def fill(below, above):
        below_corner, above_corner = below.at[NEAR : NEAR + CORNER], above.at[NEAR : NEAR + CORNER]
        for rows, near, corner in (
            (slice(0, 4), above, above_corner),
            (slice(4, 8), below, below_corner),
        ):
            for c in range(3):
                L1[c, 0:3, rows] = corner[7 * c : 7 * c + 3]
                L1[c, 3:15, rows] = near[12 * c : 12 * c + 12]
                L1[c, 15:19, rows] = corner[7 * c + 3 : 7 * c + 7]
            FR1[0:3, rows] = corner[21:24]
            FR1[3:15, rows] = near[36:48]
            FR1[15:19, rows] = corner[24:28]
        for rows, extra, near, corner in (
            (slice(24, 28), 28, above, above_corner),
            (slice(12, 16), 11, below, below_corner),
        ):
            DN[0:5, rows] = corner[28:33]
            DN[5:17, rows] = near[48:60]
            DN[17:22, rows] = corner[33:38]
            for p in range(22):
                if 5 <= p < 17:
                    one = near[60 + (p - 5) // 4, (p - 5) % 4 : (p - 5) % 4 + 1]
                else:
                    r = p if p < 5 else p - 12
                    one = corner[38 + r // 4, r % 4 : r % 4 + 1]
                DN[p, extra : extra + 1] = one
        for c in range(3):
            for p in range(12):
                n = 12 * c + p
                D1[c, p + 1, 7:8] = below[63 + n // 4, n % 4 : n % 4 + 1]
                D1[c, p + 1, 0:2] = above[63 + n // 2, 2 * (n % 2) : 2 * (n % 2) + 2]
            for m, p in enumerate((0, 13, 14)):
                n = 3 * c + m
                D1[c, p, 7:8] = below_corner[41 + n // 4, n % 4 : n % 4 + 1]
                D1[c, p, 0:2] = above_corner[41 + n // 2, 2 * (n % 2) : 2 * (n % 2) + 2]

    even = lax.axis_index("c") == 0

    @pl.when(even)
    def _():
        fill(second, first)

    @pl.when(jnp.logical_not(even))
    def _():
        fill(first, second)

    def load_of(c, i, t):
        if t == 1:
            value = L1[c, i - 1]
        elif i < 4:
            value = low[3 * c + i - 1]
        elif i < 4 + RX:
            value = load[c, i - 4]
        else:
            value = up[4 * c + i - 4 - RX]
        return value + placed[c, i - 1, t]

    def is_free(i, t):
        if t == 1:
            return FR1[i - 1] > 0.5
        if i < 4:
            return low[9 + i - 1] > 0.5
        if i < 4 + RX:
            return mask[i - 4] == 0
        return up[12 + i - 4 - RX] > 0.5

    def disp_of(c, p, t):
        if t == 1:
            return D1[c, p]
        if p == 0:
            return low[17 + c]
        return disp[c, p - 1] if p <= RX else up[21 + 2 * c + p - 1 - RX]

    near_z = 2.0 - jnp.where(lane == 0, 1.0, 0.0) - jnp.where(lane == NZ - 1, 1.0, 0.0)
    inside_y, part_a, part_b = [], [], []
    for t in range(2):
        place_y = gy * RY + (row if t == 0 else jnp.where(upper_half, row + 8, row - 8))
        inside_y.append(jnp.where((place_y >= 0) & (place_y < extent_y), 1.0, 0.0))
        near_y = 2.0 - jnp.where(place_y == 0, 1.0, 0.0) - jnp.where(place_y == extent_y - 1, 1.0, 0.0)
        part_a.append(1.5 + 0.5 * (near_y + near_z) + EDGE * near_y * near_z)
        part_b.append(0.5 + EDGE * (near_y + near_z))

    def filter_parts(cells, beside):
        deep = up_z(cells, lane) + down_z(cells, lane)
        deep_beside = up_z(beside, lane) + down_z(beside, lane)
        around = deep + beside
        return (
            1.5 * cells + 0.5 * around + EDGE * deep_beside,
            0.5 * cells + EDGE * around,
        )

    def density_rows(p, t, shift):
        if t == 0:
            return DN[p, 16 + shift : 24 + shift]
        return jnp.where(
            upper_half, DN[p, 24 + shift : 32 + shift], DN[p, 8 + shift : 16 + shift]
        )

    for t in range(2):
        window = []
        for p in range(NI + 2):
            beside = density_rows(p, t, -1) + density_rows(p, t, 1)
            window.append(filter_parts(density_rows(p, t, 0), beside))
            i = p - 2
            if i < 0:
                continue
            place_x = gx * RX - 4 + i
            inside_x = jnp.where((place_x >= 0) & (place_x < extent_x), 1.0, 0.0)
            near_x = 2.0 - jnp.where(place_x == 0, 1.0, 0.0) - jnp.where(place_x == extent_x - 1, 1.0, 0.0)
            inverse = 1.0 / (part_a[t] + near_x * part_b[t])
            physical = (window[-2][0] + window[-3][1] + window[-1][1]) * inverse
            squared = physical * physical
            inside = inside_y[t] * inside_x
            mod = inside * (SOFT + (1.0 - SOFT) * (squared * physical))
            MOD[i, t] = mod
            if 3 <= i <= NI - 4:
                SC[i - 3, t] = (inside * (PENALTY * (1.0 - SOFT))) * (squared * inverse)
            deep = mod + down_z(mod, lane)
            HP[i, 8 + 8 * t : 16 + 8 * t] = deep
            if t == 1:
                HP[i, 0:8] = deep

    zero = jnp.zeros((8, NZ), F32)

    def store_parts(c, i, t, v):
        above = up_z(v, lane)
        for s, part in ((0, v + above), (1, above - v)):
            G[2 * c + s, i, 8 * t : 8 * t + 8] = part
            if t == 0:
                G[2 * c + s, i, 16:24] = part

    def in_block(i, t):
        return t == 0 and 4 <= i < 4 + RX

    bz = zero
    for t in range(2):
        before = None
        for i in range(NI):
            summed = HP[i, 8 + 8 * t : 16 + 8 * t] + HP[i, 7 + 8 * t : 15 + 8 * t]
            if i > 0:
                inverse = jnp.where(is_free(i, t), (1.0 / CORNER_DIAG) / (summed + before), 0.0)
                W[i, t] = inverse
                for c in range(3):
                    here = load_of(c, i, t)
                    z = inverse * here
                    Z[0, c, i, t] = z
                    store_parts(c, i, t, z)
                    if in_block(i, t):
                        L0[c, i - 4] = here
                        bz = bz + z * here
            before = summed

    def yz_modes(i, t):
        result = {}
        for c, s in PARTS:
            part = G[2 * c + s, i, 8 * t : 8 * t + 8]
            higher = G[2 * c + s, i, 8 * t + 1 : 8 * t + 9]
            result[c, 0, s] = part + higher
            result[c, 1, s] = higher - part
        return result

    def apply(k):
        for t in range(2):
            near = yz_modes(1 + k, t)
            passed = None
            for i in range(1 + k, NI - 1 - k):
                far = yz_modes(i + 1, t)
                modes = modes_of(near, far)
                mixed = combine(modes)
                if 3 <= i <= NI - 4:
                    energy = None
                    for key, n in NUMBER.items():
                        factor = mixed[key] if key[0] == "s" else modes[mode_of(key)]
                        term = factor * F[n, i - 3, t]
                        energy = term if energy is None else energy + term
                    value = energy * SC[i - 3, t]
                    DV[k, i - 3, 8 + 8 * t : 16 + 8 * t] = value
                    if t == 1:
                        DV[k, i - 3, 0:8] = value
                young = MOD[i, t]
                scaled = {kind: young * factor for kind, factor in SCALES.items()}
                forces = {}
                for key, value in mixed.items():
                    force = scaled[key[0]] * value
                    forces[mode_of(key)] = force
                    if key[0] == "s":
                        forces[axes(key[1]) + (key[2],)] = force
                following = {}
                for c, s in PARTS:
                    node = {}
                    for b in (0, 1):
                        slope = forces[1, b, s, c]
                        if (0, b, s, c) in forces:
                            level = forces[0, b, s, c]
                            low, following[c, b, s] = level - slope, level + slope
                            node[b] = low if passed is None else passed[c, b, s] + low
                        else:
                            following[c, b, s] = slope
                            node[b] = -slope if passed is None else passed[c, b, s] - slope
                    if i > 1 + k:
                        DS[2 * c + s, i, t] = node[0] - node[1]
                        both = node[0] + node[1]
                        SS[2 * c + s, i, 8 + 8 * t : 16 + 8 * t] = both
                        if t == 1:
                            SS[2 * c + s, i, 0:8] = both
                passed, near = following, far

    def image(c, i, t):
        level, slope = [
            DS[2 * c + s, i, t] + SS[2 * c + s, i, 7 + 8 * t : 15 + 8 * t] for s in (0, 1)
        ]
        return level - slope + down_z(level + slope, lane)

    for p in range(RX + 3):
        for t in range(2):
            for c in range(3):
                v = disp_of(c, p, t)
                above = up_z(v, lane)
                for s, part in ((0, v + above), (1, above - v)):
                    SS[2 * c + s, p, 8 * t : 8 * t + 8] = part
                    if t == 0:
                        SS[2 * c + s, p, 16:24] = part
    for t in range(2):
        near = None
        for p in range(RX + 3):
            far = {}
            for c, s in PARTS:
                part = SS[2 * c + s, p, 8 * t : 8 * t + 8]
                higher = SS[2 * c + s, p, 8 * t + 1 : 8 * t + 9]
                far[c, 0, s] = part + higher
                far[c, 1, s] = higher - part
            if near is not None:
                for key, value in combine(modes_of(near, far)).items():
                    F[NUMBER[key], p - 1, t] = value * SCALES[key[0]]
            near = far

    def add(total, i, t, one, two):
        return total + one * two if in_block(i, t) else total

    h00 = b1 = h01 = h11 = b2 = h12 = h22 = h02 = zero
    apply(0)
    for t in range(2):
        for i in range(2, NI - 1):
            for c in range(3):
                q = image(c, i, t)
                z = Z[0, c, i, t]
                y = W[i, t] * q - z
                Z[1, c, i, t] = y
                store_parts(c, i, t, y)
                h00 = add(h00, i, t, z, q)
                h01 = add(h01, i, t, y, q)
                if in_block(i, t):
                    b1 = b1 + y * L0[c, i - 4]
    apply(1)
    for t in range(2):
        for i in range(3, NI - 2):
            for c in range(3):
                q = image(c, i, t)
                z = Z[1, c, i, t]
                y = W[i, t] * q - z
                Z[2, c, i, t] = y
                store_parts(c, i, t, y)
                h11 = add(h11, i, t, z, q)
                h12 = add(h12, i, t, y, q)
                if in_block(i, t):
                    b2 = b2 + y * L0[c, i - 4]
    apply(2)
    for i in range(4, 4 + RX):
        for c in range(3):
            q = image(c, i, 0)
            h22 = add(h22, i, 0, Z[2, c, i, 0], q)
            h02 = add(h02, i, 0, Z[0, c, i, 0], q)

    lanes = lax.broadcasted_iota(jnp.int32, (1, NZ), 1)
    line = jnp.zeros((1, NZ), F32)
    for n, value in enumerate((bz, b1, b2, h00, h01, h02, h11, h12, h22)):
        whole = jnp.sum(value, axis=0, keepdims=True)
        whole = jnp.sum(whole, axis=1, keepdims=True)
        line = line + jnp.where(lanes == n, whole, 0.0)
    for n in range(sums.shape[0]):
        sums[n] = line

    for k in range(3):
        window = []
        for p in range(RX + 2):
            beside = DV[k, p, 7:15] + DV[k, p, 9:17]
            window.append(filter_parts(DV[k, p, 8:16], beside))
            if p >= 2:
                senses[k, p - 2] = window[-2][0] + window[-3][1] + window[-1][1]
        for c in range(3):
            basis[k, c] = Z[k, c, 4 : 4 + RX, 0]


def final_kernel(gathered, basis, senses, adjoint, sensitivity):
    total = jnp.sum(gathered[...], axis=0)

    def value(n):
        return jnp.broadcast_to(total[:, n : n + 1], (1, NZ))

    b0, b1, b2, h00, h01, h02, h11, h12, h22 = [value(n) for n in range(9)]
    l1, l2 = h01 / h00, h02 / h00
    d1 = h11 - l1 * h01
    e = h12 - l1 * h02
    fine1 = d1 > 0.0
    l3 = jnp.where(fine1, e / d1, 0.0)
    d2 = h22 - l2 * h02 - l3 * e
    t1 = b1 - l1 * b0
    t2 = b2 - l2 * b0 - l3 * t1
    c2 = jnp.where(d2 > 0.0, t2 / d2, 0.0)
    c1 = jnp.where(fine1, t1 / d1, 0.0) - l3 * c2
    c0 = b0 / h00 - l1 * c1 - l2 * c2
    adjoint[...] = c0 * basis[0] + c1 * basis[1] + c2 * basis[2]
    sensitivity[...] = c0 * senses[0] + c1 * senses[1] + c2 * senses[2]


VMEM = pl.BlockSpec(memory_space=pltpu.VMEM)


def call(kernel, inputs, outs, scratch=(), limit=None, extra=0):
    single = not isinstance(outs, list)
    shapes = [outs] if single else outs
    result = pl.pallas_call(
        kernel,
        out_shape=[jax.ShapeDtypeStruct(s, F32) for s in shapes],
        in_specs=[VMEM] * (len(inputs) - extra) + [pl.BlockSpec(memory_space=pl.ANY)] * extra,
        out_specs=[VMEM] * len(shapes),
        scratch_shapes=[pltpu.VMEM(s, F32) for s in scratch],
        compiler_params=pltpu.CompilerParams(vmem_limit_bytes=limit or 32 * 1024 * 1024),
    )(*inputs)
    return result[0] if single else result


MAIN_SCRATCH = [
    (3, RX, 8, NZ),
    (3, NI - 1, 8, NZ),
    (NI - 1, 8, NZ),
    (3, RX + 3, 8, NZ),
    (NI + 2, 40, NZ),
    (NI, 2, 8, NZ),
    (RX + 2, 2, 8, NZ),
    (NI, 24, NZ),
    (NI, 2, 8, NZ),
    (3, 3, NI, 2, 8, NZ),
    (6, NI, 24, NZ),
    (6, NI, 2, 8, NZ),
    (6, NI, 24, NZ),
    (len(KEYS), RX + 2, 2, 8, NZ),
    (3, RX + 2, 24, NZ),
]


def shards(displacement, adjoint_load, density, fixed_mask, load_nodes, load_forces):
    gx = ("x", "y")
    count_x = lax.axis_size("x") * lax.axis_size("y")
    count_y = lax.axis_size("z") * lax.axis_size("c")
    own = (adjoint_load, displacement, density, fixed_mask)
    low, up = pl.pallas_call(
        pack_x_kernel,
        out_shape=[
            jax.ShapeDtypeStruct((LOW_X, RY, NZ), F32),
            jax.ShapeDtypeStruct((UP_X, RY, NZ), F32),
        ],
        in_specs=[pl.BlockSpec(memory_space=pl.ANY)] * 4,
        out_specs=[VMEM] * 2,
        scratch_shapes=[
            pltpu.VMEM((7, RY, NZ), jnp.int32),
            pltpu.SemaphoreType.DMA((16,)),
        ],
    )(*own)
    low = lax.ppermute(low, gx, [(i, i + 1) for i in range(count_x - 1)])
    up = lax.ppermute(up, gx, [(i + 1, i) for i in range(count_x - 1)])
    sizes = (NEAR + CORNER, 4, NZ)
    second = call(functools.partial(pack_y_kernel, 1), own + (low, up), (NEAR + CORNER + 1, 4, NZ))
    pairs = [(i, i + 1) for i in range(1, count_y - 1, 2)]
    pairs = pairs + [(j, i) for i, j in pairs]
    placed = call(
        loads_kernel, (load_nodes, load_forces, low), (3, NI - 1, 2, RY, NZ), extra=1
    )
    first = call(functools.partial(pack_y_kernel, 0), own + (low, up, placed), sizes, extra=1)
    second = lax.ppermute(second, ("z", "c"), pairs)
    first = lax.ppermute(first, "c", [(0, 1), (1, 0)])
    close = lax.axis_size("c") * count_x
    far = lax.axis_size("z")
    basis, senses, sums = call(
        main_kernel,
        own + (low, up, placed, first, second),
        [(3, 3, RX, RY, NZ), (3, RX, RY, NZ), (close, 1, NZ)],
        MAIN_SCRATCH,
        48 * 1024 * 1024,
    )
    sums = lax.all_to_all(sums, ("x", "y", "c"), 0, 0, tiled=True)
    sums = jnp.broadcast_to(jnp.sum(sums, axis=0, keepdims=True), (far, 1, NZ))
    sums = lax.all_to_all(sums, "z", 0, 0, tiled=True)
    adjoint, sensitivity = call(
        final_kernel, (sums, basis, senses), [(3, RX, RY, NZ), (RX, RY, NZ)]
    )
    return adjoint, sensitivity


def solution(mesh):
    size_x, size_y = mesh.shape["gx"], mesh.shape["gy"]
    side = int(round(size_x**0.5))
    whole = Mesh(
        mesh.devices.reshape(side, size_x // side, size_y // 2, 2), ("x", "y", "z", "c")
    )
    field = P(None, ("x", "y"), ("z", "c"), None)
    grid = P(("x", "y"), ("z", "c"), None)
    return jax.shard_map(
        shards,
        mesh=whole,
        in_specs=(field, field, grid, grid, P(), P()),
        out_specs=(field, grid),
        check_vma=False,
    )
```

```python
import functools

import jax
import jax.numpy as jnp
import numpy as np
from jax import lax
from jax.experimental import pallas as pl
from jax.experimental.pallas import tpu as pltpu
from jax.sharding import Mesh, PartitionSpec as P

POISSON = 0.3
PENALTY = 3.0
SOFT = 0.001
CORNERS = [(a, b, c) for c in (0, 1) for b in (0, 1) for a in (0, 1)]
EDGE = float(1.5 - np.sqrt(2.0))

RX, RY, NZ = 12, 8, 128
NI = RX + 8
LOW_X, UP_X = 20, 27
NEAR, CORNER = 81, 46
CHUNK = 256
F32 = jnp.float32


def element_stiffness():
    lame_first = POISSON / ((1.0 + POISSON) * (1.0 - 2.0 * POISSON))
    shear_mod = 1.0 / (2.0 * (1.0 + POISSON))
    elastic = np.zeros((6, 6))
    elastic[:3, :3] = lame_first
    for axis_number in range(3):
        elastic[axis_number, axis_number] = lame_first + 2.0 * shear_mod
        elastic[axis_number + 3, axis_number + 3] = shear_mod
    points = [0.5 - 0.5 / np.sqrt(3.0), 0.5 + 0.5 / np.sqrt(3.0)]
    matrix = np.zeros((24, 24))
    for point_x in points:
        for point_y in points:
            for point_z in points:
                coords = (point_x, point_y, point_z)
                strain = np.zeros((6, 24))
                for number, corner in enumerate(CORNERS):
                    factors = [coords[d] if corner[d] else 1.0 - coords[d] for d in range(3)]
                    slopes = [1.0 if corner[d] else -1.0 for d in range(3)]
                    derivs = [
                        slopes[0] * factors[1] * factors[2],
                        factors[0] * slopes[1] * factors[2],
                        factors[0] * factors[1] * slopes[2],
                    ]
                    column = 3 * number
                    strain[0, column] = derivs[0]
                    strain[1, column + 1] = derivs[1]
                    strain[2, column + 2] = derivs[2]
                    strain[3, column] = derivs[1]
                    strain[3, column + 1] = derivs[0]
                    strain[4, column + 1] = derivs[2]
                    strain[4, column + 2] = derivs[1]
                    strain[5, column] = derivs[2]
                    strain[5, column + 2] = derivs[0]
                matrix += strain.T @ elastic @ strain / 8.0
    return matrix


def modal_stiffness():
    one = np.array([[1.0, 1.0], [-1.0, 1.0]])
    change = np.zeros((8, 8))
    for row, (a, b, c) in enumerate(CORNERS):
        for column, (p, q, r) in enumerate(CORNERS):
            change[row, column] = one[a, p] * one[b, q] * one[c, r]
    inverse = np.linalg.inv(np.kron(change, np.eye(3)))
    modal = inverse.T @ element_stiffness() @ inverse
    modes = [corner + (d,) for corner in CORNERS for d in range(3)]
    return {(modes[i], modes[j]): float(modal[i, j]) for i in range(24) for j in range(24)}


MODAL_VALUE = modal_stiffness()
CORNER_DIAG = float(element_stiffness()[0, 0])


def pack_x_kernel(load, disp, dens, mask, low, up, flags, done):
    copies = [(mask.at[RX - 3 : RX], flags.at[0:3]), (mask.at[0:4], flags.at[3:7])]
    for c in range(3):
        copies.append((load.at[c, RX - 3 : RX], low.at[3 * c : 3 * c + 3]))
        copies.append((load.at[c, 0:4], up.at[4 * c : 4 * c + 4]))
        copies.append((disp.at[c, RX - 1 : RX], low.at[17 + c : 18 + c]))
        copies.append((disp.at[c, 0:2], up.at[21 + 2 * c : 23 + 2 * c]))
    copies.append((dens.at[RX - 5 : RX], low.at[12:17]))
    copies.append((dens.at[0:5], up.at[16:21]))
    copies = [
        pltpu.make_async_copy(source, target, done.at[n])
        for n, (source, target) in enumerate(copies)
    ]
    for copy in copies:
        copy.start()
    for copy in copies:
        copy.wait()
    low[9:12] = (1 - flags[0:3]).astype(F32)
    up[12:16] = (1 - flags[3:7]).astype(F32)


def loads_kernel(nodes, forces, _, out):
    first_x = (lax.axis_index("x") * lax.axis_size("y") + lax.axis_index("y")) * RX - 3
    first_y = (lax.axis_index("z") * lax.axis_size("c") + lax.axis_index("c")) * RY
    count = (NI - 1) * RY
    chunk = CHUNK
    place = lax.broadcasted_iota(jnp.int32, (count, chunk), 0)
    depth = lax.broadcasted_iota(jnp.int32, (2 * NZ, chunk), 0)
    total = jnp.zeros((9 * count, 2 * NZ), F32)
    for start in range(0, nodes.shape[1], chunk):
        cols = slice(start, start + chunk)
        local_x = nodes[0:1, cols] - first_x
        local_y = nodes[1:2, cols] - first_y
        inside = (local_x >= 0) & (local_x < NI - 1) & (local_y >= -4) & (local_y < RY + 4)
        spot = jnp.where(inside, local_x * RY + (local_y & (RY - 1)), -1)
        hit = place == spot
        outer = jnp.where((local_y < 0) | (local_y >= RY), NZ, 0)
        layer = jnp.where(depth == nodes[2:3, cols] + outer, 1.0, 0.0).astype(jnp.bfloat16)
        parts = []
        for c in range(3):
            rest = forces[c : c + 1, cols]
            for _ in range(3):
                head = rest.astype(jnp.bfloat16).astype(F32)
                rest = rest - head
                parts.append(jnp.where(hit, head, 0.0).astype(jnp.bfloat16))
        total = total + lax.dot_general(
            jnp.concatenate(parts, axis=0),
            layer,
            (((1,), (1,)), ((), ())),
            preferred_element_type=F32,
        )
    for c in range(3):
        base = 3 * c * count
        summed = (
            total[base : base + count]
            + total[base + count : base + 2 * count]
            + total[base + 2 * count : base + 3 * count]
        )
        for t in range(2):
            out[c, :, t] = summed[:, t * NZ : t * NZ + NZ].reshape(NI - 1, RY, NZ)


def pack_y_kernel(which, load, disp, dens, mask, low, up, *rest):
    out = rest[-1]

    def write(rows, extra, count, at):
        free = lambda part: (1 - part).astype(F32)
        for c in range(3):
            out[12 * c : 12 * c + 12] = load[c, :, rows]
            q = NEAR + 7 * c
            out[q : q + 3] = low[3 * c : 3 * c + 3, rows]
            out[q + 3 : q + 7] = up[4 * c : 4 * c + 4, rows]
        out[36:48] = free(mask[:, rows])
        out[48:60] = dens[:, rows]
        q = NEAR + 21
        out[q : q + 3] = low[9:12, rows]
        out[q + 3 : q + 7] = up[12:16, rows]
        out[q + 7 : q + 12] = low[12:17, rows]
        out[q + 12 : q + 17] = up[16:21, rows]
        for p in range(12):
            out[60 + p // 4, p % 4 : p % 4 + 1] = dens[p, extra : extra + 1]
        for r in range(10):
            source = low[12 + r, extra : extra + 1] if r < 5 else up[11 + r, extra : extra + 1]
            out[NEAR + 38 + r // 4, r % 4 : r % 4 + 1] = source
        per = 4 // count
        for n in range(36):
            spot = count * (n % per)
            out[63 + n // per, spot : spot + count] = disp[n // 12, n % 12, at : at + count]
        for n in range(9):
            c, m = n // 3, n % 3
            source = low[17 + c] if m == 0 else up[20 + 2 * c + m]
            spot = count * (n % per)
            out[NEAR + 41 + n // per, spot : spot + count] = source[at : at + count]

    upper = lax.axis_index("c") == which

    @pl.when(upper)
    def _():
        write(slice(4, 8), 3, 1, 7)

    @pl.when(jnp.logical_not(upper))
    def _():
        write(slice(0, 4), 4, 2, 0)


def up_z(v, lane):
    return jnp.where(lane < NZ - 1, pltpu.roll(v, NZ - 1, 1), 0.0)


def down_z(v, lane):
    return jnp.where(lane > 0, pltpu.roll(v, 1, 1), 0.0)


def axes(*ones):
    return tuple(int(n in ones) for n in range(3))


K_SHEAR = MODAL_VALUE[axes(1) + (0,), axes(0) + (1,)]
K_NORMAL = MODAL_VALUE[axes(0) + (0,), axes(0) + (0,)]
K_CROSS = MODAL_VALUE[axes(0) + (0,), axes(1) + (1,)]
K_BEND = MODAL_VALUE[axes(0, 1) + (0,), axes(0, 1) + (0,)]
K_BEND_OFF = MODAL_VALUE[axes(0, 1) + (0,), axes(1, 2) + (2,)]
K_TWIST = MODAL_VALUE[axes(0, 1) + (2,), axes(0, 2) + (1,)]
K_LAST = MODAL_VALUE[axes(0, 1, 2) + (0,), axes(0, 1, 2) + (0,)]
PAIRS = [(0, 1), (0, 2), (1, 2)]
BENDS = [(0, 1, 2), (1, 0, 2), (0, 2, 1)]


def combine(h):
    out = {}
    for d, e in PAIRS:
        out["s", d, e] = h[axes(e) + (d,)] + h[axes(d) + (e,)]
    normal = [h[axes(d) + (d,)] for d in range(3)]
    total = normal[0] + normal[1] + normal[2]
    for d in range(3):
        out["n", d] = normal[d] * ((K_NORMAL - K_CROSS) / K_CROSS) + total
    for d, e, f in BENDS:
        one, two = h[axes(d, e) + (d,)], h[axes(e, f) + (f,)]
        out["b", d, e] = one * (K_BEND / K_BEND_OFF) + two
        out["b", f, e] = two * (K_BEND / K_BEND_OFF) + one
    twist = [h[axes(*[n for n in range(3) if n != d]) + (d,)] for d in range(3)]
    total = twist[0] + twist[1] + twist[2]
    for d in range(3):
        out["t", d] = twist[d] + total
        out["l", d] = h[axes(0, 1, 2) + (d,)]
    return out


SCALES = {"s": K_SHEAR, "n": K_CROSS, "b": K_BEND_OFF, "t": K_TWIST, "l": K_LAST}


def mode_of(key):
    kind = key[0]
    if kind == "s":
        return axes(key[2]) + (key[1],)
    if kind == "n":
        return axes(key[1]) + (key[1],)
    if kind == "b":
        return axes(key[1], key[2]) + (key[1],)
    if kind == "t":
        return axes(*[n for n in range(3) if n != key[1]]) + (key[1],)
    return axes(0, 1, 2) + (key[1],)


def modes_of(near, far):
    result = {}
    for key in near:
        c, b, s = key
        result[0, b, s, c] = near[key] + far[key]
        result[1, b, s, c] = far[key] - near[key]
    return result


KEYS = [("s", d, e) for d, e in PAIRS] + [("n", d) for d in range(3)]
KEYS += [("b", d, e) for d, e, f in BENDS] + [("b", f, e) for d, e, f in BENDS]
KEYS += [("t", d) for d in range(3)] + [("l", d) for d in range(3)]
NUMBER = {key: n for n, key in enumerate(KEYS)}
PARTS = [(c, s) for c in range(3) for s in (0, 1)]


def main_kernel(load, disp, dens, mask, low, up, placed, first, second, basis, senses, sums, L0, L1, FR1, D1, DN, MOD, SC, HP, W, Z, G, DS, SS, F, DV):
    gx = lax.axis_index("x") * lax.axis_size("y") + lax.axis_index("y")
    gy = lax.axis_index("z") * lax.axis_size("c") + lax.axis_index("c")
    extent_x = RX * lax.axis_size("x") * lax.axis_size("y")
    extent_y = RY * lax.axis_size("z") * lax.axis_size("c")
    lane = lax.broadcasted_iota(jnp.int32, (8, NZ), 1)
    row = lax.broadcasted_iota(jnp.int32, (8, NZ), 0)
    upper_half = row < 4

    DN[0:5, 16:24] = low[12:17]
    DN[5 : 5 + RX, 16:24] = dens[...]
    DN[5 + RX : 10 + RX, 16:24] = up[16:21]
    D1[...] = jnp.zeros(D1.shape, F32)

    def fill(below, above):
        below_corner, above_corner = below.at[NEAR : NEAR + CORNER], above.at[NEAR : NEAR + CORNER]
        for rows, near, corner in (
            (slice(0, 4), above, above_corner),
            (slice(4, 8), below, below_corner),
        ):
            for c in range(3):
                L1[c, 0:3, rows] = corner[7 * c : 7 * c + 3]
                L1[c, 3:15, rows] = near[12 * c : 12 * c + 12]
                L1[c, 15:19, rows] = corner[7 * c + 3 : 7 * c + 7]
            FR1[0:3, rows] = corner[21:24]
            FR1[3:15, rows] = near[36:48]
            FR1[15:19, rows] = corner[24:28]
        for rows, extra, near, corner in (
            (slice(24, 28), 28, above, above_corner),
            (slice(12, 16), 11, below, below_corner),
        ):
            DN[0:5, rows] = corner[28:33]
            DN[5:17, rows] = near[48:60]
            DN[17:22, rows] = corner[33:38]
            for p in range(22):
                if 5 <= p < 17:
                    one = near[60 + (p - 5) // 4, (p - 5) % 4 : (p - 5) % 4 + 1]
                else:
                    r = p if p < 5 else p - 12
                    one = corner[38 + r // 4, r % 4 : r % 4 + 1]
                DN[p, extra : extra + 1] = one
        for c in range(3):
            for p in range(12):
                n = 12 * c + p
                D1[c, p + 1, 7:8] = below[63 + n // 4, n % 4 : n % 4 + 1]
                D1[c, p + 1, 0:2] = above[63 + n // 2, 2 * (n % 2) : 2 * (n % 2) + 2]
            for m, p in enumerate((0, 13, 14)):
                n = 3 * c + m
                D1[c, p, 7:8] = below_corner[41 + n // 4, n % 4 : n % 4 + 1]
                D1[c, p, 0:2] = above_corner[41 + n // 2, 2 * (n % 2) : 2 * (n % 2) + 2]

    even = lax.axis_index("c") == 0

    @pl.when(even)
    def _():
        fill(second, first)

    @pl.when(jnp.logical_not(even))
    def _():
        fill(first, second)

    def load_of(c, i, t):
        if t == 1:
            value = L1[c, i - 1]
        elif i < 4:
            value = low[3 * c + i - 1]
        elif i < 4 + RX:
            value = load[c, i - 4]
        else:
            value = up[4 * c + i - 4 - RX]
        return value + placed[c, i - 1, t]

    def is_free(i, t):
        if t == 1:
            return FR1[i - 1] > 0.5
        if i < 4:
            return low[9 + i - 1] > 0.5
        if i < 4 + RX:
            return mask[i - 4] == 0
        return up[12 + i - 4 - RX] > 0.5

    def disp_of(c, p, t):
        if t == 1:
            return D1[c, p]
        if p == 0:
            return low[17 + c]
        return disp[c, p - 1] if p <= RX else up[21 + 2 * c + p - 1 - RX]

    near_z = 2.0 - jnp.where(lane == 0, 1.0, 0.0) - jnp.where(lane == NZ - 1, 1.0, 0.0)
    inside_y, part_a, part_b = [], [], []
    for t in range(2):
        place_y = gy * RY + (row if t == 0 else jnp.where(upper_half, row + 8, row - 8))
        inside_y.append(jnp.where((place_y >= 0) & (place_y < extent_y), 1.0, 0.0))
        near_y = 2.0 - jnp.where(place_y == 0, 1.0, 0.0) - jnp.where(place_y == extent_y - 1, 1.0, 0.0)
        part_a.append(1.5 + 0.5 * (near_y + near_z) + EDGE * near_y * near_z)
        part_b.append(0.5 + EDGE * (near_y + near_z))

    def filtered(cells, beside, p):
        side = cells[p - 1] + cells[p + 1]
        far = beside[p - 1] + beside[p + 1]
        deep = 0.5 * cells[p] + EDGE * (beside[p] + side)
        deep = up_z(deep, lane) + down_z(deep, lane)
        return 1.5 * cells[p] + 0.5 * (beside[p] + side) + EDGE * far + deep

    def density_rows(p, t, shift):
        if t == 0:
            return DN[p, 16 + shift : 24 + shift]
        return jnp.where(
            upper_half, DN[p, 24 + shift : 32 + shift], DN[p, 8 + shift : 16 + shift]
        )

    for t in range(2):
        cells, beside = [], []
        for p in range(NI + 2):
            cells.append(density_rows(p, t, 0))
            beside.append(density_rows(p, t, -1) + density_rows(p, t, 1))
            i = p - 2
            if i < 0:
                continue
            place_x = gx * RX - 4 + i
            inside_x = jnp.where((place_x >= 0) & (place_x < extent_x), 1.0, 0.0)
            near_x = 2.0 - jnp.where(place_x == 0, 1.0, 0.0) - jnp.where(place_x == extent_x - 1, 1.0, 0.0)
            inverse = 1.0 / (part_a[t] + near_x * part_b[t])
            physical = filtered(cells, beside, p - 1) * inverse
            squared = physical * physical
            inside = inside_y[t] * inside_x
            mod = inside * (SOFT + (1.0 - SOFT) * (squared * physical))
            MOD[i, t] = mod
            if 3 <= i <= NI - 4:
                SC[i - 3, t] = (inside * (PENALTY * (1.0 - SOFT))) * (squared * inverse)
            deep = mod + down_z(mod, lane)
            HP[i, 8 + 8 * t : 16 + 8 * t] = deep
            if t == 1:
                HP[i, 0:8] = deep

    zero = jnp.zeros((8, NZ), F32)

    def store_parts(c, i, t, v):
        above = up_z(v, lane)
        for s, part in ((0, v + above), (1, above - v)):
            G[2 * c + s, i, 8 * t : 8 * t + 8] = part
            if t == 0:
                G[2 * c + s, i, 16:24] = part

    def in_block(i, t):
        return t == 0 and 4 <= i < 4 + RX

    bz = zero
    for t in range(2):
        before = None
        for i in range(NI):
            summed = HP[i, 8 + 8 * t : 16 + 8 * t] + HP[i, 7 + 8 * t : 15 + 8 * t]
            if i > 0:
                inverse = jnp.where(is_free(i, t), (1.0 / CORNER_DIAG) / (summed + before), 0.0)
                W[i, t] = inverse
                for c in range(3):
                    here = load_of(c, i, t)
                    z = inverse * here
                    Z[0, c, i, t] = z
                    store_parts(c, i, t, z)
                    if in_block(i, t):
                        L0[c, i - 4] = here
                        bz = bz + z * here
            before = summed

    def yz_modes(i, t):
        result = {}
        for c, s in PARTS:
            part = G[2 * c + s, i, 8 * t : 8 * t + 8]
            higher = G[2 * c + s, i, 8 * t + 1 : 8 * t + 9]
            result[c, 0, s] = part + higher
            result[c, 1, s] = higher - part
        return result

    def apply(k):
        for t in range(2):
            near = yz_modes(1 + k, t)
            passed = None
            for i in range(1 + k, NI - 1 - k):
                far = yz_modes(i + 1, t)
                modes = modes_of(near, far)
                mixed = combine(modes)
                if 3 <= i <= NI - 4:
                    energy = None
                    for key, n in NUMBER.items():
                        factor = mixed[key] if key[0] == "s" else modes[mode_of(key)]
                        term = factor * F[n, i - 3, t]
                        energy = term if energy is None else energy + term
                    value = energy * SC[i - 3, t]
                    DV[k, i - 3, 8 + 8 * t : 16 + 8 * t] = value
                    if t == 1:
                        DV[k, i - 3, 0:8] = value
                young = MOD[i, t]
                scaled = {kind: young * factor for kind, factor in SCALES.items()}
                forces = {}
                for key, value in mixed.items():
                    force = scaled[key[0]] * value
                    forces[mode_of(key)] = force
                    if key[0] == "s":
                        forces[axes(key[1]) + (key[2],)] = force
                following = {}
                for c, s in PARTS:
                    node = {}
                    for b in (0, 1):
                        slope = forces[1, b, s, c]
                        if (0, b, s, c) in forces:
                            level = forces[0, b, s, c]
                            low, following[c, b, s] = level - slope, level + slope
                            node[b] = low if passed is None else passed[c, b, s] + low
                        else:
                            following[c, b, s] = slope
                            node[b] = -slope if passed is None else passed[c, b, s] - slope
                    if i > 1 + k:
                        DS[2 * c + s, i, t] = node[0] - node[1]
                        both = node[0] + node[1]
                        SS[2 * c + s, i, 8 + 8 * t : 16 + 8 * t] = both
                        if t == 1:
                            SS[2 * c + s, i, 0:8] = both
                passed, near = following, far

    def image(c, i, t):
        level, slope = [
            DS[2 * c + s, i, t] + SS[2 * c + s, i, 7 + 8 * t : 15 + 8 * t] for s in (0, 1)
        ]
        return level - slope + down_z(level + slope, lane)

    for p in range(RX + 3):
        for t in range(2):
            for c in range(3):
                v = disp_of(c, p, t)
                above = up_z(v, lane)
                for s, part in ((0, v + above), (1, above - v)):
                    SS[2 * c + s, p, 8 * t : 8 * t + 8] = part
                    if t == 0:
                        SS[2 * c + s, p, 16:24] = part
    for t in range(2):
        near = None
        for p in range(RX + 3):
            far = {}
            for c, s in PARTS:
                part = SS[2 * c + s, p, 8 * t : 8 * t + 8]
                higher = SS[2 * c + s, p, 8 * t + 1 : 8 * t + 9]
                far[c, 0, s] = part + higher
                far[c, 1, s] = higher - part
            if near is not None:
                for key, value in combine(modes_of(near, far)).items():
                    F[NUMBER[key], p - 1, t] = value * SCALES[key[0]]
            near = far

    def add(total, i, t, one, two):
        return total + one * two if in_block(i, t) else total

    h00 = b1 = h01 = h11 = b2 = h12 = h22 = h02 = zero
    apply(0)
    for t in range(2):
        for i in range(2, NI - 1):
            for c in range(3):
                q = image(c, i, t)
                z = Z[0, c, i, t]
                y = W[i, t] * q - z
                Z[1, c, i, t] = y
                store_parts(c, i, t, y)
                h00 = add(h00, i, t, z, q)
                h01 = add(h01, i, t, y, q)
                if in_block(i, t):
                    b1 = b1 + y * L0[c, i - 4]
    apply(1)
    for t in range(2):
        for i in range(3, NI - 2):
            for c in range(3):
                q = image(c, i, t)
                z = Z[1, c, i, t]
                y = W[i, t] * q - z
                Z[2, c, i, t] = y
                store_parts(c, i, t, y)
                h11 = add(h11, i, t, z, q)
                h12 = add(h12, i, t, y, q)
                if in_block(i, t):
                    b2 = b2 + y * L0[c, i - 4]
    apply(2)
    for i in range(4, 4 + RX):
        for c in range(3):
            q = image(c, i, 0)
            h22 = add(h22, i, 0, Z[2, c, i, 0], q)
            h02 = add(h02, i, 0, Z[0, c, i, 0], q)

    lanes = lax.broadcasted_iota(jnp.int32, (1, NZ), 1)
    line = jnp.zeros((1, NZ), F32)
    for n, value in enumerate((bz, b1, b2, h00, h01, h02, h11, h12, h22)):
        whole = jnp.sum(value, axis=0, keepdims=True)
        whole = jnp.sum(whole, axis=1, keepdims=True)
        line = line + jnp.where(lanes == n, whole, 0.0)
    for n in range(sums.shape[0]):
        sums[n] = line

    for k in range(3):
        cells, beside = [], []
        for p in range(RX + 2):
            cells.append(DV[k, p, 8:16])
            beside.append(DV[k, p, 7:15] + DV[k, p, 9:17])
            if p >= 2:
                senses[k, p - 2] = filtered(cells, beside, p - 1)
        for c in range(3):
            basis[k, c] = Z[k, c, 4 : 4 + RX, 0]


def final_kernel(gathered, basis, senses, adjoint, sensitivity):
    total = jnp.sum(gathered[...], axis=0)

    def value(n):
        return jnp.broadcast_to(total[:, n : n + 1], (1, NZ))

    b0, b1, b2, h00, h01, h02, h11, h12, h22 = [value(n) for n in range(9)]
    l1, l2 = h01 / h00, h02 / h00
    d1 = h11 - l1 * h01
    e = h12 - l1 * h02
    fine1 = d1 > 0.0
    l3 = jnp.where(fine1, e / d1, 0.0)
    d2 = h22 - l2 * h02 - l3 * e
    t1 = b1 - l1 * b0
    t2 = b2 - l2 * b0 - l3 * t1
    c2 = jnp.where(d2 > 0.0, t2 / d2, 0.0)
    c1 = jnp.where(fine1, t1 / d1, 0.0) - l3 * c2
    c0 = b0 / h00 - l1 * c1 - l2 * c2
    adjoint[...] = c0 * basis[0] + c1 * basis[1] + c2 * basis[2]
    sensitivity[...] = c0 * senses[0] + c1 * senses[1] + c2 * senses[2]


VMEM = pl.BlockSpec(memory_space=pltpu.VMEM)


def call(kernel, inputs, outs, scratch=(), limit=None, extra=0):
    single = not isinstance(outs, list)
    shapes = [outs] if single else outs
    result = pl.pallas_call(
        kernel,
        out_shape=[jax.ShapeDtypeStruct(s, F32) for s in shapes],
        in_specs=[VMEM] * (len(inputs) - extra) + [pl.BlockSpec(memory_space=pl.ANY)] * extra,
        out_specs=[VMEM] * len(shapes),
        scratch_shapes=[pltpu.VMEM(s, F32) for s in scratch],
        compiler_params=pltpu.CompilerParams(vmem_limit_bytes=limit or 32 * 1024 * 1024),
    )(*inputs)
    return result[0] if single else result


MAIN_SCRATCH = [
    (3, RX, 8, NZ),
    (3, NI - 1, 8, NZ),
    (NI - 1, 8, NZ),
    (3, RX + 3, 8, NZ),
    (NI + 2, 40, NZ),
    (NI, 2, 8, NZ),
    (RX + 2, 2, 8, NZ),
    (NI, 24, NZ),
    (NI, 2, 8, NZ),
    (3, 3, NI, 2, 8, NZ),
    (6, NI, 24, NZ),
    (6, NI, 2, 8, NZ),
    (6, NI, 24, NZ),
    (len(KEYS), RX + 2, 2, 8, NZ),
    (3, RX + 2, 24, NZ),
]


def shards(displacement, adjoint_load, density, fixed_mask, load_nodes, load_forces):
    gx = ("x", "y")
    count_x = lax.axis_size("x") * lax.axis_size("y")
    count_y = lax.axis_size("z") * lax.axis_size("c")
    own = (adjoint_load, displacement, density, fixed_mask)
    low, up = pl.pallas_call(
        pack_x_kernel,
        out_shape=[
            pltpu.VMEM((LOW_X, RY, NZ), F32),
            pltpu.VMEM((UP_X, RY, NZ), F32),
        ],
        in_specs=[pl.BlockSpec(memory_space=pltpu.HBM)] * 4,
        out_specs=[VMEM] * 2,
        scratch_shapes=[
            pltpu.VMEM((7, RY, NZ), jnp.int32),
            pltpu.SemaphoreType.DMA((16,)),
        ],
    )(*own)
    low = lax.ppermute(low, gx, [(i, i + 1) for i in range(count_x - 1)])
    up = lax.ppermute(up, gx, [(i + 1, i) for i in range(count_x - 1)])
    sizes = (NEAR + CORNER, 4, NZ)
    second = call(functools.partial(pack_y_kernel, 1), own + (low, up), (NEAR + CORNER + 1, 4, NZ))
    pairs = [(i, i + 1) for i in range(1, count_y - 1, 2)]
    pairs = pairs + [(j, i) for i, j in pairs]
    placed = call(
        loads_kernel, (load_nodes, load_forces, low), (3, NI - 1, 2, RY, NZ), extra=1
    )
    first = call(functools.partial(pack_y_kernel, 0), own + (low, up, placed), sizes, extra=1)
    second = lax.ppermute(second, ("z", "c"), pairs)
    first = lax.ppermute(first, "c", [(0, 1), (1, 0)])
    close = lax.axis_size("c") * count_x
    far = lax.axis_size("z")
    basis, senses, sums = call(
        main_kernel,
        own + (low, up, placed, first, second),
        [(3, 3, RX, RY, NZ), (3, RX, RY, NZ), (close, 1, NZ)],
        MAIN_SCRATCH,
        48 * 1024 * 1024,
    )
    sums = lax.all_to_all(sums, ("x", "y", "c"), 0, 0, tiled=True)
    sums = jnp.broadcast_to(jnp.sum(sums, axis=0, keepdims=True), (far, 1, NZ))
    sums = lax.all_to_all(sums, "z", 0, 0, tiled=True)
    adjoint, sensitivity = call(
        final_kernel, (sums, basis, senses), [(3, RX, RY, NZ), (RX, RY, NZ)]
    )
    return adjoint, sensitivity


def solution(mesh):
    size_x, size_y = mesh.shape["gx"], mesh.shape["gy"]
    side = int(round(size_x**0.5))
    whole = Mesh(
        mesh.devices.reshape(side, size_x // side, size_y // 2, 2), ("x", "y", "z", "c")
    )
    field = P(None, ("x", "y"), ("z", "c"), None)
    grid = P(("x", "y"), ("z", "c"), None)
    return jax.shard_map(
        shards,
        mesh=whole,
        in_specs=(field, field, grid, grid, P(), P()),
        out_specs=(field, grid),
        check_vma=False,
    )
```

```python
import functools

import jax
import jax.numpy as jnp
import numpy as np
from jax import lax
from jax.experimental import pallas as pl
from jax.experimental.pallas import tpu as pltpu
from jax.sharding import Mesh, PartitionSpec as P

POISSON = 0.3
PENALTY = 3.0
SOFT = 0.001
CORNERS = [(a, b, c) for c in (0, 1) for b in (0, 1) for a in (0, 1)]
EDGE = float(1.5 - np.sqrt(2.0))

RX, RY, NZ = 12, 8, 128
NI = RX + 8
LOW_X, UP_X = 20, 27
NEAR, CORNER = 81, 46
CHUNK = 256
F32 = jnp.float32


def element_stiffness():
    lame_first = POISSON / ((1.0 + POISSON) * (1.0 - 2.0 * POISSON))
    shear_mod = 1.0 / (2.0 * (1.0 + POISSON))
    elastic = np.zeros((6, 6))
    elastic[:3, :3] = lame_first
    for axis_number in range(3):
        elastic[axis_number, axis_number] = lame_first + 2.0 * shear_mod
        elastic[axis_number + 3, axis_number + 3] = shear_mod
    points = [0.5 - 0.5 / np.sqrt(3.0), 0.5 + 0.5 / np.sqrt(3.0)]
    matrix = np.zeros((24, 24))
    for point_x in points:
        for point_y in points:
            for point_z in points:
                coords = (point_x, point_y, point_z)
                strain = np.zeros((6, 24))
                for number, corner in enumerate(CORNERS):
                    factors = [coords[d] if corner[d] else 1.0 - coords[d] for d in range(3)]
                    slopes = [1.0 if corner[d] else -1.0 for d in range(3)]
                    derivs = [
                        slopes[0] * factors[1] * factors[2],
                        factors[0] * slopes[1] * factors[2],
                        factors[0] * factors[1] * slopes[2],
                    ]
                    column = 3 * number
                    strain[0, column] = derivs[0]
                    strain[1, column + 1] = derivs[1]
                    strain[2, column + 2] = derivs[2]
                    strain[3, column] = derivs[1]
                    strain[3, column + 1] = derivs[0]
                    strain[4, column + 1] = derivs[2]
                    strain[4, column + 2] = derivs[1]
                    strain[5, column] = derivs[2]
                    strain[5, column + 2] = derivs[0]
                matrix += strain.T @ elastic @ strain / 8.0
    return matrix


def modal_stiffness():
    one = np.array([[1.0, 1.0], [-1.0, 1.0]])
    change = np.zeros((8, 8))
    for row, (a, b, c) in enumerate(CORNERS):
        for column, (p, q, r) in enumerate(CORNERS):
            change[row, column] = one[a, p] * one[b, q] * one[c, r]
    inverse = np.linalg.inv(np.kron(change, np.eye(3)))
    modal = inverse.T @ element_stiffness() @ inverse
    modes = [corner + (d,) for corner in CORNERS for d in range(3)]
    return {(modes[i], modes[j]): float(modal[i, j]) for i in range(24) for j in range(24)}


MODAL_VALUE = modal_stiffness()
CORNER_DIAG = float(element_stiffness()[0, 0])


def pack_x_kernel(load, disp, dens, mask, first, second, low, up, flags, done):
    copies = [(mask.at[RX - 3 : RX], flags.at[0:3]), (mask.at[0:4], flags.at[3:7])]
    for c in range(3):
        copies.append((load.at[c, RX - 3 : RX], low.at[3 * c : 3 * c + 3]))
        copies.append((load.at[c, 0:4], up.at[4 * c : 4 * c + 4]))
        copies.append((disp.at[c, RX - 1 : RX], low.at[17 + c : 18 + c]))
        copies.append((disp.at[c, 0:2], up.at[21 + 2 * c : 23 + 2 * c]))
    copies.append((dens.at[RX - 5 : RX], low.at[12:17]))
    copies.append((dens.at[0:5], up.at[16:21]))
    copies = [
        pltpu.make_async_copy(source, target, done.at[n])
        for n, (source, target) in enumerate(copies)
    ]
    for copy in copies:
        copy.start()
    for copy in copies:
        copy.wait()
    low[9:12] = (1 - flags[0:3]).astype(F32)
    up[12:16] = (1 - flags[3:7]).astype(F32)
    even = lax.rem(lax.axis_index("y"), 2) == 0

    @pl.when(even)
    def _():
        first[0:LOW_X] = low[...]
        second[0:UP_X] = up[...]

    @pl.when(jnp.logical_not(even))
    def _():
        first[0:UP_X] = up[...]
        second[0:LOW_X] = low[...]


def loads_kernel(nodes, forces, _, out):
    first_x = (lax.axis_index("x") * lax.axis_size("y") + lax.axis_index("y")) * RX - 3
    first_y = (lax.axis_index("z") * lax.axis_size("c") + lax.axis_index("c")) * RY
    count = (NI - 1) * RY
    chunk = CHUNK
    place = lax.broadcasted_iota(jnp.int32, (count, chunk), 0)
    depth = lax.broadcasted_iota(jnp.int32, (2 * NZ, chunk), 0)
    total = jnp.zeros((9 * count, 2 * NZ), F32)
    for start in range(0, nodes.shape[1], chunk):
        cols = slice(start, start + chunk)
        local_x = nodes[0:1, cols] - first_x
        local_y = nodes[1:2, cols] - first_y
        inside = (local_x >= 0) & (local_x < NI - 1) & (local_y >= -4) & (local_y < RY + 4)
        spot = jnp.where(inside, local_x * RY + (local_y & (RY - 1)), -1)
        hit = place == spot
        outer = jnp.where((local_y < 0) | (local_y >= RY), NZ, 0)
        layer = jnp.where(depth == nodes[2:3, cols] + outer, 1.0, 0.0).astype(jnp.bfloat16)
        parts = []
        for c in range(3):
            rest = forces[c : c + 1, cols]
            for _ in range(3):
                head = rest.astype(jnp.bfloat16).astype(F32)
                rest = rest - head
                parts.append(jnp.where(hit, head, 0.0).astype(jnp.bfloat16))
        total = total + lax.dot_general(
            jnp.concatenate(parts, axis=0),
            layer,
            (((1,), (1,)), ((), ())),
            preferred_element_type=F32,
        )
    for c in range(3):
        base = 3 * c * count
        summed = (
            total[base : base + count]
            + total[base + count : base + 2 * count]
            + total[base + 2 * count : base + 3 * count]
        )
        for t in range(2):
            out[c, :, t] = summed[:, t * NZ : t * NZ + NZ].reshape(NI - 1, RY, NZ)


def pack_second_kernel(load, disp, dens, mask, first, second, out, low, up):
    even = lax.rem(lax.axis_index("y"), 2) == 0

    @pl.when(even)
    def _():
        up[...] = first[0:UP_X]
        low[...] = second[0:LOW_X]

    @pl.when(jnp.logical_not(even))
    def _():
        up[...] = second[0:UP_X]
        low[...] = first[0:LOW_X]

    pack_y_kernel(1, load, disp, dens, mask, low, up, out)


def pack_y_kernel(which, load, disp, dens, mask, low, up, *rest):
    out = rest[-1]

    def write(rows, extra, count, at):
        free = lambda part: (1 - part).astype(F32)
        for c in range(3):
            out[12 * c : 12 * c + 12] = load[c, :, rows]
            q = NEAR + 7 * c
            out[q : q + 3] = low[3 * c : 3 * c + 3, rows]
            out[q + 3 : q + 7] = up[4 * c : 4 * c + 4, rows]
        out[36:48] = free(mask[:, rows])
        out[48:60] = dens[:, rows]
        q = NEAR + 21
        out[q : q + 3] = low[9:12, rows]
        out[q + 3 : q + 7] = up[12:16, rows]
        out[q + 7 : q + 12] = low[12:17, rows]
        out[q + 12 : q + 17] = up[16:21, rows]
        for p in range(12):
            out[60 + p // 4, p % 4 : p % 4 + 1] = dens[p, extra : extra + 1]
        for r in range(10):
            source = low[12 + r, extra : extra + 1] if r < 5 else up[11 + r, extra : extra + 1]
            out[NEAR + 38 + r // 4, r % 4 : r % 4 + 1] = source
        per = 4 // count
        for n in range(36):
            spot = count * (n % per)
            out[63 + n // per, spot : spot + count] = disp[n // 12, n % 12, at : at + count]
        for n in range(9):
            c, m = n // 3, n % 3
            source = low[17 + c] if m == 0 else up[20 + 2 * c + m]
            spot = count * (n % per)
            out[NEAR + 41 + n // per, spot : spot + count] = source[at : at + count]

    upper = lax.axis_index("c") == which

    @pl.when(upper)
    def _():
        write(slice(4, 8), 3, 1, 7)

    @pl.when(jnp.logical_not(upper))
    def _():
        write(slice(0, 4), 4, 2, 0)


def up_z(v, lane):
    return jnp.where(lane < NZ - 1, pltpu.roll(v, NZ - 1, 1), 0.0)


def down_z(v, lane):
    return jnp.where(lane > 0, pltpu.roll(v, 1, 1), 0.0)


def axes(*ones):
    return tuple(int(n in ones) for n in range(3))


K_SHEAR = MODAL_VALUE[axes(1) + (0,), axes(0) + (1,)]
K_NORMAL = MODAL_VALUE[axes(0) + (0,), axes(0) + (0,)]
K_CROSS = MODAL_VALUE[axes(0) + (0,), axes(1) + (1,)]
K_BEND = MODAL_VALUE[axes(0, 1) + (0,), axes(0, 1) + (0,)]
K_BEND_OFF = MODAL_VALUE[axes(0, 1) + (0,), axes(1, 2) + (2,)]
K_TWIST = MODAL_VALUE[axes(0, 1) + (2,), axes(0, 2) + (1,)]
K_LAST = MODAL_VALUE[axes(0, 1, 2) + (0,), axes(0, 1, 2) + (0,)]
PAIRS = [(0, 1), (0, 2), (1, 2)]
BENDS = [(0, 1, 2), (1, 0, 2), (0, 2, 1)]


def combine(h):
    out = {}
    for d, e in PAIRS:
        out["s", d, e] = h[axes(e) + (d,)] + h[axes(d) + (e,)]
    normal = [h[axes(d) + (d,)] for d in range(3)]
    total = normal[0] + normal[1] + normal[2]
    for d in range(3):
        out["n", d] = normal[d] * ((K_NORMAL - K_CROSS) / K_CROSS) + total
    for d, e, f in BENDS:
        one, two = h[axes(d, e) + (d,)], h[axes(e, f) + (f,)]
        out["b", d, e] = one * (K_BEND / K_BEND_OFF) + two
        out["b", f, e] = two * (K_BEND / K_BEND_OFF) + one
    twist = [h[axes(*[n for n in range(3) if n != d]) + (d,)] for d in range(3)]
    total = twist[0] + twist[1] + twist[2]
    for d in range(3):
        out["t", d] = twist[d] + total
        out["l", d] = h[axes(0, 1, 2) + (d,)]
    return out


SCALES = {"s": K_SHEAR, "n": K_CROSS, "b": K_BEND_OFF, "t": K_TWIST, "l": K_LAST}


def mode_of(key):
    kind = key[0]
    if kind == "s":
        return axes(key[2]) + (key[1],)
    if kind == "n":
        return axes(key[1]) + (key[1],)
    if kind == "b":
        return axes(key[1], key[2]) + (key[1],)
    if kind == "t":
        return axes(*[n for n in range(3) if n != key[1]]) + (key[1],)
    return axes(0, 1, 2) + (key[1],)


def modes_of(near, far):
    result = {}
    for key in near:
        c, b, s = key
        result[0, b, s, c] = near[key] + far[key]
        result[1, b, s, c] = far[key] - near[key]
    return result


KEYS = [("s", d, e) for d, e in PAIRS] + [("n", d) for d in range(3)]
KEYS += [("b", d, e) for d, e, f in BENDS] + [("b", f, e) for d, e, f in BENDS]
KEYS += [("t", d) for d in range(3)] + [("l", d) for d in range(3)]
NUMBER = {key: n for n, key in enumerate(KEYS)}
PARTS = [(c, s) for c in range(3) for s in (0, 1)]


def main_kernel(load, disp, dens, mask, low, up, placed, first, second, basis, senses, sums, L0, L1, FR1, D1, DN, MOD, SC, HP, W, Z, G, DS, SS, F, DV):
    gx = lax.axis_index("x") * lax.axis_size("y") + lax.axis_index("y")
    gy = lax.axis_index("z") * lax.axis_size("c") + lax.axis_index("c")
    extent_x = RX * lax.axis_size("x") * lax.axis_size("y")
    extent_y = RY * lax.axis_size("z") * lax.axis_size("c")
    lane = lax.broadcasted_iota(jnp.int32, (8, NZ), 1)
    row = lax.broadcasted_iota(jnp.int32, (8, NZ), 0)
    upper_half = row < 4

    DN[0:5, 16:24] = low[12:17]
    DN[5 : 5 + RX, 16:24] = dens[...]
    DN[5 + RX : 10 + RX, 16:24] = up[16:21]
    D1[...] = jnp.zeros(D1.shape, F32)

    def fill(below, above):
        below_corner, above_corner = below.at[NEAR : NEAR + CORNER], above.at[NEAR : NEAR + CORNER]
        for rows, near, corner in (
            (slice(0, 4), above, above_corner),
            (slice(4, 8), below, below_corner),
        ):
            for c in range(3):
                L1[c, 0:3, rows] = corner[7 * c : 7 * c + 3]
                L1[c, 3:15, rows] = near[12 * c : 12 * c + 12]
                L1[c, 15:19, rows] = corner[7 * c + 3 : 7 * c + 7]
            FR1[0:3, rows] = corner[21:24]
            FR1[3:15, rows] = near[36:48]
            FR1[15:19, rows] = corner[24:28]
        for rows, extra, near, corner in (
            (slice(24, 28), 28, above, above_corner),
            (slice(12, 16), 11, below, below_corner),
        ):
            DN[0:5, rows] = corner[28:33]
            DN[5:17, rows] = near[48:60]
            DN[17:22, rows] = corner[33:38]
            for p in range(22):
                if 5 <= p < 17:
                    one = near[60 + (p - 5) // 4, (p - 5) % 4 : (p - 5) % 4 + 1]
                else:
                    r = p if p < 5 else p - 12
                    one = corner[38 + r // 4, r % 4 : r % 4 + 1]
                DN[p, extra : extra + 1] = one
        for c in range(3):
            for p in range(12):
                n = 12 * c + p
                D1[c, p + 1, 7:8] = below[63 + n // 4, n % 4 : n % 4 + 1]
                D1[c, p + 1, 0:2] = above[63 + n // 2, 2 * (n % 2) : 2 * (n % 2) + 2]
            for m, p in enumerate((0, 13, 14)):
                n = 3 * c + m
                D1[c, p, 7:8] = below_corner[41 + n // 4, n % 4 : n % 4 + 1]
                D1[c, p, 0:2] = above_corner[41 + n // 2, 2 * (n % 2) : 2 * (n % 2) + 2]

    even = lax.axis_index("c") == 0

    @pl.when(even)
    def _():
        fill(second, first)

    @pl.when(jnp.logical_not(even))
    def _():
        fill(first, second)

    def load_of(c, i, t):
        if t == 1:
            value = L1[c, i - 1]
        elif i < 4:
            value = low[3 * c + i - 1]
        elif i < 4 + RX:
            value = load[c, i - 4]
        else:
            value = up[4 * c + i - 4 - RX]
        return value + placed[c, i - 1, t]

    def is_free(i, t):
        if t == 1:
            return FR1[i - 1] > 0.5
        if i < 4:
            return low[9 + i - 1] > 0.5
        if i < 4 + RX:
            return mask[i - 4] == 0
        return up[12 + i - 4 - RX] > 0.5

    def disp_of(c, p, t):
        if t == 1:
            return D1[c, p]
        if p == 0:
            return low[17 + c]
        return disp[c, p - 1] if p <= RX else up[21 + 2 * c + p - 1 - RX]

    near_z = 2.0 - jnp.where(lane == 0, 1.0, 0.0) - jnp.where(lane == NZ - 1, 1.0, 0.0)
    inside_y, part_a, part_b = [], [], []
    for t in range(2):
        place_y = gy * RY + (row if t == 0 else jnp.where(upper_half, row + 8, row - 8))
        inside_y.append(jnp.where((place_y >= 0) & (place_y < extent_y), 1.0, 0.0))
        near_y = 2.0 - jnp.where(place_y == 0, 1.0, 0.0) - jnp.where(place_y == extent_y - 1, 1.0, 0.0)
        part_a.append(1.5 + 0.5 * (near_y + near_z) + EDGE * near_y * near_z)
        part_b.append(0.5 + EDGE * (near_y + near_z))

    def filtered(cells, beside, p):
        side = cells[p - 1] + cells[p + 1]
        far = beside[p - 1] + beside[p + 1]
        deep = 0.5 * cells[p] + EDGE * (beside[p] + side)
        deep = up_z(deep, lane) + down_z(deep, lane)
        return 1.5 * cells[p] + 0.5 * (beside[p] + side) + EDGE * far + deep

    def density_rows(p, t, shift):
        if t == 0:
            return DN[p, 16 + shift : 24 + shift]
        return jnp.where(
            upper_half, DN[p, 24 + shift : 32 + shift], DN[p, 8 + shift : 16 + shift]
        )

    for t in range(2):
        cells, beside = [], []
        for p in range(NI + 2):
            cells.append(density_rows(p, t, 0))
            beside.append(density_rows(p, t, -1) + density_rows(p, t, 1))
            i = p - 2
            if i < 0:
                continue
            place_x = gx * RX - 4 + i
            inside_x = jnp.where((place_x >= 0) & (place_x < extent_x), 1.0, 0.0)
            near_x = 2.0 - jnp.where(place_x == 0, 1.0, 0.0) - jnp.where(place_x == extent_x - 1, 1.0, 0.0)
            inverse = 1.0 / (part_a[t] + near_x * part_b[t])
            physical = filtered(cells, beside, p - 1) * inverse
            squared = physical * physical
            inside = inside_y[t] * inside_x
            mod = inside * (SOFT + (1.0 - SOFT) * (squared * physical))
            MOD[i, t] = mod
            if 3 <= i <= NI - 4:
                SC[i - 3, t] = (inside * (PENALTY * (1.0 - SOFT))) * (squared * inverse)
            deep = mod + down_z(mod, lane)
            HP[i, 8 + 8 * t : 16 + 8 * t] = deep
            if t == 1:
                HP[i, 0:8] = deep

    zero = jnp.zeros((8, NZ), F32)

    def store_parts(c, i, t, v):
        above = up_z(v, lane)
        for s, part in ((0, v + above), (1, above - v)):
            G[2 * c + s, i, 8 * t : 8 * t + 8] = part
            if t == 0:
                G[2 * c + s, i, 16:24] = part

    def in_block(i, t):
        return t == 0 and 4 <= i < 4 + RX

    bz = zero
    for t in range(2):
        before = None
        for i in range(NI):
            summed = HP[i, 8 + 8 * t : 16 + 8 * t] + HP[i, 7 + 8 * t : 15 + 8 * t]
            if i > 0:
                inverse = jnp.where(is_free(i, t), (1.0 / CORNER_DIAG) / (summed + before), 0.0)
                W[i, t] = inverse
                for c in range(3):
                    here = load_of(c, i, t)
                    z = inverse * here
                    Z[0, c, i, t] = z
                    store_parts(c, i, t, z)
                    if in_block(i, t):
                        L0[c, i - 4] = here
                        bz = bz + z * here
            before = summed

    def yz_modes(i, t):
        result = {}
        for c, s in PARTS:
            part = G[2 * c + s, i, 8 * t : 8 * t + 8]
            higher = G[2 * c + s, i, 8 * t + 1 : 8 * t + 9]
            result[c, 0, s] = part + higher
            result[c, 1, s] = higher - part
        return result

    def apply(k):
        for t in range(2):
            near = yz_modes(1 + k, t)
            passed = None
            for i in range(1 + k, NI - 1 - k):
                far = yz_modes(i + 1, t)
                modes = modes_of(near, far)
                mixed = combine(modes)
                if 3 <= i <= NI - 4:
                    energy = None
                    for key, n in NUMBER.items():
                        factor = mixed[key] if key[0] == "s" else modes[mode_of(key)]
                        term = factor * F[n, i - 3, t]
                        energy = term if energy is None else energy + term
                    value = energy * SC[i - 3, t]
                    DV[k, i - 3, 8 + 8 * t : 16 + 8 * t] = value
                    if t == 1:
                        DV[k, i - 3, 0:8] = value
                young = MOD[i, t]
                scaled = {kind: young * factor for kind, factor in SCALES.items()}
                forces = {}
                for key, value in mixed.items():
                    force = scaled[key[0]] * value
                    forces[mode_of(key)] = force
                    if key[0] == "s":
                        forces[axes(key[1]) + (key[2],)] = force
                following = {}
                for c, s in PARTS:
                    node = {}
                    for b in (0, 1):
                        slope = forces[1, b, s, c]
                        if (0, b, s, c) in forces:
                            level = forces[0, b, s, c]
                            low, following[c, b, s] = level - slope, level + slope
                            node[b] = low if passed is None else passed[c, b, s] + low
                        else:
                            following[c, b, s] = slope
                            node[b] = -slope if passed is None else passed[c, b, s] - slope
                    if i > 1 + k:
                        DS[2 * c + s, i, t] = node[0] - node[1]
                        both = node[0] + node[1]
                        SS[2 * c + s, i, 8 + 8 * t : 16 + 8 * t] = both
                        if t == 1:
                            SS[2 * c + s, i, 0:8] = both
                passed, near = following, far

    def image(c, i, t):
        level, slope = [
            DS[2 * c + s, i, t] + SS[2 * c + s, i, 7 + 8 * t : 15 + 8 * t] for s in (0, 1)
        ]
        return level - slope + down_z(level + slope, lane)

    for p in range(RX + 3):
        for t in range(2):
            for c in range(3):
                v = disp_of(c, p, t)
                above = up_z(v, lane)
                for s, part in ((0, v + above), (1, above - v)):
                    SS[2 * c + s, p, 8 * t : 8 * t + 8] = part
                    if t == 0:
                        SS[2 * c + s, p, 16:24] = part
    for t in range(2):
        near = None
        for p in range(RX + 3):
            far = {}
            for c, s in PARTS:
                part = SS[2 * c + s, p, 8 * t : 8 * t + 8]
                higher = SS[2 * c + s, p, 8 * t + 1 : 8 * t + 9]
                far[c, 0, s] = part + higher
                far[c, 1, s] = higher - part
            if near is not None:
                for key, value in combine(modes_of(near, far)).items():
                    F[NUMBER[key], p - 1, t] = value * SCALES[key[0]]
            near = far

    def add(total, i, t, one, two):
        return total + one * two if in_block(i, t) else total

    h00 = b1 = h01 = h11 = b2 = h12 = h22 = h02 = zero
    apply(0)
    for t in range(2):
        for i in range(2, NI - 1):
            for c in range(3):
                q = image(c, i, t)
                z = Z[0, c, i, t]
                y = W[i, t] * q - z
                Z[1, c, i, t] = y
                store_parts(c, i, t, y)
                h00 = add(h00, i, t, z, q)
                h01 = add(h01, i, t, y, q)
                if in_block(i, t):
                    b1 = b1 + y * L0[c, i - 4]
    apply(1)
    for t in range(2):
        for i in range(3, NI - 2):
            for c in range(3):
                q = image(c, i, t)
                z = Z[1, c, i, t]
                y = W[i, t] * q - z
                Z[2, c, i, t] = y
                store_parts(c, i, t, y)
                h11 = add(h11, i, t, z, q)
                h12 = add(h12, i, t, y, q)
                if in_block(i, t):
                    b2 = b2 + y * L0[c, i - 4]
    apply(2)
    for i in range(4, 4 + RX):
        for c in range(3):
            q = image(c, i, 0)
            h22 = add(h22, i, 0, Z[2, c, i, 0], q)
            h02 = add(h02, i, 0, Z[0, c, i, 0], q)

    lanes = lax.broadcasted_iota(jnp.int32, (1, NZ), 1)
    line = jnp.zeros((1, NZ), F32)
    for n, value in enumerate((bz, b1, b2, h00, h01, h02, h11, h12, h22)):
        whole = jnp.sum(value, axis=0, keepdims=True)
        whole = jnp.sum(whole, axis=1, keepdims=True)
        line = line + jnp.where(lanes == n, whole, 0.0)
    for n in range(sums.shape[0]):
        sums[n] = line

    for k in range(3):
        cells, beside = [], []
        for p in range(RX + 2):
            cells.append(DV[k, p, 8:16])
            beside.append(DV[k, p, 7:15] + DV[k, p, 9:17])
            if p >= 2:
                senses[k, p - 2] = filtered(cells, beside, p - 1)
        for c in range(3):
            basis[k, c] = Z[k, c, 4 : 4 + RX, 0]


def final_kernel(gathered, basis, senses, adjoint, sensitivity):
    total = jnp.sum(gathered[...], axis=0)

    def value(n):
        return jnp.broadcast_to(total[:, n : n + 1], (1, NZ))

    b0, b1, b2, h00, h01, h02, h11, h12, h22 = [value(n) for n in range(9)]
    l1, l2 = h01 / h00, h02 / h00
    d1 = h11 - l1 * h01
    e = h12 - l1 * h02
    fine1 = d1 > 0.0
    l3 = jnp.where(fine1, e / d1, 0.0)
    d2 = h22 - l2 * h02 - l3 * e
    t1 = b1 - l1 * b0
    t2 = b2 - l2 * b0 - l3 * t1
    c2 = jnp.where(d2 > 0.0, t2 / d2, 0.0)
    c1 = jnp.where(fine1, t1 / d1, 0.0) - l3 * c2
    c0 = b0 / h00 - l1 * c1 - l2 * c2
    adjoint[...] = c0 * basis[0] + c1 * basis[1] + c2 * basis[2]
    sensitivity[...] = c0 * senses[0] + c1 * senses[1] + c2 * senses[2]


VMEM = pl.BlockSpec(memory_space=pltpu.VMEM)


def call(kernel, inputs, outs, scratch=(), limit=None, extra=0):
    single = not isinstance(outs, list)
    shapes = [outs] if single else outs
    result = pl.pallas_call(
        kernel,
        out_shape=[jax.ShapeDtypeStruct(s, F32) for s in shapes],
        in_specs=[VMEM] * (len(inputs) - extra) + [pl.BlockSpec(memory_space=pl.ANY)] * extra,
        out_specs=[VMEM] * len(shapes),
        scratch_shapes=[pltpu.VMEM(s, F32) for s in scratch],
        compiler_params=pltpu.CompilerParams(vmem_limit_bytes=limit or 32 * 1024 * 1024),
    )(*inputs)
    return result[0] if single else result


MAIN_SCRATCH = [
    (3, RX, 8, NZ),
    (3, NI - 1, 8, NZ),
    (NI - 1, 8, NZ),
    (3, RX + 3, 8, NZ),
    (NI + 2, 40, NZ),
    (NI, 2, 8, NZ),
    (RX + 2, 2, 8, NZ),
    (NI, 24, NZ),
    (NI, 2, 8, NZ),
    (3, 3, NI, 2, 8, NZ),
    (6, NI, 24, NZ),
    (6, NI, 2, 8, NZ),
    (6, NI, 24, NZ),
    (len(KEYS), RX + 2, 2, 8, NZ),
    (3, RX + 2, 24, NZ),
]


def swaps(start, count):
    pairs = [(i, i + 1) for i in range(start, count - 1, 2)]
    return pairs + [(j, i) for i, j in pairs]


def shards(displacement, adjoint_load, density, fixed_mask, load_nodes, load_forces):
    count_x = lax.axis_size("x") * lax.axis_size("y")
    count_y = lax.axis_size("z") * lax.axis_size("c")
    own = (adjoint_load, displacement, density, fixed_mask)
    first, second = pl.pallas_call(
        pack_x_kernel,
        out_shape=[pltpu.VMEM((UP_X, RY, NZ), F32), pltpu.VMEM((UP_X + 1, RY, NZ), F32)],
        in_specs=[pl.BlockSpec(memory_space=pltpu.HBM)] * 4,
        out_specs=[VMEM] * 2,
        scratch_shapes=[
            pltpu.VMEM((LOW_X, RY, NZ), F32),
            pltpu.VMEM((UP_X, RY, NZ), F32),
            pltpu.VMEM((7, RY, NZ), jnp.int32),
            pltpu.SemaphoreType.DMA((16,)),
        ],
    )(*own)
    second = lax.ppermute(second, ("x", "y"), swaps(1, count_x))
    first = lax.ppermute(first, ("x", "y"), swaps(0, count_x))
    sizes = (NEAR + CORNER, 4, NZ)
    second, low, up = call(
        pack_second_kernel,
        own + (first, second),
        [(NEAR + CORNER + 1, 4, NZ), (LOW_X, RY, NZ), (UP_X, RY, NZ)],
    )
    placed = call(
        loads_kernel, (load_nodes, load_forces, low), (3, NI - 1, 2, RY, NZ), extra=1
    )
    first = call(functools.partial(pack_y_kernel, 0), own + (low, up, placed), sizes, extra=1)
    second = lax.ppermute(second, ("z", "c"), swaps(1, count_y))
    first = lax.ppermute(first, "c", swaps(0, 2))
    close = lax.axis_size("c") * count_x
    far = lax.axis_size("z")
    basis, senses, sums = call(
        main_kernel,
        own + (low, up, placed, first, second),
        [(3, 3, RX, RY, NZ), (3, RX, RY, NZ), (close, 1, NZ)],
        MAIN_SCRATCH,
        48 * 1024 * 1024,
    )
    sums = lax.all_to_all(sums, ("x", "y", "c"), 0, 0, tiled=True)
    sums = jnp.broadcast_to(jnp.sum(sums, axis=0, keepdims=True), (far, 1, NZ))
    sums = lax.all_to_all(sums, "z", 0, 0, tiled=True)
    adjoint, sensitivity = call(
        final_kernel, (sums, basis, senses), [(3, RX, RY, NZ), (RX, RY, NZ)]
    )
    return adjoint, sensitivity


def solution(mesh):
    size_x, size_y = mesh.shape["gx"], mesh.shape["gy"]
    side = int(round(size_x**0.5))
    whole = Mesh(
        mesh.devices.reshape(side, size_x // side, size_y // 2, 2), ("x", "y", "z", "c")
    )
    field = P(None, ("x", "y"), ("z", "c"), None)
    grid = P(("x", "y"), ("z", "c"), None)
    return jax.shard_map(
        shards,
        mesh=whole,
        in_specs=(field, field, grid, grid, P(), P()),
        out_specs=(field, grid),
        check_vma=False,
    )
```

```python
import functools

import jax
import jax.numpy as jnp
import numpy as np
from jax import lax
from jax.experimental import pallas as pl
from jax.experimental.pallas import tpu as pltpu
from jax.sharding import Mesh, PartitionSpec as P

POISSON = 0.3
PENALTY = 3.0
SOFT = 0.001
CORNERS = [(a, b, c) for c in (0, 1) for b in (0, 1) for a in (0, 1)]
EDGE = float(1.5 - np.sqrt(2.0))

RX, RY, NZ = 12, 8, 128
NI = RX + 8
LOW_X, UP_X = 20, 27
NEAR, CORNER = 81, 46
CHUNK = 256
F32 = jnp.float32


def element_stiffness():
    lame_first = POISSON / ((1.0 + POISSON) * (1.0 - 2.0 * POISSON))
    shear_mod = 1.0 / (2.0 * (1.0 + POISSON))
    elastic = np.zeros((6, 6))
    elastic[:3, :3] = lame_first
    for axis_number in range(3):
        elastic[axis_number, axis_number] = lame_first + 2.0 * shear_mod
        elastic[axis_number + 3, axis_number + 3] = shear_mod
    points = [0.5 - 0.5 / np.sqrt(3.0), 0.5 + 0.5 / np.sqrt(3.0)]
    matrix = np.zeros((24, 24))
    for point_x in points:
        for point_y in points:
            for point_z in points:
                coords = (point_x, point_y, point_z)
                strain = np.zeros((6, 24))
                for number, corner in enumerate(CORNERS):
                    factors = [coords[d] if corner[d] else 1.0 - coords[d] for d in range(3)]
                    slopes = [1.0 if corner[d] else -1.0 for d in range(3)]
                    derivs = [
                        slopes[0] * factors[1] * factors[2],
                        factors[0] * slopes[1] * factors[2],
                        factors[0] * factors[1] * slopes[2],
                    ]
                    column = 3 * number
                    strain[0, column] = derivs[0]
                    strain[1, column + 1] = derivs[1]
                    strain[2, column + 2] = derivs[2]
                    strain[3, column] = derivs[1]
                    strain[3, column + 1] = derivs[0]
                    strain[4, column + 1] = derivs[2]
                    strain[4, column + 2] = derivs[1]
                    strain[5, column] = derivs[2]
                    strain[5, column + 2] = derivs[0]
                matrix += strain.T @ elastic @ strain / 8.0
    return matrix


def modal_stiffness():
    one = np.array([[1.0, 1.0], [-1.0, 1.0]])
    change = np.zeros((8, 8))
    for row, (a, b, c) in enumerate(CORNERS):
        for column, (p, q, r) in enumerate(CORNERS):
            change[row, column] = one[a, p] * one[b, q] * one[c, r]
    inverse = np.linalg.inv(np.kron(change, np.eye(3)))
    modal = inverse.T @ element_stiffness() @ inverse
    modes = [corner + (d,) for corner in CORNERS for d in range(3)]
    return {(modes[i], modes[j]): float(modal[i, j]) for i in range(24) for j in range(24)}


MODAL_VALUE = modal_stiffness()
CORNER_DIAG = float(element_stiffness()[0, 0])


def pack_x_kernel(*refs):
    sources, (first, second), targets, done = refs[:6], refs[6:8], refs[8:14], refs[14]
    copies = [
        pltpu.make_async_copy(source, target, done.at[n])
        for n, (source, target) in enumerate(zip(sources, targets))
    ]
    for copy in copies:
        copy.start()
    for copy in copies:
        copy.wait()
    load, disp, dens, mask = targets[:4]

    def put_low(out):
        for c in range(3):
            out[3 * c : 3 * c + 3] = load[c, RX - 3 : RX]
            out[17 + c] = disp[c, RX - 1]
        out[9:12] = (1 - mask[RX - 3 : RX]).astype(F32)
        out[12:17] = dens[RX - 5 : RX]

    def put_up(out):
        for c in range(3):
            out[4 * c : 4 * c + 4] = load[c, 0:4]
            out[21 + 2 * c : 23 + 2 * c] = disp[c, 0:2]
        out[12:16] = (1 - mask[0:4]).astype(F32)
        out[16:21] = dens[0:5]

    even = lax.rem(lax.axis_index("y"), 2) == 0

    @pl.when(even)
    def _():
        put_low(first)
        put_up(second)

    @pl.when(jnp.logical_not(even))
    def _():
        put_up(first)
        put_low(second)


def loads_kernel(nodes, forces, out):
    first_x = (lax.axis_index("x") * lax.axis_size("y") + lax.axis_index("y")) * RX - 3
    first_y = (lax.axis_index("z") * lax.axis_size("c") + lax.axis_index("c")) * RY
    count = (NI - 1) * RY
    chunk = CHUNK
    place = lax.broadcasted_iota(jnp.int32, (count, chunk), 0)
    depth = lax.broadcasted_iota(jnp.int32, (2 * NZ, chunk), 0)
    total = jnp.zeros((9 * count, 2 * NZ), F32)
    for start in range(0, nodes.shape[1], chunk):
        cols = slice(start, start + chunk)
        local_x = nodes[0:1, cols] - first_x
        local_y = nodes[1:2, cols] - first_y
        inside = (local_x >= 0) & (local_x < NI - 1) & (local_y >= -4) & (local_y < RY + 4)
        spot = jnp.where(inside, local_x * RY + (local_y & (RY - 1)), -1)
        hit = place == spot
        outer = jnp.where((local_y < 0) | (local_y >= RY), NZ, 0)
        layer = jnp.where(depth == nodes[2:3, cols] + outer, 1.0, 0.0).astype(jnp.bfloat16)
        parts = []
        for c in range(3):
            rest = forces[c : c + 1, cols]
            for _ in range(3):
                head = rest.astype(jnp.bfloat16).astype(F32)
                rest = rest - head
                parts.append(jnp.where(hit, head, 0.0).astype(jnp.bfloat16))
        total = total + lax.dot_general(
            jnp.concatenate(parts, axis=0),
            layer,
            (((1,), (1,)), ((), ())),
            preferred_element_type=F32,
        )
    for c in range(3):
        base = 3 * c * count
        summed = (
            total[base : base + count]
            + total[base + count : base + 2 * count]
            + total[base + 2 * count : base + 3 * count]
        )
        for t in range(2):
            out[c, :, t] = summed[:, t * NZ : t * NZ + NZ].reshape(NI - 1, RY, NZ)


def pack_second_kernel(load, disp, dens, mask, first, second, _, out, low, up):
    even = lax.rem(lax.axis_index("y"), 2) == 0

    @pl.when(even)
    def _():
        up[...] = first[0:UP_X]
        low[...] = second[0:LOW_X]

    @pl.when(jnp.logical_not(even))
    def _():
        up[...] = second[0:UP_X]
        low[...] = first[0:LOW_X]

    pack_y_kernel(1, load, disp, dens, mask, low, up, out)


def pack_y_kernel(which, load, disp, dens, mask, low, up, *rest):
    out = rest[-1]

    def write(rows, extra, count, at):
        free = lambda part: (1 - part).astype(F32)
        for c in range(3):
            out[12 * c : 12 * c + 12] = load[c, :, rows]
            q = NEAR + 7 * c
            out[q : q + 3] = low[3 * c : 3 * c + 3, rows]
            out[q + 3 : q + 7] = up[4 * c : 4 * c + 4, rows]
        out[36:48] = free(mask[:, rows])
        out[48:60] = dens[:, rows]
        q = NEAR + 21
        out[q : q + 3] = low[9:12, rows]
        out[q + 3 : q + 7] = up[12:16, rows]
        out[q + 7 : q + 12] = low[12:17, rows]
        out[q + 12 : q + 17] = up[16:21, rows]
        for p in range(12):
            out[60 + p // 4, p % 4 : p % 4 + 1] = dens[p, extra : extra + 1]
        for r in range(10):
            source = low[12 + r, extra : extra + 1] if r < 5 else up[11 + r, extra : extra + 1]
            out[NEAR + 38 + r // 4, r % 4 : r % 4 + 1] = source
        per = 4 // count
        for n in range(36):
            spot = count * (n % per)
            out[63 + n // per, spot : spot + count] = disp[n // 12, n % 12, at : at + count]
        for n in range(9):
            c, m = n // 3, n % 3
            source = low[17 + c] if m == 0 else up[20 + 2 * c + m]
            spot = count * (n % per)
            out[NEAR + 41 + n // per, spot : spot + count] = source[at : at + count]

    upper = lax.axis_index("c") == which

    @pl.when(upper)
    def _():
        write(slice(4, 8), 3, 1, 7)

    @pl.when(jnp.logical_not(upper))
    def _():
        write(slice(0, 4), 4, 2, 0)


def up_z(v, lane):
    return jnp.where(lane < NZ - 1, pltpu.roll(v, NZ - 1, 1), 0.0)


def down_z(v, lane):
    return jnp.where(lane > 0, pltpu.roll(v, 1, 1), 0.0)


def axes(*ones):
    return tuple(int(n in ones) for n in range(3))


K_SHEAR = MODAL_VALUE[axes(1) + (0,), axes(0) + (1,)]
K_NORMAL = MODAL_VALUE[axes(0) + (0,), axes(0) + (0,)]
K_CROSS = MODAL_VALUE[axes(0) + (0,), axes(1) + (1,)]
K_BEND = MODAL_VALUE[axes(0, 1) + (0,), axes(0, 1) + (0,)]
K_BEND_OFF = MODAL_VALUE[axes(0, 1) + (0,), axes(1, 2) + (2,)]
K_TWIST = MODAL_VALUE[axes(0, 1) + (2,), axes(0, 2) + (1,)]
K_LAST = MODAL_VALUE[axes(0, 1, 2) + (0,), axes(0, 1, 2) + (0,)]
PAIRS = [(0, 1), (0, 2), (1, 2)]
BENDS = [(0, 1, 2), (1, 0, 2), (0, 2, 1)]


def combine(h):
    out = {}
    for d, e in PAIRS:
        out["s", d, e] = h[axes(e) + (d,)] + h[axes(d) + (e,)]
    normal = [h[axes(d) + (d,)] for d in range(3)]
    total = normal[0] + normal[1] + normal[2]
    for d in range(3):
        out["n", d] = normal[d] * ((K_NORMAL - K_CROSS) / K_CROSS) + total
    for d, e, f in BENDS:
        one, two = h[axes(d, e) + (d,)], h[axes(e, f) + (f,)]
        out["b", d, e] = one * (K_BEND / K_BEND_OFF) + two
        out["b", f, e] = two * (K_BEND / K_BEND_OFF) + one
    twist = [h[axes(*[n for n in range(3) if n != d]) + (d,)] for d in range(3)]
    total = twist[0] + twist[1] + twist[2]
    for d in range(3):
        out["t", d] = twist[d] + total
        out["l", d] = h[axes(0, 1, 2) + (d,)]
    return out


SCALES = {"s": K_SHEAR, "n": K_CROSS, "b": K_BEND_OFF, "t": K_TWIST, "l": K_LAST}


def mode_of(key):
    kind = key[0]
    if kind == "s":
        return axes(key[2]) + (key[1],)
    if kind == "n":
        return axes(key[1]) + (key[1],)
    if kind == "b":
        return axes(key[1], key[2]) + (key[1],)
    if kind == "t":
        return axes(*[n for n in range(3) if n != key[1]]) + (key[1],)
    return axes(0, 1, 2) + (key[1],)


def modes_of(near, far):
    result = {}
    for key in near:
        c, b, s = key
        result[0, b, s, c] = near[key] + far[key]
        result[1, b, s, c] = far[key] - near[key]
    return result


def filtered(cells, beside, p, lane):
    side = cells[p - 1] + cells[p + 1]
    far = beside[p - 1] + beside[p + 1]
    deep = 0.5 * cells[p] + EDGE * (beside[p] + side)
    deep = up_z(deep, lane) + down_z(deep, lane)
    return 1.5 * cells[p] + 0.5 * (beside[p] + side) + EDGE * far + deep


KEYS = [("s", d, e) for d, e in PAIRS] + [("n", d) for d in range(3)]
KEYS += [("b", d, e) for d, e, f in BENDS] + [("b", f, e) for d, e, f in BENDS]
KEYS += [("t", d) for d in range(3)] + [("l", d) for d in range(3)]
NUMBER = {key: n for n, key in enumerate(KEYS)}
PARTS = [(c, s) for c in range(3) for s in (0, 1)]


def store_parts(parts, c, i, t, v, lane):
    above = up_z(v, lane)
    for s, part in ((0, v + above), (1, above - v)):
        parts[2 * c + s, i, 8 * t : 8 * t + 8] = part
        if t == 0:
            parts[2 * c + s, i, 16:24] = part


def yz_modes(parts, i, t):
    result = {}
    for c, s in PARTS:
        part = parts[2 * c + s, i, 8 * t : 8 * t + 8]
        higher = parts[2 * c + s, i, 8 * t + 1 : 8 * t + 9]
        result[c, 0, s] = part + higher
        result[c, 1, s] = higher - part
    return result


def main_kernel(load, disp, dens, mask, low, up, placed, first, second, Z, SC, D1, sums, G, L0, L1, FR1, DN, MOD, HP, W, DS, SS):
    gx = lax.axis_index("x") * lax.axis_size("y") + lax.axis_index("y")
    gy = lax.axis_index("z") * lax.axis_size("c") + lax.axis_index("c")
    extent_x = RX * lax.axis_size("x") * lax.axis_size("y")
    extent_y = RY * lax.axis_size("z") * lax.axis_size("c")
    lane = lax.broadcasted_iota(jnp.int32, (8, NZ), 1)
    row = lax.broadcasted_iota(jnp.int32, (8, NZ), 0)
    upper_half = row < 4

    DN[0:5, 16:24] = low[12:17]
    DN[5 : 5 + RX, 16:24] = dens[...]
    DN[5 + RX : 10 + RX, 16:24] = up[16:21]
    D1[...] = jnp.zeros(D1.shape, F32)

    def fill(below, above):
        below_corner, above_corner = below.at[NEAR : NEAR + CORNER], above.at[NEAR : NEAR + CORNER]
        for rows, near, corner in (
            (slice(0, 4), above, above_corner),
            (slice(4, 8), below, below_corner),
        ):
            for c in range(3):
                L1[c, 0:3, rows] = corner[7 * c : 7 * c + 3]
                L1[c, 3:15, rows] = near[12 * c : 12 * c + 12]
                L1[c, 15:19, rows] = corner[7 * c + 3 : 7 * c + 7]
            FR1[0:3, rows] = corner[21:24]
            FR1[3:15, rows] = near[36:48]
            FR1[15:19, rows] = corner[24:28]
        for rows, extra, near, corner in (
            (slice(24, 28), 28, above, above_corner),
            (slice(12, 16), 11, below, below_corner),
        ):
            DN[0:5, rows] = corner[28:33]
            DN[5:17, rows] = near[48:60]
            DN[17:22, rows] = corner[33:38]
            for p in range(22):
                if 5 <= p < 17:
                    one = near[60 + (p - 5) // 4, (p - 5) % 4 : (p - 5) % 4 + 1]
                else:
                    r = p if p < 5 else p - 12
                    one = corner[38 + r // 4, r % 4 : r % 4 + 1]
                DN[p, extra : extra + 1] = one
        for c in range(3):
            for p in range(12):
                n = 12 * c + p
                D1[c, p + 1, 7:8] = below[63 + n // 4, n % 4 : n % 4 + 1]
                D1[c, p + 1, 0:2] = above[63 + n // 2, 2 * (n % 2) : 2 * (n % 2) + 2]
            for m, p in enumerate((0, 13, 14)):
                n = 3 * c + m
                D1[c, p, 7:8] = below_corner[41 + n // 4, n % 4 : n % 4 + 1]
                D1[c, p, 0:2] = above_corner[41 + n // 2, 2 * (n % 2) : 2 * (n % 2) + 2]

    even = lax.axis_index("c") == 0

    @pl.when(even)
    def _():
        fill(second, first)

    @pl.when(jnp.logical_not(even))
    def _():
        fill(first, second)

    def load_of(c, i, t):
        if t == 1:
            value = L1[c, i - 1]
        elif i < 4:
            value = low[3 * c + i - 1]
        elif i < 4 + RX:
            value = load[c, i - 4]
        else:
            value = up[4 * c + i - 4 - RX]
        return value + placed[c, i - 1, t]

    def is_free(i, t):
        if t == 1:
            return FR1[i - 1] > 0.5
        if i < 4:
            return low[9 + i - 1] > 0.5
        if i < 4 + RX:
            return mask[i - 4] == 0
        return up[12 + i - 4 - RX] > 0.5

    near_z = 2.0 - jnp.where(lane == 0, 1.0, 0.0) - jnp.where(lane == NZ - 1, 1.0, 0.0)
    inside_y, part_a, part_b = [], [], []
    for t in range(2):
        place_y = gy * RY + (row if t == 0 else jnp.where(upper_half, row + 8, row - 8))
        inside_y.append(jnp.where((place_y >= 0) & (place_y < extent_y), 1.0, 0.0))
        near_y = 2.0 - jnp.where(place_y == 0, 1.0, 0.0) - jnp.where(place_y == extent_y - 1, 1.0, 0.0)
        part_a.append(1.5 + 0.5 * (near_y + near_z) + EDGE * near_y * near_z)
        part_b.append(0.5 + EDGE * (near_y + near_z))

    def density_rows(p, t, shift):
        if t == 0:
            return DN[p, 16 + shift : 24 + shift]
        return jnp.where(
            upper_half, DN[p, 24 + shift : 32 + shift], DN[p, 8 + shift : 16 + shift]
        )

    for t in range(2):
        cells, beside = [], []
        for p in range(NI + 2):
            cells.append(density_rows(p, t, 0))
            beside.append(density_rows(p, t, -1) + density_rows(p, t, 1))
            i = p - 2
            if i < 0:
                continue
            place_x = gx * RX - 4 + i
            inside_x = jnp.where((place_x >= 0) & (place_x < extent_x), 1.0, 0.0)
            near_x = 2.0 - jnp.where(place_x == 0, 1.0, 0.0) - jnp.where(place_x == extent_x - 1, 1.0, 0.0)
            inverse = 1.0 / (part_a[t] + near_x * part_b[t])
            physical = filtered(cells, beside, p - 1, lane) * inverse
            squared = physical * physical
            inside = inside_y[t] * inside_x
            mod = inside * (SOFT + (1.0 - SOFT) * (squared * physical))
            MOD[i, t] = mod
            if 3 <= i <= NI - 4:
                SC[i - 3, t] = (inside * (PENALTY * (1.0 - SOFT))) * (squared * inverse)
            deep = mod + down_z(mod, lane)
            HP[i, 8 + 8 * t : 16 + 8 * t] = deep
            if t == 1:
                HP[i, 0:8] = deep

    zero = jnp.zeros((8, NZ), F32)

    def in_block(i, t):
        return t == 0 and 4 <= i < 4 + RX

    bz = zero
    for t in range(2):
        before = None
        for i in range(NI):
            summed = HP[i, 8 + 8 * t : 16 + 8 * t] + HP[i, 7 + 8 * t : 15 + 8 * t]
            if i > 0:
                inverse = jnp.where(is_free(i, t), (1.0 / CORNER_DIAG) / (summed + before), 0.0)
                W[i, t] = inverse
                for c in range(3):
                    here = load_of(c, i, t)
                    z = inverse * here
                    Z[0, c, i, t] = z
                    store_parts(G, c, i, t, z, lane)
                    if in_block(i, t):
                        L0[c, i - 4] = here
                        bz = bz + z * here
            before = summed

    def apply(k):
        for t in range(2):
            near = yz_modes(G, 1 + k, t)
            passed = None
            for i in range(1 + k, NI - 1 - k):
                far = yz_modes(G, i + 1, t)
                modes = modes_of(near, far)
                mixed = combine(modes)
                young = MOD[i, t]
                scaled = {kind: young * factor for kind, factor in SCALES.items()}
                forces = {}
                for key, value in mixed.items():
                    force = scaled[key[0]] * value
                    forces[mode_of(key)] = force
                    if key[0] == "s":
                        forces[axes(key[1]) + (key[2],)] = force
                following = {}
                for c, s in PARTS:
                    node = {}
                    for b in (0, 1):
                        slope = forces[1, b, s, c]
                        if (0, b, s, c) in forces:
                            level = forces[0, b, s, c]
                            low, following[c, b, s] = level - slope, level + slope
                            node[b] = low if passed is None else passed[c, b, s] + low
                        else:
                            following[c, b, s] = slope
                            node[b] = -slope if passed is None else passed[c, b, s] - slope
                    if i > 1 + k:
                        DS[2 * c + s, i, t] = node[0] - node[1]
                        both = node[0] + node[1]
                        SS[2 * c + s, i, 8 + 8 * t : 16 + 8 * t] = both
                        if t == 1:
                            SS[2 * c + s, i, 0:8] = both
                passed, near = following, far

    def image(c, i, t):
        level, slope = [
            DS[2 * c + s, i, t] + SS[2 * c + s, i, 7 + 8 * t : 15 + 8 * t] for s in (0, 1)
        ]
        return level - slope + down_z(level + slope, lane)

    def add(total, i, t, one, two):
        return total + one * two if in_block(i, t) else total

    h00 = b1 = h01 = h11 = b2 = h12 = h22 = h02 = zero
    apply(0)
    for t in range(2):
        for i in range(2, NI - 1):
            for c in range(3):
                q = image(c, i, t)
                z = Z[0, c, i, t]
                y = W[i, t] * q - z
                Z[1, c, i, t] = y
                store_parts(G, c, i, t, y, lane)
                h00 = add(h00, i, t, z, q)
                h01 = add(h01, i, t, y, q)
                if in_block(i, t):
                    b1 = b1 + y * L0[c, i - 4]
    apply(1)
    for t in range(2):
        for i in range(3, NI - 2):
            for c in range(3):
                q = image(c, i, t)
                z = Z[1, c, i, t]
                y = W[i, t] * q - z
                Z[2, c, i, t] = y
                store_parts(G, c, i, t, y, lane)
                h11 = add(h11, i, t, z, q)
                h12 = add(h12, i, t, y, q)
                if in_block(i, t):
                    b2 = b2 + y * L0[c, i - 4]
    apply(2)
    for i in range(4, 4 + RX):
        for c in range(3):
            q = image(c, i, 0)
            h22 = add(h22, i, 0, Z[2, c, i, 0], q)
            h02 = add(h02, i, 0, Z[0, c, i, 0], q)

    lanes = lax.broadcasted_iota(jnp.int32, (1, NZ), 1)
    line = jnp.zeros((1, NZ), F32)
    for n, value in enumerate((bz, b1, b2, h00, h01, h02, h11, h12, h22)):
        whole = jnp.sum(value, axis=0, keepdims=True)
        whole = jnp.sum(whole, axis=1, keepdims=True)
        line = line + jnp.where(lanes == n, whole, 0.0)
    for n in range(sums.shape[0]):
        sums[n] = line


def sense_kernel(disp, low, up, D1, Z, SC, senses, U, F, DV):
    lane = lax.broadcasted_iota(jnp.int32, (8, NZ), 1)

    def disp_of(c, p, t):
        if t == 1:
            return D1[c, p]
        if p == 0:
            return low[17 + c]
        return disp[c, p - 1] if p <= RX else up[21 + 2 * c + p - 1 - RX]

    for p in range(RX + 3):
        for t in range(2):
            for c in range(3):
                store_parts(U.at[3], c, p, t, disp_of(c, p, t), lane)
                for k in range(3):
                    store_parts(U.at[k], c, p, t, Z[k, c, p + 3, t], lane)
    for t in range(2):
        near = yz_modes(U.at[3], 0, t)
        for p in range(RX + 2):
            far = yz_modes(U.at[3], p + 1, t)
            for key, value in combine(modes_of(near, far)).items():
                F[NUMBER[key], p, t] = value * SCALES[key[0]]
            near = far

    for k in range(3):
        for t in range(2):
            near = yz_modes(U.at[k], 0, t)
            for p in range(RX + 2):
                far = yz_modes(U.at[k], p + 1, t)
                modes = modes_of(near, far)
                energy = None
                for key, n in NUMBER.items():
                    factor = modes[mode_of(key)]
                    if key[0] == "s":
                        factor = factor + modes[axes(key[1]) + (key[2],)]
                    term = factor * F[n, p, t]
                    energy = term if energy is None else energy + term
                value = energy * SC[p, t]
                DV[k, p, 8 + 8 * t : 16 + 8 * t] = value
                if t == 1:
                    DV[k, p, 0:8] = value
                near = far
        cells, beside = [], []
        for p in range(RX + 2):
            cells.append(DV[k, p, 8:16])
            beside.append(DV[k, p, 7:15] + DV[k, p, 9:17])
            if p >= 2:
                senses[k, p - 2] = filtered(cells, beside, p - 1, lane)


def final_kernel(gathered, basis, senses, adjoint, sensitivity):
    total = jnp.sum(gathered[...], axis=0)

    def value(n):
        return jnp.broadcast_to(total[:, n : n + 1], (1, NZ))

    b0, b1, b2, h00, h01, h02, h11, h12, h22 = [value(n) for n in range(9)]
    l1, l2 = h01 / h00, h02 / h00
    d1 = h11 - l1 * h01
    e = h12 - l1 * h02
    fine1 = d1 > 0.0
    l3 = jnp.where(fine1, e / d1, 0.0)
    d2 = h22 - l2 * h02 - l3 * e
    t1 = b1 - l1 * b0
    t2 = b2 - l2 * b0 - l3 * t1
    c2 = jnp.where(d2 > 0.0, t2 / d2, 0.0)
    c1 = jnp.where(fine1, t1 / d1, 0.0) - l3 * c2
    c0 = b0 / h00 - l1 * c1 - l2 * c2
    own = slice(4, 4 + RX)
    for c in range(3):
        one, two, three = [basis[k, c, own, 0] for k in range(3)]
        adjoint[c] = c0 * one + c1 * two + c2 * three
    sensitivity[...] = c0 * senses[0] + c1 * senses[1] + c2 * senses[2]


VMEM = pl.BlockSpec(memory_space=pltpu.VMEM)


def call(kernel, inputs, outs, scratch=(), limit=None, extra=0, cost=None):
    single = not isinstance(outs, list)
    shapes = [outs] if single else outs
    result = pl.pallas_call(
        kernel,
        out_shape=[jax.ShapeDtypeStruct(s, F32) for s in shapes],
        in_specs=[VMEM] * (len(inputs) - extra) + [pl.BlockSpec(memory_space=pl.ANY)] * extra,
        out_specs=[VMEM] * len(shapes),
        scratch_shapes=[pltpu.VMEM(s, F32) for s in scratch],
        cost_estimate=cost and pl.CostEstimate(flops=0, bytes_accessed=cost, transcendentals=0),
        compiler_params=pltpu.CompilerParams(vmem_limit_bytes=limit or 32 * 1024 * 1024),
    )(*inputs)
    return result[0] if single else result


MAIN_SCRATCH = [
    (6, NI, 24, NZ),
    (3, RX, 8, NZ),
    (3, NI - 1, 8, NZ),
    (NI - 1, 8, NZ),
    (NI + 2, 40, NZ),
    (NI, 2, 8, NZ),
    (NI, 24, NZ),
    (NI, 2, 8, NZ),
    (6, NI, 2, 8, NZ),
    (6, NI, 24, NZ),
]
SENSE_SCRATCH = [
    (4, 6, RX + 3, 24, NZ),
    (len(KEYS), RX + 2, 2, 8, NZ),
    (3, RX + 2, 24, NZ),
]


def swaps(start, count):
    pairs = [(i, i + 1) for i in range(start, count - 1, 2)]
    return pairs + [(j, i) for i, j in pairs]


def shards(displacement, adjoint_load, density, fixed_mask, load_nodes, load_forces):
    count_x = lax.axis_size("x") * lax.axis_size("y")
    count_y = lax.axis_size("z") * lax.axis_size("c")
    given = (adjoint_load, displacement, density, fixed_mask, load_nodes, load_forces)
    first, second, *given = pl.pallas_call(
        pack_x_kernel,
        out_shape=[pltpu.VMEM((UP_X, RY, NZ), F32), pltpu.VMEM((UP_X + 1, RY, NZ), F32)]
        + [pltpu.VMEM(value.shape, value.dtype) for value in given],
        in_specs=[pl.BlockSpec(memory_space=pltpu.HBM)] * 6,
        out_specs=[VMEM] * 8,
        scratch_shapes=[pltpu.SemaphoreType.DMA((6,))],
    )(*given)
    own, loads = tuple(given[:4]), tuple(given[4:])
    second = lax.ppermute(second, ("x", "y"), swaps(1, count_x))
    first = lax.ppermute(first, ("x", "y"), swaps(0, count_x))
    placed = call(loads_kernel, loads, (3, NI - 1, 2, RY, NZ))
    sizes = (NEAR + CORNER, 4, NZ)
    second, low, up = call(
        pack_second_kernel,
        own + (first, second, placed),
        [(NEAR + CORNER + 1, 4, NZ), (LOW_X, RY, NZ), (UP_X, RY, NZ)],
        extra=1,
    )
    first = call(functools.partial(pack_y_kernel, 0), own + (low, up, second), sizes, extra=1)
    second = lax.ppermute(second, ("z", "c"), swaps(1, count_y))
    first = lax.ppermute(first, "c", swaps(0, 2))
    close = lax.axis_size("c") * count_x
    far = lax.axis_size("z")
    basis, scale, outer, sums = call(
        main_kernel,
        own + (low, up, placed, first, second),
        [
            (3, 3, NI, 2, 8, NZ),
            (RX + 2, 2, 8, NZ),
            (3, RX + 3, 8, NZ),
            (close, 1, NZ),
        ],
        MAIN_SCRATCH,
        48 * 1024 * 1024,
    )
    senses = call(
        sense_kernel,
        (own[1], low, up, outer, basis, scale),
        (3, RX, RY, NZ),
        SENSE_SCRATCH,
        cost=6_000_000,
    )
    sums = lax.all_to_all(sums, ("x", "y", "c"), 0, 0, tiled=True)
    sums = jnp.broadcast_to(jnp.sum(sums, axis=0, keepdims=True), (far, 1, NZ))
    sums = lax.all_to_all(sums, "z", 0, 0, tiled=True)
    adjoint, sensitivity = call(
        final_kernel, (sums, basis, senses), [(3, RX, RY, NZ), (RX, RY, NZ)]
    )
    return adjoint, sensitivity


def solution(mesh):
    size_x, size_y = mesh.shape["gx"], mesh.shape["gy"]
    side = int(round(size_x**0.5))
    whole = Mesh(
        mesh.devices.reshape(side, size_x // side, size_y // 2, 2), ("x", "y", "z", "c")
    )
    field = P(None, ("x", "y"), ("z", "c"), None)
    grid = P(("x", "y"), ("z", "c"), None)
    return jax.shard_map(
        shards,
        mesh=whole,
        in_specs=(field, field, grid, grid, P(), P()),
        out_specs=(field, grid),
        check_vma=False,
    )
```

```python
import functools

import jax
import jax.numpy as jnp
import numpy as np
from jax import lax
from jax.experimental import pallas as pl
from jax.experimental.pallas import tpu as pltpu
from jax.sharding import Mesh, PartitionSpec as P

POISSON = 0.3
PENALTY = 3.0
SOFT = 0.001
CORNERS = [(a, b, c) for c in (0, 1) for b in (0, 1) for a in (0, 1)]
EDGE = float(1.5 - np.sqrt(2.0))

RX, RY, NZ = 12, 8, 128
NI = RX + 8
LOW_X, UP_X = 20, 27
NEAR, CORNER = 81, 46
CHUNK = 256
F32 = jnp.float32


def element_stiffness():
    lame_first = POISSON / ((1.0 + POISSON) * (1.0 - 2.0 * POISSON))
    shear_mod = 1.0 / (2.0 * (1.0 + POISSON))
    elastic = np.zeros((6, 6))
    elastic[:3, :3] = lame_first
    for axis_number in range(3):
        elastic[axis_number, axis_number] = lame_first + 2.0 * shear_mod
        elastic[axis_number + 3, axis_number + 3] = shear_mod
    points = [0.5 - 0.5 / np.sqrt(3.0), 0.5 + 0.5 / np.sqrt(3.0)]
    matrix = np.zeros((24, 24))
    for point_x in points:
        for point_y in points:
            for point_z in points:
                coords = (point_x, point_y, point_z)
                strain = np.zeros((6, 24))
                for number, corner in enumerate(CORNERS):
                    factors = [coords[d] if corner[d] else 1.0 - coords[d] for d in range(3)]
                    slopes = [1.0 if corner[d] else -1.0 for d in range(3)]
                    derivs = [
                        slopes[0] * factors[1] * factors[2],
                        factors[0] * slopes[1] * factors[2],
                        factors[0] * factors[1] * slopes[2],
                    ]
                    column = 3 * number
                    strain[0, column] = derivs[0]
                    strain[1, column + 1] = derivs[1]
                    strain[2, column + 2] = derivs[2]
                    strain[3, column] = derivs[1]
                    strain[3, column + 1] = derivs[0]
                    strain[4, column + 1] = derivs[2]
                    strain[4, column + 2] = derivs[1]
                    strain[5, column] = derivs[2]
                    strain[5, column + 2] = derivs[0]
                matrix += strain.T @ elastic @ strain / 8.0
    return matrix


def modal_stiffness():
    one = np.array([[1.0, 1.0], [-1.0, 1.0]])
    change = np.zeros((8, 8))
    for row, (a, b, c) in enumerate(CORNERS):
        for column, (p, q, r) in enumerate(CORNERS):
            change[row, column] = one[a, p] * one[b, q] * one[c, r]
    inverse = np.linalg.inv(np.kron(change, np.eye(3)))
    modal = inverse.T @ element_stiffness() @ inverse
    modes = [corner + (d,) for corner in CORNERS for d in range(3)]
    return {(modes[i], modes[j]): float(modal[i, j]) for i in range(24) for j in range(24)}


MODAL_VALUE = modal_stiffness()
CORNER_DIAG = float(element_stiffness()[0, 0])


def pack_x_kernel(*refs):
    sources, (first, second), targets, done = refs[:6], refs[6:8], refs[8:14], refs[14]
    copies = [
        pltpu.make_async_copy(source, target, done.at[n])
        for n, (source, target) in enumerate(zip(sources, targets))
    ]
    for copy in copies:
        copy.start()
    for copy in copies:
        copy.wait()
    load, disp, dens, mask = targets[:4]

    def put_low(out):
        for c in range(3):
            out[3 * c : 3 * c + 3] = load[c, RX - 3 : RX]
            out[17 + c] = disp[c, RX - 1]
        out[9:12] = (1 - mask[RX - 3 : RX]).astype(F32)
        out[12:17] = dens[RX - 5 : RX]

    def put_up(out):
        for c in range(3):
            out[4 * c : 4 * c + 4] = load[c, 0:4]
            out[21 + 2 * c : 23 + 2 * c] = disp[c, 0:2]
        out[12:16] = (1 - mask[0:4]).astype(F32)
        out[16:21] = dens[0:5]

    even = lax.rem(lax.axis_index("y"), 2) == 0

    @pl.when(even)
    def _():
        put_low(first)
        put_up(second)

    @pl.when(jnp.logical_not(even))
    def _():
        put_up(first)
        put_low(second)


def loads_kernel(nodes, forces, out):
    first_x = (lax.axis_index("x") * lax.axis_size("y") + lax.axis_index("y")) * RX - 3
    first_y = (lax.axis_index("z") * lax.axis_size("c") + lax.axis_index("c")) * RY
    count = (NI - 1) * RY
    chunk = CHUNK
    place = lax.broadcasted_iota(jnp.int32, (count, chunk), 0)
    depth = lax.broadcasted_iota(jnp.int32, (2 * NZ, chunk), 0)
    total = jnp.zeros((9 * count, 2 * NZ), F32)
    for start in range(0, nodes.shape[1], chunk):
        cols = slice(start, start + chunk)
        local_x = nodes[0:1, cols] - first_x
        local_y = nodes[1:2, cols] - first_y
        inside = (local_x >= 0) & (local_x < NI - 1) & (local_y >= -4) & (local_y < RY + 4)
        spot = jnp.where(inside, local_x * RY + (local_y & (RY - 1)), -1)
        hit = place == spot
        outer = jnp.where((local_y < 0) | (local_y >= RY), NZ, 0)
        layer = jnp.where(depth == nodes[2:3, cols] + outer, 1.0, 0.0).astype(jnp.bfloat16)
        parts = []
        for c in range(3):
            rest = forces[c : c + 1, cols]
            for _ in range(3):
                head = rest.astype(jnp.bfloat16).astype(F32)
                rest = rest - head
                parts.append(jnp.where(hit, head, 0.0))
        total = total + lax.dot_general(
            jnp.concatenate(parts, axis=0).astype(jnp.bfloat16),
            layer,
            (((1,), (1,)), ((), ())),
            preferred_element_type=F32,
        )
    for c in range(3):
        base = 3 * c * count
        summed = (
            total[base : base + count]
            + total[base + count : base + 2 * count]
            + total[base + 2 * count : base + 3 * count]
        )
        for t in range(2):
            out[c, :, t] = summed[:, t * NZ : t * NZ + NZ].reshape(NI - 1, RY, NZ)


def pack_second_kernel(load, disp, dens, mask, first, second, _, out, low, up):
    even = lax.rem(lax.axis_index("y"), 2) == 0

    @pl.when(even)
    def _():
        up[...] = first[0:UP_X]
        low[...] = second[0:LOW_X]

    @pl.when(jnp.logical_not(even))
    def _():
        up[...] = second[0:UP_X]
        low[...] = first[0:LOW_X]

    pack_y_kernel(1, load, disp, dens, mask, low, up, out)


def pack_y_kernel(which, load, disp, dens, mask, low, up, *rest):
    out = rest[-1]

    def write(rows, extra, count, at):
        free = lambda part: (1 - part).astype(F32)
        for c in range(3):
            out[12 * c : 12 * c + 12] = load[c, :, rows]
            q = NEAR + 7 * c
            out[q : q + 3] = low[3 * c : 3 * c + 3, rows]
            out[q + 3 : q + 7] = up[4 * c : 4 * c + 4, rows]
        out[36:48] = free(mask[:, rows])
        out[48:60] = dens[:, rows]
        q = NEAR + 21
        out[q : q + 3] = low[9:12, rows]
        out[q + 3 : q + 7] = up[12:16, rows]
        out[q + 7 : q + 12] = low[12:17, rows]
        out[q + 12 : q + 17] = up[16:21, rows]
        for p in range(12):
            out[60 + p // 4, p % 4 : p % 4 + 1] = dens[p, extra : extra + 1]
        for r in range(10):
            source = low[12 + r, extra : extra + 1] if r < 5 else up[11 + r, extra : extra + 1]
            out[NEAR + 38 + r // 4, r % 4 : r % 4 + 1] = source
        per = 4 // count
        for n in range(36):
            spot = count * (n % per)
            out[63 + n // per, spot : spot + count] = disp[n // 12, n % 12, at : at + count]
        for n in range(9):
            c, m = n // 3, n % 3
            source = low[17 + c] if m == 0 else up[20 + 2 * c + m]
            spot = count * (n % per)
            out[NEAR + 41 + n // per, spot : spot + count] = source[at : at + count]

    upper = lax.axis_index("c") == which

    @pl.when(upper)
    def _():
        write(slice(4, 8), 3, 1, 7)

    @pl.when(jnp.logical_not(upper))
    def _():
        write(slice(0, 4), 4, 2, 0)


def up_z(v, lane):
    return jnp.where(lane < NZ - 1, pltpu.roll(v, NZ - 1, 1), 0.0)


def down_z(v, lane):
    return jnp.where(lane > 0, pltpu.roll(v, 1, 1), 0.0)


def axes(*ones):
    return tuple(int(n in ones) for n in range(3))


K_SHEAR = MODAL_VALUE[axes(1) + (0,), axes(0) + (1,)]
K_NORMAL = MODAL_VALUE[axes(0) + (0,), axes(0) + (0,)]
K_CROSS = MODAL_VALUE[axes(0) + (0,), axes(1) + (1,)]
K_BEND = MODAL_VALUE[axes(0, 1) + (0,), axes(0, 1) + (0,)]
K_BEND_OFF = MODAL_VALUE[axes(0, 1) + (0,), axes(1, 2) + (2,)]
K_TWIST = MODAL_VALUE[axes(0, 1) + (2,), axes(0, 2) + (1,)]
K_LAST = MODAL_VALUE[axes(0, 1, 2) + (0,), axes(0, 1, 2) + (0,)]
PAIRS = [(0, 1), (0, 2), (1, 2)]
BENDS = [(0, 1, 2), (1, 0, 2), (0, 2, 1)]


def combine(h):
    out = {}
    for d, e in PAIRS:
        out["s", d, e] = h[axes(e) + (d,)] + h[axes(d) + (e,)]
    normal = [h[axes(d) + (d,)] for d in range(3)]
    total = normal[0] + normal[1] + normal[2]
    for d in range(3):
        out["n", d] = normal[d] * ((K_NORMAL - K_CROSS) / K_CROSS) + total
    for d, e, f in BENDS:
        one, two = h[axes(d, e) + (d,)], h[axes(e, f) + (f,)]
        out["b", d, e] = one * (K_BEND / K_BEND_OFF) + two
        out["b", f, e] = two * (K_BEND / K_BEND_OFF) + one
    twist = [h[axes(*[n for n in range(3) if n != d]) + (d,)] for d in range(3)]
    total = twist[0] + twist[1] + twist[2]
    for d in range(3):
        out["t", d] = twist[d] + total
        out["l", d] = h[axes(0, 1, 2) + (d,)]
    return out


SCALES = {"s": K_SHEAR, "n": K_CROSS, "b": K_BEND_OFF, "t": K_TWIST, "l": K_LAST}


def mode_of(key):
    kind = key[0]
    if kind == "s":
        return axes(key[2]) + (key[1],)
    if kind == "n":
        return axes(key[1]) + (key[1],)
    if kind == "b":
        return axes(key[1], key[2]) + (key[1],)
    if kind == "t":
        return axes(*[n for n in range(3) if n != key[1]]) + (key[1],)
    return axes(0, 1, 2) + (key[1],)


def modes_of(near, far):
    result = {}
    for key in near:
        c, b, s = key
        result[0, b, s, c] = near[key] + far[key]
        result[1, b, s, c] = far[key] - near[key]
    return result


def filtered(cells, beside, p, lane):
    side = cells[p - 1] + cells[p + 1]
    far = beside[p - 1] + beside[p + 1]
    deep = 0.5 * cells[p] + EDGE * (beside[p] + side)
    deep = up_z(deep, lane) + down_z(deep, lane)
    return 1.5 * cells[p] + 0.5 * (beside[p] + side) + EDGE * far + deep


KEYS = [("s", d, e) for d, e in PAIRS] + [("n", d) for d in range(3)]
KEYS += [("b", d, e) for d, e, f in BENDS] + [("b", f, e) for d, e, f in BENDS]
KEYS += [("t", d) for d in range(3)] + [("l", d) for d in range(3)]
NUMBER = {key: n for n, key in enumerate(KEYS)}
PARTS = [(c, s) for c in range(3) for s in (0, 1)]


def store_parts(parts, c, i, t, v, lane):
    above = up_z(v, lane)
    for s, part in ((0, v + above), (1, above - v)):
        parts[2 * c + s, i, 8 * t : 8 * t + 8] = part
        if t == 0:
            parts[2 * c + s, i, 16:24] = part


def yz_modes(parts, i, t):
    result = {}
    for c, s in PARTS:
        part = parts[2 * c + s, i, 8 * t : 8 * t + 8]
        higher = parts[2 * c + s, i, 8 * t + 1 : 8 * t + 9]
        result[c, 0, s] = part + higher
        result[c, 1, s] = higher - part
    return result


def main_kernel(load, disp, dens, mask, low, up, placed, first, second, Z, SC, D1, sums, G, L0, L1, FR1, DN, MOD, HP, W, DS, SS):
    gx = lax.axis_index("x") * lax.axis_size("y") + lax.axis_index("y")
    gy = lax.axis_index("z") * lax.axis_size("c") + lax.axis_index("c")
    extent_x = RX * lax.axis_size("x") * lax.axis_size("y")
    extent_y = RY * lax.axis_size("z") * lax.axis_size("c")
    lane = lax.broadcasted_iota(jnp.int32, (8, NZ), 1)
    row = lax.broadcasted_iota(jnp.int32, (8, NZ), 0)
    upper_half = row < 4

    DN[0:5, 16:24] = low[12:17]
    DN[5 : 5 + RX, 16:24] = dens[...]
    DN[5 + RX : 10 + RX, 16:24] = up[16:21]
    D1[...] = jnp.zeros(D1.shape, F32)

    def fill(below, above):
        below_corner, above_corner = below.at[NEAR : NEAR + CORNER], above.at[NEAR : NEAR + CORNER]
        for rows, near, corner in (
            (slice(0, 4), above, above_corner),
            (slice(4, 8), below, below_corner),
        ):
            for c in range(3):
                L1[c, 0:3, rows] = corner[7 * c : 7 * c + 3]
                L1[c, 3:15, rows] = near[12 * c : 12 * c + 12]
                L1[c, 15:19, rows] = corner[7 * c + 3 : 7 * c + 7]
            FR1[0:3, rows] = corner[21:24]
            FR1[3:15, rows] = near[36:48]
            FR1[15:19, rows] = corner[24:28]
        for rows, extra, near, corner in (
            (slice(24, 28), 28, above, above_corner),
            (slice(12, 16), 11, below, below_corner),
        ):
            DN[0:5, rows] = corner[28:33]
            DN[5:17, rows] = near[48:60]
            DN[17:22, rows] = corner[33:38]
            for p in range(22):
                if 5 <= p < 17:
                    one = near[60 + (p - 5) // 4, (p - 5) % 4 : (p - 5) % 4 + 1]
                else:
                    r = p if p < 5 else p - 12
                    one = corner[38 + r // 4, r % 4 : r % 4 + 1]
                DN[p, extra : extra + 1] = one
        for c in range(3):
            for p in range(12):
                n = 12 * c + p
                D1[c, p + 1, 7:8] = below[63 + n // 4, n % 4 : n % 4 + 1]
                D1[c, p + 1, 0:2] = above[63 + n // 2, 2 * (n % 2) : 2 * (n % 2) + 2]
            for m, p in enumerate((0, 13, 14)):
                n = 3 * c + m
                D1[c, p, 7:8] = below_corner[41 + n // 4, n % 4 : n % 4 + 1]
                D1[c, p, 0:2] = above_corner[41 + n // 2, 2 * (n % 2) : 2 * (n % 2) + 2]

    even = lax.axis_index("c") == 0

    @pl.when(even)
    def _():
        fill(second, first)

    @pl.when(jnp.logical_not(even))
    def _():
        fill(first, second)

    def load_of(c, i, t):
        if t == 1:
            value = L1[c, i - 1]
        elif i < 4:
            value = low[3 * c + i - 1]
        elif i < 4 + RX:
            value = load[c, i - 4]
        else:
            value = up[4 * c + i - 4 - RX]
        return value + placed[c, i - 1, t]

    def is_free(i, t):
        if t == 1:
            return FR1[i - 1] > 0.5
        if i < 4:
            return low[9 + i - 1] > 0.5
        if i < 4 + RX:
            return mask[i - 4] == 0
        return up[12 + i - 4 - RX] > 0.5

    near_z = 2.0 - jnp.where(lane == 0, 1.0, 0.0) - jnp.where(lane == NZ - 1, 1.0, 0.0)
    inside_y, part_a, part_b = [], [], []
    for t in range(2):
        place_y = gy * RY + (row if t == 0 else jnp.where(upper_half, row + 8, row - 8))
        inside_y.append(jnp.where((place_y >= 0) & (place_y < extent_y), 1.0, 0.0))
        near_y = 2.0 - jnp.where(place_y == 0, 1.0, 0.0) - jnp.where(place_y == extent_y - 1, 1.0, 0.0)
        part_a.append(1.5 + 0.5 * (near_y + near_z) + EDGE * near_y * near_z)
        part_b.append(0.5 + EDGE * (near_y + near_z))

    def density_rows(p, t, shift):
        if t == 0:
            return DN[p, 16 + shift : 24 + shift]
        return jnp.where(
            upper_half, DN[p, 24 + shift : 32 + shift], DN[p, 8 + shift : 16 + shift]
        )

    for t in range(2):
        cells, beside = [], []
        for p in range(NI + 2):
            cells.append(density_rows(p, t, 0))
            beside.append(density_rows(p, t, -1) + density_rows(p, t, 1))
            i = p - 2
            if i < 0:
                continue
            place_x = gx * RX - 4 + i
            inside_x = jnp.where((place_x >= 0) & (place_x < extent_x), 1.0, 0.0)
            near_x = 2.0 - jnp.where(place_x == 0, 1.0, 0.0) - jnp.where(place_x == extent_x - 1, 1.0, 0.0)
            inverse = 1.0 / (part_a[t] + near_x * part_b[t])
            physical = filtered(cells, beside, p - 1, lane) * inverse
            squared = physical * physical
            inside = inside_y[t] * inside_x
            mod = inside * (SOFT + (1.0 - SOFT) * (squared * physical))
            MOD[i, t] = mod
            if 3 <= i <= NI - 4:
                SC[i - 3, t] = (inside * (PENALTY * (1.0 - SOFT))) * (squared * inverse)
            deep = mod + down_z(mod, lane)
            HP[i, 8 + 8 * t : 16 + 8 * t] = deep
            if t == 1:
                HP[i, 0:8] = deep

    zero = jnp.zeros((8, NZ), F32)

    def in_block(i, t):
        return t == 0 and 4 <= i < 4 + RX

    bz = zero
    for t in range(2):
        before = None
        for i in range(NI):
            summed = HP[i, 8 + 8 * t : 16 + 8 * t] + HP[i, 7 + 8 * t : 15 + 8 * t]
            if i > 0:
                inverse = jnp.where(is_free(i, t), (1.0 / CORNER_DIAG) / (summed + before), 0.0)
                W[i, t] = inverse
                for c in range(3):
                    here = load_of(c, i, t)
                    z = inverse * here
                    Z[0, c, i, t] = z
                    store_parts(G, c, i, t, z, lane)
                    if in_block(i, t):
                        L0[c, i - 4] = here
                        bz = bz + z * here
            before = summed

    def apply(k):
        for t in range(2):
            near = yz_modes(G, 1 + k, t)
            passed = None
            for i in range(1 + k, NI - 1 - k):
                far = yz_modes(G, i + 1, t)
                modes = modes_of(near, far)
                mixed = combine(modes)
                young = MOD[i, t]
                scaled = {kind: young * factor for kind, factor in SCALES.items()}
                forces = {}
                for key, value in mixed.items():
                    force = scaled[key[0]] * value
                    forces[mode_of(key)] = force
                    if key[0] == "s":
                        forces[axes(key[1]) + (key[2],)] = force
                following = {}
                for c, s in PARTS:
                    node = {}
                    for b in (0, 1):
                        slope = forces[1, b, s, c]
                        if (0, b, s, c) in forces:
                            level = forces[0, b, s, c]
                            low, following[c, b, s] = level - slope, level + slope
                            node[b] = low if passed is None else passed[c, b, s] + low
                        else:
                            following[c, b, s] = slope
                            node[b] = -slope if passed is None else passed[c, b, s] - slope
                    if i > 1 + k:
                        DS[2 * c + s, i, t] = node[0] - node[1]
                        both = node[0] + node[1]
                        SS[2 * c + s, i, 8 + 8 * t : 16 + 8 * t] = both
                        if t == 1:
                            SS[2 * c + s, i, 0:8] = both
                passed, near = following, far

    def image(c, i, t):
        level, slope = [
            DS[2 * c + s, i, t] + SS[2 * c + s, i, 7 + 8 * t : 15 + 8 * t] for s in (0, 1)
        ]
        return level - slope + down_z(level + slope, lane)

    def add(total, i, t, one, two):
        return total + one * two if in_block(i, t) else total

    h00 = b1 = h01 = h11 = b2 = h12 = h22 = h02 = zero
    apply(0)
    for t in range(2):
        for i in range(2, NI - 1):
            for c in range(3):
                q = image(c, i, t)
                z = Z[0, c, i, t]
                y = W[i, t] * q - z
                Z[1, c, i, t] = y
                store_parts(G, c, i, t, y, lane)
                h00 = add(h00, i, t, z, q)
                h01 = add(h01, i, t, y, q)
                if in_block(i, t):
                    b1 = b1 + y * L0[c, i - 4]
    apply(1)
    for t in range(2):
        for i in range(3, NI - 2):
            for c in range(3):
                q = image(c, i, t)
                z = Z[1, c, i, t]
                y = W[i, t] * q - z
                Z[2, c, i, t] = y
                store_parts(G, c, i, t, y, lane)
                h11 = add(h11, i, t, z, q)
                h12 = add(h12, i, t, y, q)
                if in_block(i, t):
                    b2 = b2 + y * L0[c, i - 4]
    apply(2)
    for i in range(4, 4 + RX):
        for c in range(3):
            q = image(c, i, 0)
            h22 = add(h22, i, 0, Z[2, c, i, 0], q)
            h02 = add(h02, i, 0, Z[0, c, i, 0], q)

    lanes = lax.broadcasted_iota(jnp.int32, (1, NZ), 1)
    line = jnp.zeros((1, NZ), F32)
    for n, value in enumerate((bz, b1, b2, h00, h01, h02, h11, h12, h22)):
        whole = jnp.sum(value, axis=0, keepdims=True)
        whole = jnp.sum(whole, axis=1, keepdims=True)
        line = line + jnp.where(lanes == n, whole, 0.0)
    for n in range(sums.shape[0]):
        sums[n] = line


def sense_kernel(disp, low, up, D1, Z, SC, senses, U, F, DV):
    lane = lax.broadcasted_iota(jnp.int32, (8, NZ), 1)

    def disp_of(c, p, t):
        if t == 1:
            return D1[c, p]
        if p == 0:
            return low[17 + c]
        return disp[c, p - 1] if p <= RX else up[21 + 2 * c + p - 1 - RX]

    for p in range(RX + 3):
        for t in range(2):
            for c in range(3):
                store_parts(U.at[3], c, p, t, disp_of(c, p, t), lane)
                for k in range(3):
                    store_parts(U.at[k], c, p, t, Z[k, c, p + 3, t], lane)
    for t in range(2):
        near = yz_modes(U.at[3], 0, t)
        for p in range(RX + 2):
            far = yz_modes(U.at[3], p + 1, t)
            for key, value in combine(modes_of(near, far)).items():
                F[NUMBER[key], p, t] = value * SCALES[key[0]]
            near = far

    for k in range(3):
        for t in range(2):
            near = yz_modes(U.at[k], 0, t)
            for p in range(RX + 2):
                far = yz_modes(U.at[k], p + 1, t)
                modes = modes_of(near, far)
                energy = None
                for key, n in NUMBER.items():
                    factor = modes[mode_of(key)]
                    if key[0] == "s":
                        factor = factor + modes[axes(key[1]) + (key[2],)]
                    term = factor * F[n, p, t]
                    energy = term if energy is None else energy + term
                value = energy * SC[p, t]
                DV[k, p, 8 + 8 * t : 16 + 8 * t] = value
                if t == 1:
                    DV[k, p, 0:8] = value
                near = far
        cells, beside = [], []
        for p in range(RX + 2):
            cells.append(DV[k, p, 8:16])
            beside.append(DV[k, p, 7:15] + DV[k, p, 9:17])
            if p >= 2:
                senses[k, p - 2] = filtered(cells, beside, p - 1, lane)


def final_kernel(gathered, basis, senses, adjoint, sensitivity):
    total = jnp.sum(gathered[...], axis=0)

    def value(n):
        return jnp.broadcast_to(total[:, n : n + 1], (1, NZ))

    b0, b1, b2, h00, h01, h02, h11, h12, h22 = [value(n) for n in range(9)]
    l1, l2 = h01 / h00, h02 / h00
    d1 = h11 - l1 * h01
    e = h12 - l1 * h02
    fine1 = d1 > 0.0
    l3 = jnp.where(fine1, e / d1, 0.0)
    d2 = h22 - l2 * h02 - l3 * e
    t1 = b1 - l1 * b0
    t2 = b2 - l2 * b0 - l3 * t1
    c2 = jnp.where(d2 > 0.0, t2 / d2, 0.0)
    c1 = jnp.where(fine1, t1 / d1, 0.0) - l3 * c2
    c0 = b0 / h00 - l1 * c1 - l2 * c2
    own = slice(4, 4 + RX)
    for c in range(3):
        one, two, three = [basis[k, c, own, 0] for k in range(3)]
        adjoint[c] = c0 * one + c1 * two + c2 * three
    sensitivity[...] = c0 * senses[0] + c1 * senses[1] + c2 * senses[2]


VMEM = pl.BlockSpec(memory_space=pltpu.VMEM)


def call(kernel, inputs, outs, scratch=(), limit=None, extra=0, cost=None):
    single = not isinstance(outs, list)
    shapes = [outs] if single else outs
    result = pl.pallas_call(
        kernel,
        out_shape=[jax.ShapeDtypeStruct(s, F32) for s in shapes],
        in_specs=[VMEM] * (len(inputs) - extra) + [pl.BlockSpec(memory_space=pl.ANY)] * extra,
        out_specs=[VMEM] * len(shapes),
        scratch_shapes=[pltpu.VMEM(s, F32) for s in scratch],
        cost_estimate=cost and pl.CostEstimate(flops=0, bytes_accessed=cost, transcendentals=0),
        compiler_params=pltpu.CompilerParams(vmem_limit_bytes=limit or 32 * 1024 * 1024),
    )(*inputs)
    return result[0] if single else result


MAIN_SCRATCH = [
    (6, NI, 24, NZ),
    (3, RX, 8, NZ),
    (3, NI - 1, 8, NZ),
    (NI - 1, 8, NZ),
    (NI + 2, 40, NZ),
    (NI, 2, 8, NZ),
    (NI, 24, NZ),
    (NI, 2, 8, NZ),
    (6, NI, 2, 8, NZ),
    (6, NI, 24, NZ),
]
SENSE_SCRATCH = [
    (4, 6, RX + 3, 24, NZ),
    (len(KEYS), RX + 2, 2, 8, NZ),
    (3, RX + 2, 24, NZ),
]


def swaps(start, count):
    pairs = [(i, i + 1) for i in range(start, count - 1, 2)]
    return pairs + [(j, i) for i, j in pairs]


def shards(displacement, adjoint_load, density, fixed_mask, load_nodes, load_forces):
    count_x = lax.axis_size("x") * lax.axis_size("y")
    count_y = lax.axis_size("z") * lax.axis_size("c")
    given = (adjoint_load, displacement, density, fixed_mask, load_nodes, load_forces)
    first, second, *given = pl.pallas_call(
        pack_x_kernel,
        out_shape=[pltpu.VMEM((UP_X, RY, NZ), F32), pltpu.VMEM((UP_X + 1, RY, NZ), F32)]
        + [pltpu.VMEM(value.shape, value.dtype) for value in given],
        in_specs=[pl.BlockSpec(memory_space=pltpu.HBM)] * 6,
        out_specs=[VMEM] * 8,
        scratch_shapes=[pltpu.SemaphoreType.DMA((6,))],
    )(*given)
    own, loads = tuple(given[:4]), tuple(given[4:])
    second = lax.ppermute(second, ("x", "y"), swaps(1, count_x))
    first = lax.ppermute(first, ("x", "y"), swaps(0, count_x))
    placed = call(loads_kernel, loads, (3, NI - 1, 2, RY, NZ))
    sizes = (NEAR + CORNER, 4, NZ)
    second, low, up = call(
        pack_second_kernel,
        own + (first, second, placed),
        [(NEAR + CORNER + 1, 4, NZ), (LOW_X, RY, NZ), (UP_X, RY, NZ)],
        extra=1,
    )
    first = call(functools.partial(pack_y_kernel, 0), own + (low, up, second), sizes, extra=1)
    second = lax.ppermute(second, ("z", "c"), swaps(1, count_y))
    first = lax.ppermute(first, "c", swaps(0, 2))
    close = lax.axis_size("c") * count_x
    far = lax.axis_size("z")
    basis, scale, outer, sums = call(
        main_kernel,
        own + (low, up, placed, first, second),
        [
            (3, 3, NI, 2, 8, NZ),
            (RX + 2, 2, 8, NZ),
            (3, RX + 3, 8, NZ),
            (close, 1, NZ),
        ],
        MAIN_SCRATCH,
        48 * 1024 * 1024,
    )
    senses = call(
        sense_kernel,
        (own[1], low, up, outer, basis, scale),
        (3, RX, RY, NZ),
        SENSE_SCRATCH,
        cost=6_000_000,
    )
    sums = lax.all_to_all(sums, ("x", "y", "c"), 0, 0, tiled=True)
    sums = jnp.broadcast_to(jnp.sum(sums, axis=0, keepdims=True), (far, 1, NZ))
    sums = lax.all_to_all(sums, "z", 0, 0, tiled=True)
    adjoint, sensitivity = call(
        final_kernel, (sums, basis, senses), [(3, RX, RY, NZ), (RX, RY, NZ)]
    )
    return adjoint, sensitivity


def solution(mesh):
    size_x, size_y = mesh.shape["gx"], mesh.shape["gy"]
    side = int(round(size_x**0.5))
    whole = Mesh(
        mesh.devices.reshape(side, size_x // side, size_y // 2, 2), ("x", "y", "z", "c")
    )
    field = P(None, ("x", "y"), ("z", "c"), None)
    grid = P(("x", "y"), ("z", "c"), None)
    return jax.shard_map(
        shards,
        mesh=whole,
        in_specs=(field, field, grid, grid, P(), P()),
        out_specs=(field, grid),
        check_vma=False,
    )
```

```python
import functools

import jax
import jax.numpy as jnp
import numpy as np
from jax import lax
from jax.experimental import pallas as pl
from jax.experimental.pallas import tpu as pltpu
from jax.sharding import Mesh, PartitionSpec as P

POISSON = 0.3
PENALTY = 3.0
SOFT = 0.001
CORNERS = [(a, b, c) for c in (0, 1) for b in (0, 1) for a in (0, 1)]
EDGE = float(1.5 - np.sqrt(2.0))

RX, RY, NZ = 12, 8, 128
NI = RX + 8
LOW_X, UP_X = 20, 27
NEAR, CORNER = 81, 46
CHUNK = 256
F32 = jnp.float32


def element_stiffness():
    lame_first = POISSON / ((1.0 + POISSON) * (1.0 - 2.0 * POISSON))
    shear_mod = 1.0 / (2.0 * (1.0 + POISSON))
    elastic = np.zeros((6, 6))
    elastic[:3, :3] = lame_first
    for axis_number in range(3):
        elastic[axis_number, axis_number] = lame_first + 2.0 * shear_mod
        elastic[axis_number + 3, axis_number + 3] = shear_mod
    points = [0.5 - 0.5 / np.sqrt(3.0), 0.5 + 0.5 / np.sqrt(3.0)]
    matrix = np.zeros((24, 24))
    for point_x in points:
        for point_y in points:
            for point_z in points:
                coords = (point_x, point_y, point_z)
                strain = np.zeros((6, 24))
                for number, corner in enumerate(CORNERS):
                    factors = [coords[d] if corner[d] else 1.0 - coords[d] for d in range(3)]
                    slopes = [1.0 if corner[d] else -1.0 for d in range(3)]
                    derivs = [
                        slopes[0] * factors[1] * factors[2],
                        factors[0] * slopes[1] * factors[2],
                        factors[0] * factors[1] * slopes[2],
                    ]
                    column = 3 * number
                    strain[0, column] = derivs[0]
                    strain[1, column + 1] = derivs[1]
                    strain[2, column + 2] = derivs[2]
                    strain[3, column] = derivs[1]
                    strain[3, column + 1] = derivs[0]
                    strain[4, column + 1] = derivs[2]
                    strain[4, column + 2] = derivs[1]
                    strain[5, column] = derivs[2]
                    strain[5, column + 2] = derivs[0]
                matrix += strain.T @ elastic @ strain / 8.0
    return matrix


def modal_stiffness():
    one = np.array([[1.0, 1.0], [-1.0, 1.0]])
    change = np.zeros((8, 8))
    for row, (a, b, c) in enumerate(CORNERS):
        for column, (p, q, r) in enumerate(CORNERS):
            change[row, column] = one[a, p] * one[b, q] * one[c, r]
    inverse = np.linalg.inv(np.kron(change, np.eye(3)))
    modal = inverse.T @ element_stiffness() @ inverse
    modes = [corner + (d,) for corner in CORNERS for d in range(3)]
    return {(modes[i], modes[j]): float(modal[i, j]) for i in range(24) for j in range(24)}


MODAL_VALUE = modal_stiffness()
CORNER_DIAG = float(element_stiffness()[0, 0])


def pack_x_kernel(*refs):
    sources, (first, second), targets, done = refs[:6], refs[6:8], refs[8:14], refs[14]
    copies = [
        pltpu.make_async_copy(source, target, done.at[n])
        for n, (source, target) in enumerate(zip(sources, targets))
    ]
    for copy in copies:
        copy.start()
    for copy in copies:
        copy.wait()
    load, disp, dens, mask = targets[:4]

    def put_low(out):
        for c in range(3):
            out[3 * c : 3 * c + 3] = load[c, RX - 3 : RX]
            out[17 + c] = disp[c, RX - 1]
        out[9:12] = (1 - mask[RX - 3 : RX]).astype(F32)
        out[12:17] = dens[RX - 5 : RX]

    def put_up(out):
        for c in range(3):
            out[4 * c : 4 * c + 4] = load[c, 0:4]
            out[21 + 2 * c : 23 + 2 * c] = disp[c, 0:2]
        out[12:16] = (1 - mask[0:4]).astype(F32)
        out[16:21] = dens[0:5]

    even = lax.rem(lax.axis_index("y"), 2) == 0

    @pl.when(even)
    def _():
        put_low(first)
        put_up(second)

    @pl.when(jnp.logical_not(even))
    def _():
        put_up(first)
        put_low(second)


def loads_kernel(nodes, forces, out):
    first_x = (lax.axis_index("x") * lax.axis_size("y") + lax.axis_index("y")) * RX - 3
    first_y = (lax.axis_index("z") * lax.axis_size("c") + lax.axis_index("c")) * RY
    count = (NI - 1) * RY
    chunk = CHUNK
    place = lax.broadcasted_iota(jnp.int32, (count, chunk), 0)
    depth = lax.broadcasted_iota(jnp.int32, (2 * NZ, chunk), 0)
    total = jnp.zeros((9 * count, 2 * NZ), F32)
    for start in range(0, nodes.shape[1], chunk):
        cols = slice(start, start + chunk)
        local_x = nodes[0:1, cols] - first_x
        local_y = nodes[1:2, cols] - first_y
        inside = (local_x >= 0) & (local_x < NI - 1) & (local_y >= -4) & (local_y < RY + 4)
        spot = jnp.where(inside, local_x * RY + (local_y & (RY - 1)), -1)
        hit = place == spot
        outer = jnp.where((local_y < 0) | (local_y >= RY), NZ, 0)
        layer = jnp.where(depth == nodes[2:3, cols] + outer, 1.0, 0.0).astype(jnp.bfloat16)
        parts = []
        for c in range(3):
            rest = forces[c : c + 1, cols]
            for _ in range(3):
                head = rest.astype(jnp.bfloat16).astype(F32)
                rest = rest - head
                parts.append(jnp.where(hit, head, 0.0))
        total = total + lax.dot_general(
            jnp.concatenate(parts, axis=0).astype(jnp.bfloat16),
            layer,
            (((1,), (1,)), ((), ())),
            preferred_element_type=F32,
        )
    for c in range(3):
        base = 3 * c * count
        summed = (
            total[base : base + count]
            + total[base + count : base + 2 * count]
            + total[base + 2 * count : base + 3 * count]
        )
        for t in range(2):
            out[c, :, t] = summed[:, t * NZ : t * NZ + NZ].reshape(NI - 1, RY, NZ)


def pack_second_kernel(load, disp, dens, mask, first, second, _, out, low, up):
    even = lax.rem(lax.axis_index("y"), 2) == 0

    @pl.when(even)
    def _():
        up[...] = first[0:UP_X]
        low[...] = second[0:LOW_X]

    @pl.when(jnp.logical_not(even))
    def _():
        up[...] = second[0:UP_X]
        low[...] = first[0:LOW_X]

    pack_y_kernel(1, load, disp, dens, mask, low, up, out)


def pack_y_kernel(which, load, disp, dens, mask, low, up, *rest):
    out = rest[-1]

    def write(rows, extra, count, at):
        free = lambda part: (1 - part).astype(F32)
        for c in range(3):
            out[12 * c : 12 * c + 12] = load[c, :, rows]
            q = NEAR + 7 * c
            out[q : q + 3] = low[3 * c : 3 * c + 3, rows]
            out[q + 3 : q + 7] = up[4 * c : 4 * c + 4, rows]
        out[36:48] = free(mask[:, rows])
        out[48:60] = dens[:, rows]
        q = NEAR + 21
        out[q : q + 3] = low[9:12, rows]
        out[q + 3 : q + 7] = up[12:16, rows]
        out[q + 7 : q + 12] = low[12:17, rows]
        out[q + 12 : q + 17] = up[16:21, rows]
        for p in range(12):
            out[60 + p // 4, p % 4 : p % 4 + 1] = dens[p, extra : extra + 1]
        for r in range(10):
            source = low[12 + r, extra : extra + 1] if r < 5 else up[11 + r, extra : extra + 1]
            out[NEAR + 38 + r // 4, r % 4 : r % 4 + 1] = source
        per = 4 // count
        for n in range(36):
            spot = count * (n % per)
            out[63 + n // per, spot : spot + count] = disp[n // 12, n % 12, at : at + count]
        for n in range(9):
            c, m = n // 3, n % 3
            source = low[17 + c] if m == 0 else up[20 + 2 * c + m]
            spot = count * (n % per)
            out[NEAR + 41 + n // per, spot : spot + count] = source[at : at + count]

    upper = lax.axis_index("c") == which

    @pl.when(upper)
    def _():
        write(slice(4, 8), 3, 1, 7)

    @pl.when(jnp.logical_not(upper))
    def _():
        write(slice(0, 4), 4, 2, 0)


def up_z(v, lane):
    return jnp.where(lane < NZ - 1, pltpu.roll(v, NZ - 1, 1), 0.0)


def down_z(v, lane):
    return jnp.where(lane > 0, pltpu.roll(v, 1, 1), 0.0)


def axes(*ones):
    return tuple(int(n in ones) for n in range(3))


K_SHEAR = MODAL_VALUE[axes(1) + (0,), axes(0) + (1,)]
K_NORMAL = MODAL_VALUE[axes(0) + (0,), axes(0) + (0,)]
K_CROSS = MODAL_VALUE[axes(0) + (0,), axes(1) + (1,)]
K_BEND = MODAL_VALUE[axes(0, 1) + (0,), axes(0, 1) + (0,)]
K_BEND_OFF = MODAL_VALUE[axes(0, 1) + (0,), axes(1, 2) + (2,)]
K_TWIST = MODAL_VALUE[axes(0, 1) + (2,), axes(0, 2) + (1,)]
K_LAST = MODAL_VALUE[axes(0, 1, 2) + (0,), axes(0, 1, 2) + (0,)]
PAIRS = [(0, 1), (0, 2), (1, 2)]
BENDS = [(0, 1, 2), (1, 0, 2), (0, 2, 1)]


def combine(h):
    out = {}
    for d, e in PAIRS:
        out["s", d, e] = h[axes(e) + (d,)] + h[axes(d) + (e,)]
    normal = [h[axes(d) + (d,)] for d in range(3)]
    total = normal[0] + normal[1] + normal[2]
    for d in range(3):
        out["n", d] = normal[d] * ((K_NORMAL - K_CROSS) / K_CROSS) + total
    for d, e, f in BENDS:
        one, two = h[axes(d, e) + (d,)], h[axes(e, f) + (f,)]
        out["b", d, e] = one * (K_BEND / K_BEND_OFF) + two
        out["b", f, e] = two * (K_BEND / K_BEND_OFF) + one
    twist = [h[axes(*[n for n in range(3) if n != d]) + (d,)] for d in range(3)]
    total = twist[0] + twist[1] + twist[2]
    for d in range(3):
        out["t", d] = twist[d] + total
        out["l", d] = h[axes(0, 1, 2) + (d,)]
    return out


SCALES = {"s": K_SHEAR, "n": K_CROSS, "b": K_BEND_OFF, "t": K_TWIST, "l": K_LAST}


def mode_of(key):
    kind = key[0]
    if kind == "s":
        return axes(key[2]) + (key[1],)
    if kind == "n":
        return axes(key[1]) + (key[1],)
    if kind == "b":
        return axes(key[1], key[2]) + (key[1],)
    if kind == "t":
        return axes(*[n for n in range(3) if n != key[1]]) + (key[1],)
    return axes(0, 1, 2) + (key[1],)


def modes_of(near, far):
    result = {}
    for key in near:
        c, b, s = key
        result[0, b, s, c] = near[key] + far[key]
        result[1, b, s, c] = far[key] - near[key]
    return result


def filtered(cells, beside, p, lane):
    side = cells[p - 1] + cells[p + 1]
    far = beside[p - 1] + beside[p + 1]
    deep = 0.5 * cells[p] + EDGE * (beside[p] + side)
    deep = up_z(deep, lane) + down_z(deep, lane)
    return 1.5 * cells[p] + 0.5 * (beside[p] + side) + EDGE * far + deep


KEYS = [("s", d, e) for d, e in PAIRS] + [("n", d) for d in range(3)]
KEYS += [("b", d, e) for d, e, f in BENDS] + [("b", f, e) for d, e, f in BENDS]
KEYS += [("t", d) for d in range(3)] + [("l", d) for d in range(3)]
NUMBER = {key: n for n, key in enumerate(KEYS)}
PARTS = [(c, s) for c in range(3) for s in (0, 1)]


def store_parts(parts, c, i, t, v, lane):
    above = up_z(v, lane)
    for s, part in ((0, v + above), (1, above - v)):
        parts[2 * c + s, i, 8 * t : 8 * t + 8] = part
        if t == 0:
            parts[2 * c + s, i, 16:24] = part


def yz_modes(parts, i, t):
    result = {}
    for c, s in PARTS:
        part = parts[2 * c + s, i, 8 * t : 8 * t + 8]
        higher = parts[2 * c + s, i, 8 * t + 1 : 8 * t + 9]
        result[c, 0, s] = part + higher
        result[c, 1, s] = higher - part
    return result


def main_kernel(load, disp, dens, mask, low, up, placed, first, second, Z, SC, sums, G, L0, L1, FR1, DN, MOD, HP, W, DS, SS):
    gx = lax.axis_index("x") * lax.axis_size("y") + lax.axis_index("y")
    gy = lax.axis_index("z") * lax.axis_size("c") + lax.axis_index("c")
    extent_x = RX * lax.axis_size("x") * lax.axis_size("y")
    extent_y = RY * lax.axis_size("z") * lax.axis_size("c")
    lane = lax.broadcasted_iota(jnp.int32, (8, NZ), 1)
    row = lax.broadcasted_iota(jnp.int32, (8, NZ), 0)
    upper_half = row < 4

    DN[0:5, 16:24] = low[12:17]
    DN[5 : 5 + RX, 16:24] = dens[...]
    DN[5 + RX : 10 + RX, 16:24] = up[16:21]

    def fill(below, above):
        below_corner, above_corner = below.at[NEAR : NEAR + CORNER], above.at[NEAR : NEAR + CORNER]
        for rows, near, corner in (
            (slice(0, 4), above, above_corner),
            (slice(4, 8), below, below_corner),
        ):
            for c in range(3):
                L1[c, 0:3, rows] = corner[7 * c : 7 * c + 3]
                L1[c, 3:15, rows] = near[12 * c : 12 * c + 12]
                L1[c, 15:19, rows] = corner[7 * c + 3 : 7 * c + 7]
            FR1[0:3, rows] = corner[21:24]
            FR1[3:15, rows] = near[36:48]
            FR1[15:19, rows] = corner[24:28]
        for rows, extra, near, corner in (
            (slice(24, 28), 28, above, above_corner),
            (slice(12, 16), 11, below, below_corner),
        ):
            DN[0:5, rows] = corner[28:33]
            DN[5:17, rows] = near[48:60]
            DN[17:22, rows] = corner[33:38]
            for p in range(22):
                if 5 <= p < 17:
                    one = near[60 + (p - 5) // 4, (p - 5) % 4 : (p - 5) % 4 + 1]
                else:
                    r = p if p < 5 else p - 12
                    one = corner[38 + r // 4, r % 4 : r % 4 + 1]
                DN[p, extra : extra + 1] = one

    even = lax.axis_index("c") == 0

    @pl.when(even)
    def _():
        fill(second, first)

    @pl.when(jnp.logical_not(even))
    def _():
        fill(first, second)

    def load_of(c, i, t):
        if t == 1:
            value = L1[c, i - 1]
        elif i < 4:
            value = low[3 * c + i - 1]
        elif i < 4 + RX:
            value = load[c, i - 4]
        else:
            value = up[4 * c + i - 4 - RX]
        return value + placed[c, i - 1, t]

    def is_free(i, t):
        if t == 1:
            return FR1[i - 1] > 0.5
        if i < 4:
            return low[9 + i - 1] > 0.5
        if i < 4 + RX:
            return mask[i - 4] == 0
        return up[12 + i - 4 - RX] > 0.5

    near_z = 2.0 - jnp.where(lane == 0, 1.0, 0.0) - jnp.where(lane == NZ - 1, 1.0, 0.0)
    inside_y, part_a, part_b = [], [], []
    for t in range(2):
        place_y = gy * RY + (row if t == 0 else jnp.where(upper_half, row + 8, row - 8))
        inside_y.append(jnp.where((place_y >= 0) & (place_y < extent_y), 1.0, 0.0))
        near_y = 2.0 - jnp.where(place_y == 0, 1.0, 0.0) - jnp.where(place_y == extent_y - 1, 1.0, 0.0)
        part_a.append(1.5 + 0.5 * (near_y + near_z) + EDGE * near_y * near_z)
        part_b.append(0.5 + EDGE * (near_y + near_z))

    def density_rows(p, t, shift):
        if t == 0:
            return DN[p, 16 + shift : 24 + shift]
        return jnp.where(
            upper_half, DN[p, 24 + shift : 32 + shift], DN[p, 8 + shift : 16 + shift]
        )

    for t in range(2):
        cells, beside = [], []
        for p in range(NI + 2):
            cells.append(density_rows(p, t, 0))
            beside.append(density_rows(p, t, -1) + density_rows(p, t, 1))
            i = p - 2
            if i < 0:
                continue
            place_x = gx * RX - 4 + i
            inside_x = jnp.where((place_x >= 0) & (place_x < extent_x), 1.0, 0.0)
            near_x = 2.0 - jnp.where(place_x == 0, 1.0, 0.0) - jnp.where(place_x == extent_x - 1, 1.0, 0.0)
            inverse = 1.0 / (part_a[t] + near_x * part_b[t])
            physical = filtered(cells, beside, p - 1, lane) * inverse
            squared = physical * physical
            inside = inside_y[t] * inside_x
            mod = inside * (SOFT + (1.0 - SOFT) * (squared * physical))
            MOD[i, t] = mod
            if 3 <= i <= NI - 4:
                SC[i - 3, t] = (inside * (PENALTY * (1.0 - SOFT))) * (squared * inverse)
            deep = mod + down_z(mod, lane)
            HP[i, 8 + 8 * t : 16 + 8 * t] = deep
            if t == 1:
                HP[i, 0:8] = deep

    zero = jnp.zeros((8, NZ), F32)

    def in_block(i, t):
        return t == 0 and 4 <= i < 4 + RX

    bz = zero
    for t in range(2):
        before = None
        for i in range(NI):
            summed = HP[i, 8 + 8 * t : 16 + 8 * t] + HP[i, 7 + 8 * t : 15 + 8 * t]
            if i > 0:
                inverse = jnp.where(is_free(i, t), (1.0 / CORNER_DIAG) / (summed + before), 0.0)
                W[i, t] = inverse
                for c in range(3):
                    here = load_of(c, i, t)
                    z = inverse * here
                    Z[0, c, i, t] = z
                    store_parts(G, c, i, t, z, lane)
                    if in_block(i, t):
                        L0[c, i - 4] = here
                        bz = bz + z * here
            before = summed

    def apply(k):
        for t in range(2):
            near = yz_modes(G, 1 + k, t)
            passed = None
            for i in range(1 + k, NI - 1 - k):
                far = yz_modes(G, i + 1, t)
                modes = modes_of(near, far)
                mixed = combine(modes)
                young = MOD[i, t]
                scaled = {kind: young * factor for kind, factor in SCALES.items()}
                forces = {}
                for key, value in mixed.items():
                    force = scaled[key[0]] * value
                    forces[mode_of(key)] = force
                    if key[0] == "s":
                        forces[axes(key[1]) + (key[2],)] = force
                following = {}
                for c, s in PARTS:
                    node = {}
                    for b in (0, 1):
                        slope = forces[1, b, s, c]
                        if (0, b, s, c) in forces:
                            level = forces[0, b, s, c]
                            low, following[c, b, s] = level - slope, level + slope
                            node[b] = low if passed is None else passed[c, b, s] + low
                        else:
                            following[c, b, s] = slope
                            node[b] = -slope if passed is None else passed[c, b, s] - slope
                    if i > 1 + k:
                        DS[2 * c + s, i, t] = node[0] - node[1]
                        both = node[0] + node[1]
                        SS[2 * c + s, i, 8 + 8 * t : 16 + 8 * t] = both
                        if t == 1:
                            SS[2 * c + s, i, 0:8] = both
                passed, near = following, far

    def image(c, i, t):
        level, slope = [
            DS[2 * c + s, i, t] + SS[2 * c + s, i, 7 + 8 * t : 15 + 8 * t] for s in (0, 1)
        ]
        return level - slope + down_z(level + slope, lane)

    def add(total, i, t, one, two):
        return total + one * two if in_block(i, t) else total

    h00 = b1 = h01 = h11 = b2 = h12 = h22 = h02 = zero
    apply(0)
    for t in range(2):
        for i in range(2, NI - 1):
            for c in range(3):
                q = image(c, i, t)
                z = Z[0, c, i, t]
                y = W[i, t] * q - z
                Z[1, c, i, t] = y
                store_parts(G, c, i, t, y, lane)
                h00 = add(h00, i, t, z, q)
                h01 = add(h01, i, t, y, q)
                if in_block(i, t):
                    b1 = b1 + y * L0[c, i - 4]
    apply(1)
    for t in range(2):
        for i in range(3, NI - 2):
            for c in range(3):
                q = image(c, i, t)
                z = Z[1, c, i, t]
                y = W[i, t] * q - z
                Z[2, c, i, t] = y
                store_parts(G, c, i, t, y, lane)
                h11 = add(h11, i, t, z, q)
                h12 = add(h12, i, t, y, q)
                if in_block(i, t):
                    b2 = b2 + y * L0[c, i - 4]
    apply(2)
    for i in range(4, 4 + RX):
        for c in range(3):
            q = image(c, i, 0)
            h22 = add(h22, i, 0, Z[2, c, i, 0], q)
            h02 = add(h02, i, 0, Z[0, c, i, 0], q)

    lanes = lax.broadcasted_iota(jnp.int32, (1, NZ), 1)
    line = jnp.zeros((1, NZ), F32)
    for n, value in enumerate((bz, b1, b2, h00, h01, h02, h11, h12, h22)):
        whole = jnp.sum(value, axis=0, keepdims=True)
        whole = jnp.sum(whole, axis=1, keepdims=True)
        line = line + jnp.where(lanes == n, whole, 0.0)
    for n in range(sums.shape[0]):
        sums[n] = line


def sense_kernel(disp, low, up, first, second, Z, SC, senses, D1, U, F, DV):
    D1[...] = jnp.zeros(D1.shape, F32)

    def fill(below, below_corner, above, above_corner):
        for c in range(3):
            for p in range(12):
                n = 12 * c + p
                D1[c, p + 1, 7:8] = below[63 + n // 4, n % 4 : n % 4 + 1]
                D1[c, p + 1, 0:2] = above[63 + n // 2, 2 * (n % 2) : 2 * (n % 2) + 2]
            for m, p in enumerate((0, 13, 14)):
                n = 3 * c + m
                D1[c, p, 7:8] = below_corner[41 + n // 4, n % 4 : n % 4 + 1]
                D1[c, p, 0:2] = above_corner[41 + n // 2, 2 * (n % 2) : 2 * (n % 2) + 2]

    even = lax.axis_index("c") == 0

    @pl.when(even)
    def _():
        near, corner = second.at[0:NEAR], second.at[NEAR : NEAR + CORNER]
        fill(near, corner, first.at[0:NEAR], first.at[NEAR : NEAR + CORNER])

    @pl.when(jnp.logical_not(even))
    def _():
        near, corner = second.at[0:NEAR], second.at[NEAR : NEAR + CORNER]
        fill(first.at[0:NEAR], first.at[NEAR : NEAR + CORNER], near, corner)

    lane = lax.broadcasted_iota(jnp.int32, (8, NZ), 1)

    def disp_of(c, p, t):
        if t == 1:
            return D1[c, p]
        if p == 0:
            return low[17 + c]
        return disp[c, p - 1] if p <= RX else up[21 + 2 * c + p - 1 - RX]

    for p in range(RX + 3):
        for t in range(2):
            for c in range(3):
                store_parts(U.at[3], c, p, t, disp_of(c, p, t), lane)
                for k in range(3):
                    store_parts(U.at[k], c, p, t, Z[k, c, p + 3, t], lane)
    for t in range(2):
        near = yz_modes(U.at[3], 0, t)
        for p in range(RX + 2):
            far = yz_modes(U.at[3], p + 1, t)
            for key, value in combine(modes_of(near, far)).items():
                F[NUMBER[key], p, t] = value * SCALES[key[0]]
            near = far

    for k in range(3):
        for t in range(2):
            near = yz_modes(U.at[k], 0, t)
            for p in range(RX + 2):
                far = yz_modes(U.at[k], p + 1, t)
                modes = modes_of(near, far)
                energy = None
                for key, n in NUMBER.items():
                    factor = modes[mode_of(key)]
                    if key[0] == "s":
                        factor = factor + modes[axes(key[1]) + (key[2],)]
                    term = factor * F[n, p, t]
                    energy = term if energy is None else energy + term
                value = energy * SC[p, t]
                DV[k, p, 8 + 8 * t : 16 + 8 * t] = value
                if t == 1:
                    DV[k, p, 0:8] = value
                near = far
        cells, beside = [], []
        for p in range(RX + 2):
            cells.append(DV[k, p, 8:16])
            beside.append(DV[k, p, 7:15] + DV[k, p, 9:17])
            if p >= 2:
                senses[k, p - 2] = filtered(cells, beside, p - 1, lane)


def final_kernel(gathered, basis, senses, adjoint, sensitivity):
    total = jnp.sum(gathered[...], axis=0)

    def value(n):
        return jnp.broadcast_to(total[:, n : n + 1], (1, NZ))

    b0, b1, b2, h00, h01, h02, h11, h12, h22 = [value(n) for n in range(9)]
    l1, l2 = h01 / h00, h02 / h00
    d1 = h11 - l1 * h01
    e = h12 - l1 * h02
    fine1 = d1 > 0.0
    l3 = jnp.where(fine1, e / d1, 0.0)
    d2 = h22 - l2 * h02 - l3 * e
    t1 = b1 - l1 * b0
    t2 = b2 - l2 * b0 - l3 * t1
    c2 = jnp.where(d2 > 0.0, t2 / d2, 0.0)
    c1 = jnp.where(fine1, t1 / d1, 0.0) - l3 * c2
    c0 = b0 / h00 - l1 * c1 - l2 * c2
    own = slice(4, 4 + RX)
    for c in range(3):
        one, two, three = [basis[k, c, own, 0] for k in range(3)]
        adjoint[c] = c0 * one + c1 * two + c2 * three
    sensitivity[...] = c0 * senses[0] + c1 * senses[1] + c2 * senses[2]


VMEM = pl.BlockSpec(memory_space=pltpu.VMEM)


def call(kernel, inputs, outs, scratch=(), limit=None, extra=0, cost=None):
    single = not isinstance(outs, list)
    shapes = [outs] if single else outs
    result = pl.pallas_call(
        kernel,
        out_shape=[jax.ShapeDtypeStruct(s, F32) for s in shapes],
        in_specs=[VMEM] * (len(inputs) - extra) + [pl.BlockSpec(memory_space=pl.ANY)] * extra,
        out_specs=[VMEM] * len(shapes),
        scratch_shapes=[pltpu.VMEM(s, F32) for s in scratch],
        cost_estimate=cost and pl.CostEstimate(flops=0, bytes_accessed=cost, transcendentals=0),
        compiler_params=pltpu.CompilerParams(vmem_limit_bytes=limit or 32 * 1024 * 1024),
    )(*inputs)
    return result[0] if single else result


MAIN_SCRATCH = [
    (6, NI, 24, NZ),
    (3, RX, 8, NZ),
    (3, NI - 1, 8, NZ),
    (NI - 1, 8, NZ),
    (NI + 2, 40, NZ),
    (NI, 2, 8, NZ),
    (NI, 24, NZ),
    (NI, 2, 8, NZ),
    (6, NI, 2, 8, NZ),
    (6, NI, 24, NZ),
]
SENSE_SCRATCH = [
    (3, RX + 3, 8, NZ),
    (4, 6, RX + 3, 24, NZ),
    (len(KEYS), RX + 2, 2, 8, NZ),
    (3, RX + 2, 24, NZ),
]


def swaps(start, count):
    pairs = [(i, i + 1) for i in range(start, count - 1, 2)]
    return pairs + [(j, i) for i, j in pairs]


def shards(displacement, adjoint_load, density, fixed_mask, load_nodes, load_forces):
    count_x = lax.axis_size("x") * lax.axis_size("y")
    count_y = lax.axis_size("z") * lax.axis_size("c")
    given = (adjoint_load, displacement, density, fixed_mask, load_nodes, load_forces)
    first, second, *given = pl.pallas_call(
        pack_x_kernel,
        out_shape=[pltpu.VMEM((UP_X, RY, NZ), F32), pltpu.VMEM((UP_X + 1, RY, NZ), F32)]
        + [pltpu.VMEM(value.shape, value.dtype) for value in given],
        in_specs=[pl.BlockSpec(memory_space=pltpu.HBM)] * 6,
        out_specs=[VMEM] * 8,
        scratch_shapes=[pltpu.SemaphoreType.DMA((6,))],
    )(*given)
    own, loads = tuple(given[:4]), tuple(given[4:])
    second = lax.ppermute(second, ("x", "y"), swaps(1, count_x))
    first = lax.ppermute(first, ("x", "y"), swaps(0, count_x))
    placed = call(loads_kernel, loads, (3, NI - 1, 2, RY, NZ))
    sizes = (NEAR + CORNER, 4, NZ)
    second, low, up = call(
        pack_second_kernel,
        own + (first, second, placed),
        [(NEAR + CORNER + 1, 4, NZ), (LOW_X, RY, NZ), (UP_X, RY, NZ)],
        extra=1,
    )
    first = call(functools.partial(pack_y_kernel, 0), own + (low, up, second), sizes, extra=1)
    second = lax.ppermute(second, ("z", "c"), swaps(1, count_y))
    first = lax.ppermute(first, "c", swaps(0, 2))
    close = lax.axis_size("c") * count_x
    far = lax.axis_size("z")
    basis, scale, sums = call(
        main_kernel,
        own + (low, up, placed, first, second),
        [
            (3, 3, NI, 2, 8, NZ),
            (RX + 2, 2, 8, NZ),
            (close, 1, NZ),
        ],
        MAIN_SCRATCH,
        48 * 1024 * 1024,
    )
    senses = call(
        sense_kernel,
        (own[1], low, up, first, second, basis, scale),
        (3, RX, RY, NZ),
        SENSE_SCRATCH,
        cost=6_000_000,
    )
    sums = lax.all_to_all(sums, ("x", "y", "c"), 0, 0, tiled=True)
    sums = jnp.broadcast_to(jnp.sum(sums, axis=0, keepdims=True), (far, 1, NZ))
    sums = lax.all_to_all(sums, "z", 0, 0, tiled=True)
    adjoint, sensitivity = call(
        final_kernel, (sums, basis, senses), [(3, RX, RY, NZ), (RX, RY, NZ)]
    )
    return adjoint, sensitivity


def solution(mesh):
    size_x, size_y = mesh.shape["gx"], mesh.shape["gy"]
    side = int(round(size_x**0.5))
    whole = Mesh(
        mesh.devices.reshape(side, size_x // side, size_y // 2, 2), ("x", "y", "z", "c")
    )
    field = P(None, ("x", "y"), ("z", "c"), None)
    grid = P(("x", "y"), ("z", "c"), None)
    return jax.shard_map(
        shards,
        mesh=whole,
        in_specs=(field, field, grid, grid, P(), P()),
        out_specs=(field, grid),
        check_vma=False,
    )
```
